32 devices in a mesh: grp: 4 (over y, core), own: 8 (over z, x).
Axes of the slice: x: 2, y: 2, z: 4, core: 2. Of those that a mesh axis runs over, the one named last changes fastest.
Arguments:
- fields: bfloat16 [192, 256, 128], P(None, 'grp'), may hold values from -6 to 6
- labels: int32 [192], replicated, may hold values 0 or 1
- pair_first: int32 [4, 8, 16], P('grp', 'own'), may hold values from 0 to 255, as said below
- pair_second: int32 [4, 8, 16], P(None, 'own'), may hold values from 0 to 255, as said below
- pair_count: int32 [4, 8], P('grp', 'own'), may hold values from 4 to 16, as said below
- pair_mats: float32 [4, 8, 16, 128, 128], P('grp', 'own'), may hold values from -6 to 6
Outputs:
- logits: float32 [192], replicated
- field_grad: float32 [192, 256, 128], P('own', 'grp')
- new_mats: float32 [4, 8, 16, 128, 128], P('grp', 'own')
The draws below stay inside these ranges and needn't reach their ends.
Inputs may be any that keep to these rules, and one draw needn't show every extreme that they name: pair_first[g, o, s] lies in the block of fields g * 64 to (g + 1) * 64 - 1. `pair_second`: on every device (g, o), each block of 64 fields holds the second field of exactly 4 of the 16 slots; the second field is never the first. `pair_count`: slots at and beyond the count hold no pair; one device has all 16 slots live.
All inputs are finite; a program needn't handle non-finite values.
Results may differ from the reference program's by a relative error of at most 0.0003.
Values may be sent and summed in bfloat16 or wider, within the bound.
A program may use at most 64 MiB of HBM per device.

```python
import math
import jax
import jax.numpy as jnp
from jax import lax

K = 128
F = 256
B = 192
SLOTS = 16
STEPS = 2
N_GRP = 4
N_OWN = 8


def pair_tables(key):
    key_order, key_first, key_second, key_count, key_full = jax.random.split(jax.random.fold_in(key, 7), 5)
    capacity = SLOTS // N_GRP
    per_block = F // N_GRP
    shape_all = (N_GRP, N_OWN, SLOTS)
    base_blocks = jnp.arange(SLOTS, dtype=jnp.int32) // capacity
    scores = jax.random.randint(key_order, shape_all, 0, 1 << 20) * SLOTS + jnp.arange(SLOTS, dtype=jnp.int32)
    ordering = jnp.argsort(scores, axis=-1)
    block_ids = base_blocks[ordering]
    first_off = jax.random.randint(key_first, shape_all, 0, per_block)
    second_off = (first_off + 1 + jax.random.randint(key_second, shape_all, 0, per_block - 1)) % per_block
    group_ids = jnp.arange(N_GRP, dtype=jnp.int32)[:, None, None]
    first_ids = group_ids * per_block + first_off
    second_ids = block_ids * per_block + second_off
    counts = jax.random.randint(key_count, (N_GRP, N_OWN), SLOTS // 4, SLOTS * 5 // 8 + 1)
    full_device = jax.random.randint(key_full, (), 0, N_GRP * N_OWN)
    device_ids = jnp.arange(N_GRP * N_OWN, dtype=jnp.int32).reshape(N_GRP, N_OWN)
    counts = jnp.where(device_ids == full_device, SLOTS, counts)
    return (first_ids.astype(jnp.int32), second_ids.astype(jnp.int32), counts.astype(jnp.int32))


def draw_pair_first(key, part):
    return pair_tables(key)[0]


def draw_pair_second(key, part):
    return pair_tables(key)[1]


def draw_pair_count(key, part):
    return pair_tables(key)[2]


def place_ends(result, stream_key, least, top_value):
    longest = result.shape.index(max(result.shape))
    spots = []
    for shift in (0, 1):
        where = [jax.random.randint(jax.random.fold_in(stream_key, axis), (), 0, length) for axis, length in enumerate(result.shape)]
        where[longest] = (where[longest] + shift) % result.shape[longest]
        spots.append(tuple(where))
    return result.at[spots[0]].set(least).at[spots[1]].set(top_value)


def levels(own_key, dims, pieces, least, high):
    def one(position, blocks):
        steps = jax.random.uniform(jax.random.fold_in(jax.random.fold_in(own_key, 6), position), (blocks,), jnp.float32, least / len(pieces), high / len(pieces))
        return jnp.repeat(jnp.exp(steps), dims[position] // blocks).reshape((-1,) + (1,) * (len(dims) - position - 1))

    factor_of = one(*pieces[0])
    for cut in pieces[1:]:
        factor_of = factor_of * one(*cut)
    return factor_of


def gaussian(rng, shape, width, bound, pieces=(), kind=jnp.bfloat16):
    array = width * jax.random.normal(rng, shape, jnp.float32)
    if pieces:
        array = array * levels(rng, shape, pieces, -0.22, 0.18)
    return jnp.clip(array, -bound, bound).astype(kind)


def setup_inputs(seed: int = 0) -> dict:
    keys = jax.random.split(jax.random.key(seed), 7)
    fields = gaussian(keys[0], (B, F, K), 1.0, 6.0, ((1, 4),))
    labels = place_ends((jax.random.randint(keys[1], (B,), 0, 2) < 1).astype(jnp.int32), jax.random.fold_in(keys[1], 1), 0, 1)
    pair_first = draw_pair_first(jax.random.fold_in(keys[6], 71), 0)
    pair_second = draw_pair_second(jax.random.fold_in(keys[6], 71), 0)
    pair_count = draw_pair_count(jax.random.fold_in(keys[6], 71), 0)
    pair_mats = gaussian(keys[5], (N_GRP, N_OWN, SLOTS, K, K), 1.0, 6.0, ((0, 4), (1, 8)), jnp.float32)
    return dict(fields=fields, labels=labels, pair_first=pair_first, pair_second=pair_second, pair_count=pair_count, pair_mats=pair_mats)


logit_gain = 1.5
step_size = 1000.0
highest = lax.Precision.HIGHEST

def device_view(field_data, first_ids, second_ids, matrices):
    first_vec = jnp.take(field_data, first_ids, axis=1)
    second_vec = jnp.take(field_data, second_ids, axis=1)
    mixed = jnp.einsum('bsk,skl->bsl', first_vec, matrices, precision=highest)
    return (first_vec, second_vec, mixed)

def reference(fields, labels, pair_first, pair_second, pair_count, pair_mats):
    groups, owners, slot_count = pair_first.shape
    devices = groups * owners
    samples, _, feature = fields.shape
    field_data = fields.astype(jnp.float32)
    targets = labels.astype(jnp.float32)
    firsts = pair_first.reshape(devices, slot_count)
    seconds = pair_second.reshape(devices, slot_count)
    live_mask = (jnp.arange(slot_count, dtype=jnp.int32)[None, :] < pair_count.reshape(devices, 1)).astype(jnp.float32)
    matrices = pair_mats.reshape(devices, slot_count, feature, feature)
    logit_scale = logit_gain / math.sqrt(devices * slot_count)
    root_width = math.sqrt(feature)
    logits = jnp.zeros((samples,), jnp.float32)
    dense_grad = jnp.zeros(fields.shape, jnp.float32)
    for step_index in range(STEPS):

        def partial_of(accum, device_item):
            first_ids, second_ids, alive, mats_here = device_item
            first_vec, second_vec, mixed = device_view(field_data, first_ids, second_ids, mats_here)
            partial_value = lax.optimization_barrier(jnp.sum(lax.optimization_barrier(jnp.sum(mixed * second_vec, axis=2)) / feature * alive[None, :], axis=1))
            return (accum + partial_value, None)
        total_sum, _ = lax.scan(partial_of, jnp.zeros((samples,), jnp.float32), (firsts, seconds, live_mask, matrices))
        logits = logit_scale * total_sum
        errors = jax.nn.sigmoid(logits) - targets
        last_step = step_index == STEPS - 1

        def update_of(accum, device_item):
            first_ids, second_ids, alive, mats_here = device_item
            first_vec, second_vec, mixed = device_view(field_data, first_ids, second_ids, mats_here)
            if last_step:
                grad_first = errors[:, None, None] * jnp.einsum('skl,bsl->bsk', mats_here, second_vec, precision=highest) / root_width * alive[None, :, None]
                grad_second = errors[:, None, None] * mixed / root_width * alive[None, :, None]
                accum = accum.at[:, first_ids].add(grad_first).at[:, second_ids].add(grad_second)
            gradient = jnp.einsum('bsk,bsl->skl', first_vec * errors[:, None, None], second_vec, precision=highest)
            updated = mats_here - step_size * logit_scale / (samples * feature) * alive[:, None, None] * gradient
            return (accum, updated)
        dense_grad, matrices = lax.scan(update_of, jnp.zeros(fields.shape, jnp.float32), (firsts, seconds, live_mask, matrices))
    return (logits, dense_grad, matrices.reshape(pair_mats.shape))
```

```python
import functools
import math

import jax
import jax.numpy as jnp
from jax import lax
from jax.experimental import pallas as pl
from jax.experimental.pallas import tpu as pltpu
from jax.sharding import PartitionSpec as P

STEPS = 2


logit_gain = 1.5
step_size = 1000.0
highest = lax.Precision.HIGHEST


def logit_errors(partial_value, targets, logit_scale):
    total_sum = lax.psum(partial_value, ("grp", "own"))
    logits = logit_scale * total_sum
    errors = jax.nn.sigmoid(logits) - targets
    return (logits, errors)


def on_device(fields, labels, pair_first, pair_second, pair_count, pair_mats):
    groups = lax.axis_size("grp")
    owners = lax.axis_size("own")
    my_group = lax.axis_index("grp")
    samples, per_block, feature = fields.shape
    slot_count = pair_first.shape[2]
    capacity = slot_count // groups
    second_table = pair_second[:, 0, :]
    block_ids = second_table // per_block
    offsets = second_table % per_block
    member = (block_ids[:, :, None] == jnp.arange(groups, dtype=jnp.int32)[None, None, :]).astype(
        jnp.int32
    )
    slot_ranks = jnp.sum((jnp.cumsum(member, axis=1) - 1) * member, axis=2)
    places = block_ids * capacity + slot_ranks
    chosen = (block_ids[:, :, None] == my_group) & (
        slot_ranks[:, :, None] == jnp.arange(capacity, dtype=jnp.int32)[None, None, :]
    )
    served = jnp.sum(jnp.where(chosen, offsets[:, :, None], 0), axis=1).reshape(-1)
    outgoing = jnp.take(fields, served, axis=1)
    incoming = lax.all_to_all(outgoing, "grp", split_axis=1, concat_axis=1, tiled=True)
    my_places = lax.dynamic_index_in_dim(places, my_group, 0, keepdims=False)
    second_vec = jnp.take(incoming, my_places, axis=1).astype(jnp.float32)
    first_local = pair_first[0, 0] - my_group * per_block
    first_vec = jnp.take(fields, first_local, axis=1).astype(jnp.float32)
    live_mask = (jnp.arange(slot_count, dtype=jnp.int32) < pair_count[0, 0]).astype(jnp.float32)
    matrices = pair_mats[0, 0]
    targets = labels.astype(jnp.float32)
    logit_scale = logit_gain / math.sqrt(groups * owners * slot_count)
    root_width = math.sqrt(feature)
    logits = jnp.zeros((samples,), jnp.float32)
    grad_first = jnp.zeros(first_vec.shape, jnp.float32)
    grad_second = jnp.zeros(first_vec.shape, jnp.float32)
    for step_index in range(STEPS):
        mixed = jnp.einsum("bsk,skl->bsl", first_vec, matrices, precision=highest)
        partial_value = jnp.sum(
            jnp.sum(mixed * second_vec, axis=2) / feature * live_mask[None, :], axis=1
        )
        logits, errors = logit_errors(partial_value, targets, logit_scale)
        if step_index == STEPS - 1:
            grad_first = (
                errors[:, None, None]
                * jnp.einsum("skl,bsl->bsk", matrices, second_vec, precision=highest)
                / root_width
                * live_mask[None, :, None]
            )
            grad_second = errors[:, None, None] * mixed / root_width * live_mask[None, :, None]
        gradient = jnp.einsum(
            "bsk,bsl->skl", first_vec * errors[:, None, None], second_vec, precision=highest
        )
        matrices = (
            matrices
            - step_size * logit_scale / (samples * feature) * live_mask[:, None, None] * gradient
        )
    slot_iota = jnp.arange(slot_count, dtype=jnp.int32)
    slot_of = jnp.sum(
        jnp.where(my_places[None, :] == slot_iota[:, None], slot_iota[None, :], 0), axis=1
    )
    returned = lax.all_to_all(
        jnp.take(grad_second, slot_of, axis=1), "grp", split_axis=1, concat_axis=1, tiled=True
    )
    block_iota = jnp.arange(per_block, dtype=jnp.int32)
    pick_second = (served[:, None] == block_iota[None, :]).astype(jnp.float32)
    pick_first = (first_local[:, None] == block_iota[None, :]).astype(jnp.float32)
    dense_grad = jnp.einsum("bsk,sf->bfk", grad_first, pick_first, precision=highest)
    dense_grad = dense_grad + jnp.einsum("bpk,pf->bfk", returned, pick_second, precision=highest)
    field_grad = lax.psum_scatter(dense_grad, "own", scatter_dimension=0, tiled=True)
    return (logits, field_grad, matrices[None, None])


LANES = 128
SUB = 8
TOP = 32760.0
MESH = pl.DeviceIdType.MESH
NT = (((1,), (1,)), ((), ()))


def two_parts(x):
    high = x.astype(jnp.bfloat16)
    low = (x - high.astype(jnp.float32)).astype(jnp.bfloat16)
    return high, low


def dot32(a, b):
    return jnp.dot(a, b, preferred_element_type=jnp.float32)


def step_kernel(
    groups, owners,
    slot_of, places, live_place,
    fields, tcol, msg0, targets, mats,
    logits_out, grad_out, mats_out,
    first_vec, first_t, served_vec, second_vec, mats_mid, total,
    msg1, got1, msg2, got2, term_a, term_b, send_a, send_b, got_a, got_b, err_col, acc,
    sem_v, sem_m1, sem_m2, sem_a, sem_b,
):
    samples, per_block, feature = fields.shape
    slots = mats.shape[0]
    cap = slots // groups
    chunk = samples // owners
    devices = groups * owners
    pairs = cap // 2
    g, o = lax.axis_index("grp"), lax.axis_index("own")
    me = g * owners + o
    logit_scale = logit_gain / math.sqrt(devices * slots)
    rate = step_size * logit_scale / (samples * feature)
    inv_root = 1.0 / math.sqrt(feature)
    extra = 2 * LANES - samples

    barrier = pltpu.get_barrier_semaphore()

    def greet(d, _):
        peer = lax.rem(me + d, devices)
        pl.semaphore_signal(
            barrier, inc=1, device_id=(lax.div(peer, owners), lax.rem(peer, owners)), device_id_type=MESH
        )
        return 0

    lax.fori_loop(1, devices, greet, 0)

    def gather(lo, out):
        wide = SUB * per_block
        rows = slots * SUB
        lanes = lax.broadcasted_iota(jnp.int32, (rows, wide), 1)
        pick = jnp.where(lanes == tcol[lo : lo + rows, :], 1.0, 0.0).astype(jnp.bfloat16)

        def part(i, _):
            halves = []
            for h in range(2):
                block = fields[pl.ds(i * 16 + h * SUB, SUB)].reshape(wide, feature)
                halves.append(dot32(pick, block).reshape(slots, SUB, feature))
            out[:, pl.ds(pl.multiple_of(i * 16, 16), 16), :] = jnp.concatenate(halves, axis=1).astype(jnp.bfloat16)
            return 0

        lax.fori_loop(0, samples // 16, part, 0)

    def vec_copy(j):
        to = lax.rem(g + j, groups)
        return pltpu.make_async_remote_copy(
            src_ref=served_vec.at[pl.ds(to * cap, cap)],
            dst_ref=second_vec.at[pl.ds(g * cap, cap)],
            send_sem=sem_v.at[0, j],
            recv_sem=sem_v.at[1, j],
            device_id=(to, o),
            device_id_type=MESH,
        )

    gather(slots * SUB, served_vec)
    pl.semaphore_wait(barrier, devices - 1)
    for j in range(1, groups):
        vec_copy(j).start()
    second_vec[pl.ds(g * cap, cap)] = served_vec[pl.ds(g * cap, cap)]
    gather(0, first_vec)

    def turn(p, _):
        v = first_vec[p].astype(jnp.float32)
        v = jnp.concatenate([v, jnp.zeros((extra, feature), jnp.float32)], axis=0)
        first_t[p] = v.T.astype(jnp.bfloat16)
        return 0

    lax.fori_loop(0, slots, turn, 0)
    total[...] = jnp.zeros_like(total)

    def mix(p, mat):
        v1 = first_vec[p]
        high, low = two_parts(mat)
        return dot32(jnp.concatenate([v1, v1], axis=1), jnp.concatenate([high, low], axis=0)), high, low

    def first_pass(q):
        sums = total[...]
        for c in range(cap):
            p = q * cap + c
            mixed, _, _ = mix(p, mats[slot_of[p]])
            sums = sums + (mixed * second_vec[p].astype(jnp.float32)) * live_place[p]
        total[...] = sums

    first_pass(g)
    for j in range(1, groups):
        vec_copy(j).wait_recv()
        first_pass(lax.rem(g + groups - j, groups))

    def partial_rows():
        ones = jnp.ones((SUB, feature), jnp.float32)
        tail = jnp.concatenate([total[LANES:samples], jnp.zeros((extra, feature), jnp.float32)], axis=0)
        return [
            lax.dot_general(ones, t, NT, precision=highest, preferred_element_type=jnp.float32)
            for t in (total[0:LANES], tail)
        ]

    row_id = lax.broadcasted_iota(jnp.int32, (SUB, LANES), 0)
    r0, r1 = partial_rows()
    for q in range(groups):
        msg1[q] = jnp.where(row_id == 0, r0, jnp.where(row_id == 1, r1, msg0[q]))

    def tile_copy(src, dst, sems, d, pick_own):
        peer = lax.rem(me + d, devices)
        pg, po = lax.div(peer, owners), lax.rem(peer, owners)
        return pltpu.make_async_remote_copy(
            src_ref=src.at[po if pick_own else pg],
            dst_ref=dst.at[me],
            send_sem=sems.at[0, peer],
            recv_sem=sems.at[1, me],
            device_id=(pg, po),
            device_id_type=MESH,
        )

    def tile_arrival(src, dst, sems, d):
        peer = lax.rem(me + d, devices)
        return pltpu.make_async_remote_copy(
            src_ref=src.at[0],
            dst_ref=dst.at[peer],
            send_sem=sems.at[0, peer],
            recv_sem=sems.at[1, peer],
            device_id=(lax.div(peer, owners), lax.rem(peer, owners)),
            device_id_type=MESH,
        )

    def send_tiles(src, dst, sems, pick_own):
        def one(d, _):
            tile_copy(src, dst, sems, d, pick_own).start()
            return 0

        lax.fori_loop(1, devices, one, 0)

    def wait_tiles(src, dst, sems):
        def one(d, _):
            tile_arrival(src, dst, sems, d).wait_recv()
            return 0

        lax.fori_loop(1, devices, one, 0)

    def errors_of(got, at):
        sums = got[0]
        for d in range(1, devices):
            sums = sums + got[d]
        sums = sums[at : at + 2] * (1.0 / feature)
        logits = logit_scale * sums
        return logits, jax.nn.sigmoid(logits) - targets[0:2]

    def error_row(err):
        return jnp.concatenate([err[0:1], err[1:2, 0 : samples - LANES]], axis=1)

    def gradient(p, erow):
        v = first_t[p][:, 0:samples].astype(jnp.float32) * erow
        high, low = two_parts(v)
        v2 = second_vec[p]
        return dot32(high, v2) + dot32(low, v2)

    send_tiles(msg1, got1, sem_m1, False)
    got1[me] = msg1[g]
    wait_tiles(msg1, got1, sem_m1)
    _, err = errors_of(got1, 0)
    erow = error_row(err)
    total[...] = jnp.zeros_like(total)
    msg2[...] = jnp.zeros_like(msg2)

    def second_pass(j):
        q = lax.rem(g + j, groups)
        sums = total[...]
        for c in range(cap):
            p = q * cap + c
            live = live_place[p]
            mid = mats[slot_of[p]] - (rate * live) * gradient(p, erow)
            mats_mid[p] = mid
            mixed, high, low = mix(p, mid)
            v2 = second_vec[p]
            first = lax.dot_general(
                jnp.concatenate([v2, v2], axis=1),
                jnp.concatenate([high, low], axis=1),
                NT,
                preferred_element_type=jnp.float32,
            )
            sums = sums + (mixed * v2.astype(jnp.float32)) * live
            factor = live * inv_root
            term_a[c] = first * factor
            term_b[c] = mixed * factor
        total[...] = sums

        def code(w, _):
            rows = pl.ds(pl.multiple_of(w * chunk, SUB), chunk)
            terms = [t[c, rows, :] for t in (term_a, term_b) for c in range(cap)]
            big = functools.reduce(jnp.maximum, [jnp.abs(t) for t in terms])
            big = jnp.maximum(jnp.max(big, axis=0, keepdims=True), 1e-30)
            gain = TOP / big
            whole = [jnp.floor(t * gain + 0.5).astype(jnp.int32) for t in terms]
            for at, out in ((0, send_a), (cap, send_b)):
                for k in range(pairs):
                    a, b = whole[at + 2 * k], whole[at + 2 * k + 1]
                    out[q, w, pl.ds(k * chunk, chunk), :] = (a & 0xFFFF) | (b << 16)
            msg2[w, pl.ds(q, 1), :] = big * (1.0 / TOP)
            return 0

        lax.fori_loop(0, owners, code, 0)

    def unit_a(j, k):
        q, w = lax.rem(g + j, groups), lax.rem(o + k, owners)
        return pltpu.make_async_remote_copy(
            src_ref=send_a.at[q, w], dst_ref=got_a.at[o, q], send_sem=sem_a.at[0, q, w],
            recv_sem=sem_a.at[1, q, o], device_id=(g, w), device_id_type=MESH,
        )

    def unit_b(j, k):
        q, w = lax.rem(g + j, groups), lax.rem(o + k, owners)
        return pltpu.make_async_remote_copy(
            src_ref=send_b.at[q, w], dst_ref=got_b.at[g, o], send_sem=sem_b.at[0, q, w],
            recv_sem=sem_b.at[1, g, o], device_id=(q, w), device_id_type=MESH,
        )

    def send_units(j):
        def one(k, _):
            unit_a(j, k).start()
            unit_b(j, k).start()
            return 0

        lax.fori_loop(1, owners, one, 0)
        q = lax.rem(g + j, groups)
        got_a[o, q] = send_a[q, o]

    second_pass(0)
    got_b[g, o] = send_b[g, o]
    send_units(0)

    def middle(j, _):
        second_pass(j)
        send_units(j)
        unit_b(j, 0).start()
        return 0

    lax.fori_loop(1, groups - 1, middle, 0)
    second_pass(groups - 1)
    r0, r1 = partial_rows()
    for w in range(owners):
        msg2[w] = jnp.where(row_id == groups, r0, jnp.where(row_id == groups + 1, r1, msg2[w]))
    send_tiles(msg2, got2, sem_m2, True)
    send_units(groups - 1)
    unit_b(groups - 1, 0).start()
    got2[me] = msg2[o]
    wait_tiles(msg2, got2, sem_m2)
    logits, err = errors_of(got2, groups)
    logits_out[...] = jnp.concatenate([logits, jnp.zeros((SUB - 2, LANES), jnp.float32)], axis=0)
    erow = error_row(err)
    eye = lax.broadcasted_iota(jnp.int32, (LANES, LANES), 0) == lax.broadcasted_iota(jnp.int32, (LANES, LANES), 1)
    for half in range(2):
        column = jnp.sum(jnp.where(eye, err[half : half + 1], 0.0), axis=1, keepdims=True)
        err_col[pl.ds(half * LANES, LANES), :] = jnp.broadcast_to(column, (LANES, LANES))

    def last_update(s, _):
        p = places[s]
        mats_out[s] = mats_mid[p] - (rate * live_place[p]) * gradient(p, erow)
        return 0

    lax.fori_loop(0, slots, last_update, 0)

    col = err_col[pl.ds(pl.multiple_of(o * chunk, SUB), chunk), :]
    parts = chunk // SUB
    field_rows = lax.broadcasted_iota(jnp.int32, (SUB * per_block, LANES), 0)

    def decode(word_of, scale):
        out = []
        factor = col * scale
        for k in range(pairs):
            w = word_of(k)
            out.append(((w << 16) >> 16).astype(jnp.float32) * factor)
            out.append((w >> 16).astype(jnp.float32) * factor)
        return out

    def place_terms(terms, spots, fresh=False):
        spots = (spots + 0.5).astype(jnp.int32)
        pick = jnp.where(field_rows == spots, 1.0, 0.0).astype(jnp.bfloat16)
        x = jnp.concatenate(
            [jnp.concatenate([t[i * SUB : (i + 1) * SUB] for t in terms], axis=0) for i in range(parts)], axis=1
        )
        high, low = two_parts(x)
        out = dot32(jnp.concatenate([pick, pick], axis=1), jnp.concatenate([high, low], axis=0))
        acc[...] = out if fresh else acc[...] + out

    span = LANES // (cap * SUB)

    acc[...] = jnp.zeros_like(acc)

    def arrive_b(j, k):
        @pl.when(j + k > 0)
        def _():
            q, w = lax.rem(g + groups - j, groups), lax.rem(o + owners - k, owners)
            pltpu.make_async_remote_copy(
                src_ref=send_b.at[q, w], dst_ref=got_b.at[q, w], send_sem=sem_b.at[0, q, w],
                recv_sem=sem_b.at[1, q, w], device_id=(q, w), device_id_type=MESH,
            ).wait_recv()

    def from_seconds(j, _):
        q = lax.rem(g + groups - j, groups)

        def one(k, _):
            arrive_b(j, k)
            return 0

        lax.fori_loop(0, owners, one, 0)

        def half(h, _):
            terms, spots = [], 0.0
            for i in range(span):
                w = h * span + i
                src = q * owners + w
                scale = got2[src, pl.ds(g, 1), :]
                terms += decode(lambda k: got_b[q, w, pl.ds(k * chunk, chunk), :], scale)
                spots = spots + got1[src][3:4]
            place_terms(terms, spots)
            return 0

        lax.fori_loop(0, owners // span, half, 0)
        return 0

    lax.fori_loop(0, groups, from_seconds, 0)

    def from_firsts(k, _):
        w = lax.rem(o + owners - k, owners)
        src = g * owners + w

        @pl.when(k > 0)
        def _():
            for q in range(groups):
                pltpu.make_async_remote_copy(
                    src_ref=send_a.at[q, w], dst_ref=got_a.at[w, q], send_sem=sem_a.at[0, q, w],
                    recv_sem=sem_a.at[1, q, w], device_id=(g, w), device_id_type=MESH,
                ).wait_recv()

        terms = []
        for q in range(groups):
            scale = got2[src][q : q + 1]
            terms += decode(lambda m: got_a[w, q, pl.ds(m * chunk, chunk), :], scale)
        place_terms(terms, got1[src][2:3])
        return 0

    lax.fori_loop(0, owners, from_firsts, 0)
    for i in range(parts):
        grad_out[i * SUB : (i + 1) * SUB] = acc[:, i * feature : (i + 1) * feature].reshape(SUB, per_block, feature)

    for j in range(1, groups):
        vec_copy(j).wait_send()

    def drain_tiles(d, _):
        tile_copy(msg1, got1, sem_m1, d, False).wait_send()
        tile_copy(msg2, got2, sem_m2, d, True).wait_send()
        return 0

    lax.fori_loop(1, devices, drain_tiles, 0)

    def drain_units(j, _):
        def one(k, _):
            unit_a(j, k).wait_send()
            unit_b(j, k).wait_send()
            return 0

        lax.fori_loop(1, owners, one, 0)

        @pl.when(j > 0)
        def _():
            unit_b(j, 0).wait_send()

        return 0

    lax.fori_loop(0, groups, drain_units, 0)


def on_device_kernel(fields, labels, pair_first, pair_second, pair_count, pair_mats):
    groups = lax.axis_size("grp")
    owners = lax.axis_size("own")
    g, o = lax.axis_index("grp"), lax.axis_index("own")
    samples, per_block, feature = fields.shape
    slots = pair_first.shape[2]
    cap = slots // groups
    chunk = samples // owners
    devices = groups * owners
    table = pair_second[:, 0, :]
    block_ids = table // per_block
    offsets = table % per_block
    same = block_ids[:, :, None] == block_ids[:, None, :]
    slot_iota = jnp.arange(slots, dtype=jnp.int32)
    before = slot_iota[None, :] < slot_iota[:, None]
    ranks = jnp.sum((same & before[None]).astype(jnp.int32), axis=2)
    places_all = block_ids * cap + ranks
    match = places_all[:, :, None] == slot_iota[None, None, :]
    off_place = jnp.sum(jnp.where(match, offsets[:, :, None], 0), axis=1)
    served = lax.dynamic_slice_in_dim(off_place, g * cap, cap, axis=1).reshape(-1)
    places = lax.dynamic_index_in_dim(places_all, g, 0, keepdims=False)
    mine = places[:, None] == slot_iota[None, :]
    slot_of = jnp.sum(jnp.where(mine, slot_iota[:, None], 0), axis=0)
    first_local = pair_first[0, 0] - g * per_block
    first_place = jnp.sum(jnp.where(mine, first_local[:, None], 0), axis=0)
    second_place = lax.dynamic_index_in_dim(off_place, g, 0, keepdims=False)
    live_place = (slot_of < pair_count[0, 0]).astype(jnp.float32)
    lift = jnp.arange(SUB, dtype=jnp.int32) * per_block
    spots = lambda idx: (idx[:, None] + lift[None, :]).reshape(-1)
    tcol = spots(jnp.concatenate([first_place, served]))[:, None]
    span = LANES // (cap * SUB)
    segments = jnp.tile(spots(second_place).reshape(groups, cap * SUB), (1, span))
    lane_seg = jnp.arange(LANES, dtype=jnp.int32) // (cap * SUB)
    segments = jnp.where(lane_seg[None, :] == o % span, segments, 0)
    firsts = jnp.broadcast_to(spots(first_place)[None], (groups, LANES))
    zero = jnp.zeros((groups, 2, LANES), jnp.int32)
    msg0 = jnp.concatenate([zero, firsts[:, None], segments[:, None], zero, zero], axis=1).astype(jnp.float32)
    targets = jnp.pad(labels.astype(jnp.float32), (0, SUB * LANES - samples)).reshape(SUB, LANES)
    smem = pl.BlockSpec(memory_space=pltpu.SMEM)
    vmem = pl.BlockSpec(memory_space=pltpu.VMEM)
    rows = cap // 2 * chunk
    f32, bf16, i32 = jnp.float32, jnp.bfloat16, jnp.int32
    logits, grad, new_mats = pl.pallas_call(
        functools.partial(step_kernel, groups, owners),
        out_shape=(
            jax.ShapeDtypeStruct((SUB, LANES), f32),
            jax.ShapeDtypeStruct((chunk, per_block, feature), f32),
            jax.ShapeDtypeStruct((slots, feature, feature), f32),
        ),
        in_specs=[smem] * 3 + [vmem] * 5,
        out_specs=(vmem,) * 3,
        scratch_shapes=[
            pltpu.VMEM((slots, samples, feature), bf16),
            pltpu.VMEM((slots, feature, 2 * LANES), bf16),
            pltpu.VMEM((slots, samples, feature), bf16),
            pltpu.VMEM((slots, samples, feature), bf16),
            pltpu.VMEM((slots, feature, feature), f32),
            pltpu.VMEM((samples, feature), f32),
            pltpu.VMEM((groups, SUB, LANES), f32),
            pltpu.VMEM((devices, SUB, LANES), f32),
            pltpu.VMEM((owners, SUB, LANES), f32),
            pltpu.VMEM((devices, SUB, LANES), f32),
            pltpu.VMEM((cap, samples, feature), f32),
            pltpu.VMEM((cap, samples, feature), f32),
            pltpu.VMEM((groups, owners, rows, feature), i32),
            pltpu.VMEM((groups, owners, rows, feature), i32),
            pltpu.VMEM((owners, groups, rows, feature), i32),
            pltpu.VMEM((groups, owners, rows, feature), i32),
            pltpu.VMEM((2 * LANES, LANES), f32),
            pltpu.VMEM((SUB * per_block, chunk // SUB * feature), f32),
            pltpu.SemaphoreType.DMA((2, groups)),
            pltpu.SemaphoreType.DMA((2, devices)),
            pltpu.SemaphoreType.DMA((2, devices)),
            pltpu.SemaphoreType.DMA((2, groups, owners)),
            pltpu.SemaphoreType.DMA((2, groups, owners)),
        ],
        compiler_params=pltpu.CompilerParams(
            collective_id=0, has_side_effects=True, vmem_limit_bytes=40 * 1024 * 1024
        ),
        cost_estimate=pl.CostEstimate(flops=4 * 10**9, bytes_accessed=8 * 10**6, transcendentals=400),
    )(slot_of, places, live_place, fields, tcol, msg0, targets, pair_mats[0, 0])
    return (logits.reshape(-1)[:samples], grad, new_mats[None, None])


def fits(groups, owners, fields, pair_first):
    samples, _, feature = fields.shape
    slots = pair_first.shape[2]
    cap = slots // groups
    return (
        feature == LANES
        and slots * SUB == LANES
        and slots % groups == 0
        and cap % 2 == 0
        and LANES < samples <= 2 * LANES
        and samples % (SUB * owners) == 0
        and samples % 16 == 0
        and owners % (LANES // (cap * SUB)) == 0
        and groups + 2 <= SUB
    )


def dispatch(groups, owners, fields, labels, pair_first, pair_second, pair_count, pair_mats):
    args = (fields, labels, pair_first, pair_second, pair_count, pair_mats)
    if fits(groups, owners, fields, pair_first):
        return on_device_kernel(*args)
    return on_device(*args)


def solution(mesh):
    in_specs = (
        P(None, "grp", None),
        P(),
        P("grp", "own", None),
        P(None, "own", None),
        P("grp", "own"),
        P("grp", "own", None, None, None),
    )
    out_specs = (P(), P("own", "grp", None), P("grp", "own", None, None, None))
    per_device = functools.partial(dispatch, mesh.shape["grp"], mesh.shape["own"])
    return jax.shard_map(
        per_device, mesh=mesh, in_specs=in_specs, out_specs=out_specs, check_vma=False
    )
```

```python
import functools
import math

import jax
import jax.numpy as jnp
from jax import lax
from jax.experimental import pallas as pl
from jax.experimental.pallas import tpu as pltpu
from jax.sharding import PartitionSpec as P

STEPS = 2


logit_gain = 1.5
step_size = 1000.0
highest = lax.Precision.HIGHEST


def logit_errors(partial_value, targets, logit_scale):
    total_sum = lax.psum(partial_value, ("grp", "own"))
    logits = logit_scale * total_sum
    errors = jax.nn.sigmoid(logits) - targets
    return (logits, errors)


def on_device(fields, labels, pair_first, pair_second, pair_count, pair_mats):
    groups = lax.axis_size("grp")
    owners = lax.axis_size("own")
    my_group = lax.axis_index("grp")
    samples, per_block, feature = fields.shape
    slot_count = pair_first.shape[2]
    capacity = slot_count // groups
    second_table = pair_second[:, 0, :]
    block_ids = second_table // per_block
    offsets = second_table % per_block
    member = (block_ids[:, :, None] == jnp.arange(groups, dtype=jnp.int32)[None, None, :]).astype(
        jnp.int32
    )
    slot_ranks = jnp.sum((jnp.cumsum(member, axis=1) - 1) * member, axis=2)
    places = block_ids * capacity + slot_ranks
    chosen = (block_ids[:, :, None] == my_group) & (
        slot_ranks[:, :, None] == jnp.arange(capacity, dtype=jnp.int32)[None, None, :]
    )
    served = jnp.sum(jnp.where(chosen, offsets[:, :, None], 0), axis=1).reshape(-1)
    outgoing = jnp.take(fields, served, axis=1)
    incoming = lax.all_to_all(outgoing, "grp", split_axis=1, concat_axis=1, tiled=True)
    my_places = lax.dynamic_index_in_dim(places, my_group, 0, keepdims=False)
    second_vec = jnp.take(incoming, my_places, axis=1).astype(jnp.float32)
    first_local = pair_first[0, 0] - my_group * per_block
    first_vec = jnp.take(fields, first_local, axis=1).astype(jnp.float32)
    live_mask = (jnp.arange(slot_count, dtype=jnp.int32) < pair_count[0, 0]).astype(jnp.float32)
    matrices = pair_mats[0, 0]
    targets = labels.astype(jnp.float32)
    logit_scale = logit_gain / math.sqrt(groups * owners * slot_count)
    root_width = math.sqrt(feature)
    logits = jnp.zeros((samples,), jnp.float32)
    grad_first = jnp.zeros(first_vec.shape, jnp.float32)
    grad_second = jnp.zeros(first_vec.shape, jnp.float32)
    for step_index in range(STEPS):
        mixed = jnp.einsum("bsk,skl->bsl", first_vec, matrices, precision=highest)
        partial_value = jnp.sum(
            jnp.sum(mixed * second_vec, axis=2) / feature * live_mask[None, :], axis=1
        )
        logits, errors = logit_errors(partial_value, targets, logit_scale)
        if step_index == STEPS - 1:
            grad_first = (
                errors[:, None, None]
                * jnp.einsum("skl,bsl->bsk", matrices, second_vec, precision=highest)
                / root_width
                * live_mask[None, :, None]
            )
            grad_second = errors[:, None, None] * mixed / root_width * live_mask[None, :, None]
        gradient = jnp.einsum(
            "bsk,bsl->skl", first_vec * errors[:, None, None], second_vec, precision=highest
        )
        matrices = (
            matrices
            - step_size * logit_scale / (samples * feature) * live_mask[:, None, None] * gradient
        )
    slot_iota = jnp.arange(slot_count, dtype=jnp.int32)
    slot_of = jnp.sum(
        jnp.where(my_places[None, :] == slot_iota[:, None], slot_iota[None, :], 0), axis=1
    )
    returned = lax.all_to_all(
        jnp.take(grad_second, slot_of, axis=1), "grp", split_axis=1, concat_axis=1, tiled=True
    )
    block_iota = jnp.arange(per_block, dtype=jnp.int32)
    pick_second = (served[:, None] == block_iota[None, :]).astype(jnp.float32)
    pick_first = (first_local[:, None] == block_iota[None, :]).astype(jnp.float32)
    dense_grad = jnp.einsum("bsk,sf->bfk", grad_first, pick_first, precision=highest)
    dense_grad = dense_grad + jnp.einsum("bpk,pf->bfk", returned, pick_second, precision=highest)
    field_grad = lax.psum_scatter(dense_grad, "own", scatter_dimension=0, tiled=True)
    return (logits, field_grad, matrices[None, None])


LANES = 128
SUB = 8
TOP = 32760.0
RUNS = 4
SECOND_ROW = 2
FIRST_ROW = 4
MESH = pl.DeviceIdType.MESH
NT = (((1,), (1,)), ((), ()))


def two_parts(x):
    high = x.astype(jnp.bfloat16)
    low = (x - high.astype(jnp.float32)).astype(jnp.bfloat16)
    return high, low


def dot32(a, b):
    return jnp.dot(a, b, preferred_element_type=jnp.float32)


def step_kernel(
    groups, owners,
    first_ids, second_ids, count, labels, fields_in, mats_in,
    logits_out, grad_out, mats_out,
    slot_of, places, fields, mats, mats_new,
    first_vec, first_t, served_vec, second_vec, mats_mid, total,
    msg1, got1, msg2, got2, term_a, term_b, send_a, send_b, got_a, got_b, err_col, acc,
    sem_f, sem_m, sem_v, sem_m1, sem_m2, sem_a, sem_b,
):
    samples, per_block, feature = fields.shape
    shift = per_block.bit_length() - 1
    slots = mats.shape[0]
    cap = slots // groups
    chunk = samples // owners
    devices = groups * owners
    pairs = cap // 2
    g, o = lax.axis_index("grp"), lax.axis_index("own")
    me = g * owners + o
    logit_scale = logit_gain / math.sqrt(devices * slots)
    rate = step_size * logit_scale / (samples * feature)
    inv_root = 1.0 / math.sqrt(feature)
    extra = 2 * LANES - samples

    run = samples // RUNS

    def load_fields(r):
        part = pl.ds(r * run, run)
        return pltpu.make_async_copy(fields_in.at[part], fields.at[part], sem_f.at[r])

    for r in range(RUNS):
        load_fields(r).start()
    load_mats = pltpu.make_async_copy(mats_in, mats, sem_m.at[0])
    load_mats.start()

    barrier = pltpu.get_barrier_semaphore()

    def greet(d, _):
        peer = lax.rem(me + d, devices)
        pl.semaphore_signal(
            barrier, inc=1, device_id=(lax.div(peer, owners), lax.rem(peer, owners)), device_id_type=MESH
        )
        return 0

    lax.fori_loop(1, devices, greet, 0)

    def gather(spots):
        wide = SUB * per_block
        lanes = lax.broadcasted_iota(jnp.int32, (SUB, wide), 1)
        lanes = lanes - lax.broadcasted_iota(jnp.int32, (SUB, wide), 0) * per_block
        pick = jnp.concatenate([jnp.where(lanes == f, 1.0, 0.0) for f in spots], axis=0).astype(jnp.bfloat16)

        def rows(out, start, size):
            def part(i, _):
                at = pl.multiple_of(start + i * 16, 16)
                halves = []
                for h in range(2):
                    block = fields[pl.ds(at + h * SUB, SUB)].reshape(wide, feature)
                    halves.append(dot32(pick, block).reshape(slots, SUB, feature))
                out[:, pl.ds(at, 16), :] = jnp.concatenate(halves, axis=1).astype(jnp.bfloat16)
                return 0

            lax.fori_loop(0, size // 16, part, 0)

        return rows

    def vec_copy(j, r):
        to = lax.rem(g + j, groups)
        part = pl.ds(r * run, run)
        return pltpu.make_async_remote_copy(
            src_ref=served_vec.at[pl.ds(to * cap, cap), part],
            dst_ref=second_vec.at[pl.ds(g * cap, cap), part],
            send_sem=sem_v.at[0, j, r],
            recv_sem=sem_v.at[1, j, r],
            device_id=(to, o),
            device_id_type=MESH,
        )

    served = []
    for q in range(groups):
        found, seen = [jnp.int32(0)] * cap, jnp.int32(0)
        for s in range(slots):
            field = second_ids[q, 0, s]
            hit = (field >> shift) == g
            found = [
                jnp.where(jnp.logical_and(hit, seen == c), field & (per_block - 1), f) for c, f in enumerate(found)
            ]
            seen = seen + hit.astype(jnp.int32)
        served += found
    gather_served = gather(served)
    for r in range(RUNS):
        load_fields(r).wait()
        gather_served(served_vec, r * run, run)
        if r == 0:
            pl.semaphore_wait(barrier, devices - 1)
        for j in range(1, groups):
            vec_copy(j, r).start()
    second_vec[pl.ds(g * cap, cap)] = served_vec[pl.ds(g * cap, cap)]

    owner_of = [jnp.int32(0)] * slots
    seen = [jnp.int32(0)] * groups
    for s in range(slots):
        block = second_ids[g, 0, s] >> shift
        place = jnp.int32(0)
        for q in range(groups):
            hit = block == q
            place = jnp.where(hit, q * cap + seen[q], place)
            seen[q] = seen[q] + hit.astype(jnp.int32)
        places[s] = place
        owner_of = [jnp.where(place == p, s, t) for p, t in enumerate(owner_of)]
    for p in range(slots):
        slot_of[p] = owner_of[p]
    first_at = [first_ids[0, 0, t] - g * per_block for t in owner_of]
    second_at = [second_ids[g, 0, t] & (per_block - 1) for t in owner_of]

    def live_of(p):
        return jnp.where(slot_of[p] < count[0, 0], 1.0, 0.0)

    gather(first_at)(first_vec, 0, samples)

    def turn(p, _):
        v = first_vec[p].astype(jnp.float32)
        v = jnp.concatenate([v, jnp.zeros((extra, feature), jnp.float32)], axis=0)
        first_t[p] = v.T.astype(jnp.bfloat16)
        return 0

    lax.fori_loop(0, slots, turn, 0)
    total[...] = jnp.zeros_like(total)

    def mix(p, mat):
        v1 = first_vec[p]
        high, low = two_parts(mat)
        return dot32(jnp.concatenate([v1, v1], axis=1), jnp.concatenate([high, low], axis=0)), high, low

    def first_pass(q):
        sums = total[...]
        for c in range(cap):
            p = q * cap + c
            mixed, _, _ = mix(p, mats[slot_of[p]])
            sums = sums + (mixed * second_vec[p].astype(jnp.float32)) * live_of(p)
        total[...] = sums

    load_mats.wait()
    first_pass(g)
    for j in range(1, groups):
        for r in range(RUNS):
            vec_copy(j, r).wait_recv()
        first_pass(lax.rem(g + groups - j, groups))

    def partial_rows():
        ones = jnp.ones((SUB, feature), jnp.float32)
        tail = jnp.concatenate([total[LANES:samples], jnp.zeros((extra, feature), jnp.float32)], axis=0)
        return [
            lax.dot_general(ones, t, NT, precision=highest, preferred_element_type=jnp.float32)
            for t in (total[0:LANES], tail)
        ]

    row_id = lax.broadcasted_iota(jnp.int32, (SUB, LANES), 0)
    lane_id = lax.broadcasted_iota(jnp.int32, (SUB, LANES), 1)
    segment = cap * SUB
    span = LANES // segment

    def spot_row(ids, q):
        spots = jnp.zeros((SUB, LANES), jnp.int32)
        for c in range(cap):
            spots = jnp.where((lane_id % segment) // SUB == c, ids[q * cap + c], spots)
        spots = spots + (lane_id % SUB) * per_block
        return jnp.where(lane_id // segment == lax.rem(o, span), spots, 0).astype(jnp.float32)

    tables = jnp.zeros((SUB, LANES), jnp.float32)
    for q in range(groups):
        tables = jnp.where(row_id == FIRST_ROW + q, spot_row(first_at, q), tables)
    r0, r1 = partial_rows()
    tables = jnp.where(row_id == 0, r0, jnp.where(row_id == 1, r1, tables))
    for q in range(groups):
        msg1[q] = jnp.where(row_id == SECOND_ROW, spot_row(second_at, q), tables)

    def tile_copy(src, dst, sems, d, pick_own):
        peer = lax.rem(me + d, devices)
        pg, po = lax.div(peer, owners), lax.rem(peer, owners)
        return pltpu.make_async_remote_copy(
            src_ref=src.at[po if pick_own else pg],
            dst_ref=dst.at[me],
            send_sem=sems.at[0, peer],
            recv_sem=sems.at[1, me],
            device_id=(pg, po),
            device_id_type=MESH,
        )

    def tile_arrival(src, dst, sems, d):
        peer = lax.rem(me + d, devices)
        return pltpu.make_async_remote_copy(
            src_ref=src.at[0],
            dst_ref=dst.at[peer],
            send_sem=sems.at[0, peer],
            recv_sem=sems.at[1, peer],
            device_id=(lax.div(peer, owners), lax.rem(peer, owners)),
            device_id_type=MESH,
        )

    def send_tiles(src, dst, sems, pick_own):
        def one(d, _):
            tile_copy(src, dst, sems, d, pick_own).start()
            return 0

        lax.fori_loop(1, devices, one, 0)

    def wait_tiles(src, dst, sems):
        def one(d, _):
            tile_arrival(src, dst, sems, d).wait_recv()
            return 0

        lax.fori_loop(1, devices, one, 0)

    wanted = labels[...].astype(jnp.float32)
    targets = jnp.concatenate(
        [
            wanted[:, 0:LANES],
            jnp.concatenate([wanted[:, LANES:samples], jnp.zeros((1, extra), jnp.float32)], axis=1),
        ],
        axis=0,
    )

    def errors_of(got, at):
        sums = got[0]
        for d in range(1, devices):
            sums = sums + got[d]
        sums = sums[at : at + 2] * (1.0 / feature)
        logits = logit_scale * sums
        return logits, jax.nn.sigmoid(logits) - targets

    def error_row(err):
        return jnp.concatenate([err[0:1], err[1:2, 0 : samples - LANES]], axis=1)

    def gradient(p, erow):
        v = first_t[p][:, 0:samples].astype(jnp.float32) * erow
        high, low = two_parts(v)
        v2 = second_vec[p]
        return dot32(high, v2) + dot32(low, v2)

    send_tiles(msg1, got1, sem_m1, False)
    got1[me] = msg1[g]
    wait_tiles(msg1, got1, sem_m1)
    _, err = errors_of(got1, 0)
    erow = error_row(err)
    total[...] = jnp.zeros_like(total)
    msg2[...] = jnp.zeros_like(msg2)

    def second_pass(j):
        q = lax.rem(g + j, groups)
        sums = total[...]
        for c in range(cap):
            p = q * cap + c
            live = live_of(p)
            mid = mats[slot_of[p]] - (rate * live) * gradient(p, erow)
            mats_mid[p] = mid
            mixed, high, low = mix(p, mid)
            v2 = second_vec[p]
            first = lax.dot_general(
                jnp.concatenate([v2, v2], axis=1),
                jnp.concatenate([high, low], axis=1),
                NT,
                preferred_element_type=jnp.float32,
            )
            sums = sums + (mixed * v2.astype(jnp.float32)) * live
            factor = live * inv_root
            term_a[c] = first * factor
            term_b[c] = mixed * factor
        total[...] = sums

        def code(w, _):
            rows = pl.ds(pl.multiple_of(w * chunk, SUB), chunk)
            terms = [t[c, rows, :] for t in (term_a, term_b) for c in range(cap)]
            big = functools.reduce(jnp.maximum, [jnp.abs(t) for t in terms])
            big = jnp.maximum(jnp.max(big, axis=0, keepdims=True), 1e-30)
            gain = TOP / big
            whole = [jnp.floor(t * gain + 0.5).astype(jnp.int32) for t in terms]
            for at, out in ((0, send_a), (cap, send_b)):
                for k in range(pairs):
                    a, b = whole[at + 2 * k], whole[at + 2 * k + 1]
                    out[q, w, pl.ds(k * chunk, chunk), :] = (a & 0xFFFF) | (b << 16)
            msg2[w, pl.ds(q, 1), :] = big * (1.0 / TOP)
            return 0

        lax.fori_loop(0, owners, code, 0)

    def unit_a(j, k):
        q, w = lax.rem(g + j, groups), lax.rem(o + k, owners)
        return pltpu.make_async_remote_copy(
            src_ref=send_a.at[q, w], dst_ref=got_a.at[o, q], send_sem=sem_a.at[0, q, w],
            recv_sem=sem_a.at[1, q, o], device_id=(g, w), device_id_type=MESH,
        )

    def unit_b(j, k):
        q, w = lax.rem(g + j, groups), lax.rem(o + k, owners)
        return pltpu.make_async_remote_copy(
            src_ref=send_b.at[q, w], dst_ref=got_b.at[g, o], send_sem=sem_b.at[0, q, w],
            recv_sem=sem_b.at[1, g, o], device_id=(q, w), device_id_type=MESH,
        )

    def send_units(j):
        def one(k, _):
            unit_a(j, k).start()
            unit_b(j, k).start()
            return 0

        lax.fori_loop(1, owners, one, 0)
        q = lax.rem(g + j, groups)
        got_a[o, q] = send_a[q, o]

    second_pass(0)
    got_b[g, o] = send_b[g, o]
    send_units(0)

    def later(j, _):
        second_pass(j)
        return 0

    lax.fori_loop(1, groups, later, 0)
    r0, r1 = partial_rows()
    for w in range(owners):
        msg2[w] = jnp.where(row_id == groups, r0, jnp.where(row_id == groups + 1, r1, msg2[w]))
    send_tiles(msg2, got2, sem_m2, True)

    def send_later(j, _):
        unit_b(j, 0).start()
        send_units(j)
        return 0

    lax.fori_loop(1, groups, send_later, 0)
    got2[me] = msg2[o]
    wait_tiles(msg2, got2, sem_m2)
    logits, err = errors_of(got2, groups)
    logits_out[...] = error_row(logits)
    erow = error_row(err)
    eye = lax.broadcasted_iota(jnp.int32, (LANES, LANES), 0) == lax.broadcasted_iota(jnp.int32, (LANES, LANES), 1)
    for half in range(2):
        column = jnp.sum(jnp.where(eye, err[half : half + 1], 0.0), axis=1, keepdims=True)
        err_col[pl.ds(half * LANES, LANES), :] = jnp.broadcast_to(column, (LANES, LANES))

    def last_update(s, _):
        p = places[s]
        mats_new[s] = mats_mid[p] - (rate * live_of(p)) * gradient(p, erow)
        return 0

    lax.fori_loop(0, slots, last_update, 0)
    store_mats = pltpu.make_async_copy(mats_new, mats_out, sem_m.at[0])
    store_mats.start()

    col = err_col[pl.ds(pl.multiple_of(o * chunk, SUB), chunk), :]
    parts = chunk // SUB
    field_rows = lax.broadcasted_iota(jnp.int32, (SUB * per_block, LANES), 0)

    def decode(word_of, scale):
        out = []
        factor = col * scale
        for k in range(pairs):
            w = word_of(k)
            out.append(((w << 16) >> 16).astype(jnp.float32) * factor)
            out.append((w >> 16).astype(jnp.float32) * factor)
        return out

    def pick_of(spots):
        spots = (spots + 0.5).astype(jnp.int32)
        pick = jnp.where(field_rows == spots, 1.0, 0.0).astype(jnp.bfloat16)
        return [pick, pick]

    def rows_of(terms):
        x = jnp.concatenate(
            [jnp.concatenate([t[i * SUB : (i + 1) * SUB] for t in terms], axis=0) for i in range(parts)], axis=1
        )
        return list(two_parts(x))

    def wait_a(q, w):
        pltpu.make_async_remote_copy(
            src_ref=send_a.at[q, w], dst_ref=got_a.at[w, q], send_sem=sem_a.at[0, q, w],
            recv_sem=sem_a.at[1, q, w], device_id=(g, w), device_id_type=MESH,
        ).wait_recv()

    def wait_b(q, w):
        pltpu.make_async_remote_copy(
            src_ref=send_b.at[q, w], dst_ref=got_b.at[q, w], send_sem=sem_b.at[0, q, w],
            recv_sem=sem_b.at[1, q, w], device_id=(q, w), device_id_type=MESH,
        ).wait_recv()

    acc[...] = jnp.zeros_like(acc)

    def arrivals(n, _):
        j, h = n // (owners // span), n % (owners // span)
        qa, qb = lax.rem(g + j, groups), lax.rem(g + groups - j, groups)
        terms_a, terms_b, spots_a, spots_b = [], [], 0.0, 0.0
        for i in range(span):
            k = h * span + lax.rem(o + span - i, span)
            w = lax.rem(o + owners - k, owners)

            @pl.when(k > 0)
            def _():
                wait_a(qa, w)

            @pl.when(j + k > 0)
            def _():
                wait_b(qb, w)

            scale = got2[g * owners + w, pl.ds(qa, 1), :]
            terms_a += decode(lambda m: got_a[w, qa, pl.ds(m * chunk, chunk), :], scale)
            spots_a = spots_a + got1[g * owners + w, pl.ds(FIRST_ROW + qa, 1), :]
            scale = got2[qb * owners + w, pl.ds(g, 1), :]
            terms_b += decode(lambda m: got_b[qb, w, pl.ds(m * chunk, chunk), :], scale)
            spots_b = spots_b + got1[qb * owners + w][SECOND_ROW : SECOND_ROW + 1]
        pick = jnp.concatenate(pick_of(spots_a) + pick_of(spots_b), axis=1)
        acc[...] += dot32(pick, jnp.concatenate(rows_of(terms_a) + rows_of(terms_b), axis=0))
        return 0

    lax.fori_loop(0, groups * (owners // span), arrivals, 0)
    for i in range(parts):
        grad_out[i * SUB : (i + 1) * SUB] = acc[:, i * feature : (i + 1) * feature].reshape(SUB, per_block, feature)

    for j in range(1, groups):
        for r in range(RUNS):
            vec_copy(j, r).wait_send()

    def drain_tiles(d, _):
        tile_copy(msg1, got1, sem_m1, d, False).wait_send()
        tile_copy(msg2, got2, sem_m2, d, True).wait_send()
        return 0

    lax.fori_loop(1, devices, drain_tiles, 0)

    def drain_units(j, _):
        def one(k, _):
            unit_a(j, k).wait_send()
            unit_b(j, k).wait_send()
            return 0

        lax.fori_loop(1, owners, one, 0)

        @pl.when(j > 0)
        def _():
            unit_b(j, 0).wait_send()

        return 0

    lax.fori_loop(0, groups, drain_units, 0)
    store_mats.wait()


def on_device_kernel(fields, labels, pair_first, pair_second, pair_count, pair_mats):
    groups = lax.axis_size("grp")
    owners = lax.axis_size("own")
    samples, per_block, feature = fields.shape
    slots = pair_first.shape[2]
    cap = slots // groups
    chunk = samples // owners
    devices = groups * owners
    smem = pl.BlockSpec(memory_space=pltpu.SMEM)
    vmem = pl.BlockSpec(memory_space=pltpu.VMEM)
    hbm = pl.BlockSpec(memory_space=pl.ANY)
    rows = cap // 2 * chunk
    f32, bf16, i32 = jnp.float32, jnp.bfloat16, jnp.int32
    logits, grad, new_mats = pl.pallas_call(
        functools.partial(step_kernel, groups, owners),
        out_shape=(
            jax.ShapeDtypeStruct((1, samples), f32),
            jax.ShapeDtypeStruct((chunk, per_block, feature), f32),
            jax.ShapeDtypeStruct((slots, feature, feature), f32),
        ),
        in_specs=[smem] * 3 + [vmem] + [hbm] * 2,
        out_specs=(vmem, vmem, hbm),
        scratch_shapes=[
            pltpu.SMEM((slots,), i32),
            pltpu.SMEM((slots,), i32),
            pltpu.VMEM(fields.shape, bf16),
            pltpu.VMEM((slots, feature, feature), f32),
            pltpu.VMEM((slots, feature, feature), f32),
            pltpu.VMEM((slots, samples, feature), bf16),
            pltpu.VMEM((slots, feature, 2 * LANES), bf16),
            pltpu.VMEM((slots, samples, feature), bf16),
            pltpu.VMEM((slots, samples, feature), bf16),
            pltpu.VMEM((slots, feature, feature), f32),
            pltpu.VMEM((samples, feature), f32),
            pltpu.VMEM((groups, SUB, LANES), f32),
            pltpu.VMEM((devices, SUB, LANES), f32),
            pltpu.VMEM((owners, SUB, LANES), f32),
            pltpu.VMEM((devices, SUB, LANES), f32),
            pltpu.VMEM((cap, samples, feature), f32),
            pltpu.VMEM((cap, samples, feature), f32),
            pltpu.VMEM((groups, owners, rows, feature), i32),
            pltpu.VMEM((groups, owners, rows, feature), i32),
            pltpu.VMEM((owners, groups, rows, feature), i32),
            pltpu.VMEM((groups, owners, rows, feature), i32),
            pltpu.VMEM((2 * LANES, LANES), f32),
            pltpu.VMEM((SUB * per_block, chunk // SUB * feature), f32),
            pltpu.SemaphoreType.DMA((RUNS,)),
            pltpu.SemaphoreType.DMA((1,)),
            pltpu.SemaphoreType.DMA((2, groups, RUNS)),
            pltpu.SemaphoreType.DMA((2, devices)),
            pltpu.SemaphoreType.DMA((2, devices)),
            pltpu.SemaphoreType.DMA((2, groups, owners)),
            pltpu.SemaphoreType.DMA((2, groups, owners)),
        ],
        compiler_params=pltpu.CompilerParams(
            collective_id=0, has_side_effects=True, vmem_limit_bytes=56 * 1024 * 1024
        ),
        cost_estimate=pl.CostEstimate(flops=4 * 10**9, bytes_accessed=8 * 10**6, transcendentals=400),
    )(pair_first, pair_second, pair_count, labels.reshape(1, samples), fields, pair_mats[0, 0])
    return (logits.reshape(samples), grad, new_mats[None, None])


def fits(groups, owners, fields, pair_first):
    samples, _, feature = fields.shape
    slots = pair_first.shape[2]
    cap = slots // groups
    return (
        feature == LANES
        and slots * SUB == LANES
        and slots % groups == 0
        and cap % 2 == 0
        and LANES < samples <= 2 * LANES
        and samples % (SUB * owners) == 0
        and samples % (16 * RUNS) == 0
        and fields.shape[1] & (fields.shape[1] - 1) == 0
        and owners % (LANES // (cap * SUB)) == 0
        and FIRST_ROW + groups <= SUB
    )


def dispatch(groups, owners, fields, labels, pair_first, pair_second, pair_count, pair_mats):
    args = (fields, labels, pair_first, pair_second, pair_count, pair_mats)
    if fits(groups, owners, fields, pair_first):
        return on_device_kernel(*args)
    return on_device(*args)


def solution(mesh):
    in_specs = (
        P(None, "grp", None),
        P(),
        P("grp", "own", None),
        P(None, "own", None),
        P("grp", "own"),
        P("grp", "own", None, None, None),
    )
    out_specs = (P(), P("own", "grp", None), P("grp", "own", None, None, None))
    per_device = functools.partial(dispatch, mesh.shape["grp"], mesh.shape["own"])
    return jax.shard_map(
        per_device, mesh=mesh, in_specs=in_specs, out_specs=out_specs, check_vma=False
    )
```

```python
import functools
import math

import jax
import jax.numpy as jnp
from jax import lax
from jax.experimental import pallas as pl
from jax.experimental.pallas import tpu as pltpu
from jax.sharding import PartitionSpec as P

STEPS = 2


logit_gain = 1.5
step_size = 1000.0
highest = lax.Precision.HIGHEST


def logit_errors(partial_value, targets, logit_scale):
    total_sum = lax.psum(partial_value, ("grp", "own"))
    logits = logit_scale * total_sum
    errors = jax.nn.sigmoid(logits) - targets
    return (logits, errors)


def on_device(fields, labels, pair_first, pair_second, pair_count, pair_mats):
    groups = lax.axis_size("grp")
    owners = lax.axis_size("own")
    my_group = lax.axis_index("grp")
    samples, per_block, feature = fields.shape
    slot_count = pair_first.shape[2]
    capacity = slot_count // groups
    second_table = pair_second[:, 0, :]
    block_ids = second_table // per_block
    offsets = second_table % per_block
    member = (block_ids[:, :, None] == jnp.arange(groups, dtype=jnp.int32)[None, None, :]).astype(
        jnp.int32
    )
    slot_ranks = jnp.sum((jnp.cumsum(member, axis=1) - 1) * member, axis=2)
    places = block_ids * capacity + slot_ranks
    chosen = (block_ids[:, :, None] == my_group) & (
        slot_ranks[:, :, None] == jnp.arange(capacity, dtype=jnp.int32)[None, None, :]
    )
    served = jnp.sum(jnp.where(chosen, offsets[:, :, None], 0), axis=1).reshape(-1)
    outgoing = jnp.take(fields, served, axis=1)
    incoming = lax.all_to_all(outgoing, "grp", split_axis=1, concat_axis=1, tiled=True)
    my_places = lax.dynamic_index_in_dim(places, my_group, 0, keepdims=False)
    second_vec = jnp.take(incoming, my_places, axis=1).astype(jnp.float32)
    first_local = pair_first[0, 0] - my_group * per_block
    first_vec = jnp.take(fields, first_local, axis=1).astype(jnp.float32)
    live_mask = (jnp.arange(slot_count, dtype=jnp.int32) < pair_count[0, 0]).astype(jnp.float32)
    matrices = pair_mats[0, 0]
    targets = labels.astype(jnp.float32)
    logit_scale = logit_gain / math.sqrt(groups * owners * slot_count)
    root_width = math.sqrt(feature)
    logits = jnp.zeros((samples,), jnp.float32)
    grad_first = jnp.zeros(first_vec.shape, jnp.float32)
    grad_second = jnp.zeros(first_vec.shape, jnp.float32)
    for step_index in range(STEPS):
        mixed = jnp.einsum("bsk,skl->bsl", first_vec, matrices, precision=highest)
        partial_value = jnp.sum(
            jnp.sum(mixed * second_vec, axis=2) / feature * live_mask[None, :], axis=1
        )
        logits, errors = logit_errors(partial_value, targets, logit_scale)
        if step_index == STEPS - 1:
            grad_first = (
                errors[:, None, None]
                * jnp.einsum("skl,bsl->bsk", matrices, second_vec, precision=highest)
                / root_width
                * live_mask[None, :, None]
            )
            grad_second = errors[:, None, None] * mixed / root_width * live_mask[None, :, None]
        gradient = jnp.einsum(
            "bsk,bsl->skl", first_vec * errors[:, None, None], second_vec, precision=highest
        )
        matrices = (
            matrices
            - step_size * logit_scale / (samples * feature) * live_mask[:, None, None] * gradient
        )
    slot_iota = jnp.arange(slot_count, dtype=jnp.int32)
    slot_of = jnp.sum(
        jnp.where(my_places[None, :] == slot_iota[:, None], slot_iota[None, :], 0), axis=1
    )
    returned = lax.all_to_all(
        jnp.take(grad_second, slot_of, axis=1), "grp", split_axis=1, concat_axis=1, tiled=True
    )
    block_iota = jnp.arange(per_block, dtype=jnp.int32)
    pick_second = (served[:, None] == block_iota[None, :]).astype(jnp.float32)
    pick_first = (first_local[:, None] == block_iota[None, :]).astype(jnp.float32)
    dense_grad = jnp.einsum("bsk,sf->bfk", grad_first, pick_first, precision=highest)
    dense_grad = dense_grad + jnp.einsum("bpk,pf->bfk", returned, pick_second, precision=highest)
    field_grad = lax.psum_scatter(dense_grad, "own", scatter_dimension=0, tiled=True)
    return (logits, field_grad, matrices[None, None])


LANES = 128
SUB = 8
TOP = 32760.0
RUNS = 4
SECOND_ROW = 2
FIRST_ROW = 4
MESH = pl.DeviceIdType.MESH
NT = (((1,), (1,)), ((), ()))


def two_parts(x):
    high = x.astype(jnp.bfloat16)
    low = (x - high.astype(jnp.float32)).astype(jnp.bfloat16)
    return high, low


def dot32(a, b):
    return jnp.dot(a, b, preferred_element_type=jnp.float32)


def step_kernel(
    groups, owners,
    first_ids, second_ids, count, labels, fields_in, mats_in,
    logits_out, grad_out, mats_out,
    slot_of, places, fields, mats,
    first_vec, first_t, served_vec, second_vec, mats_mid, total,
    msg1, got1, msg2, got2, term_a, term_b, send_a, send_b, got_a, got_b, err_col, acc,
    sem_f, sem_m, sem_v, sem_m1, sem_m2, sem_a, sem_b,
):
    samples, per_block, feature = fields.shape
    shift = per_block.bit_length() - 1
    slots = mats.shape[0]
    cap = slots // groups
    chunk = samples // owners
    devices = groups * owners
    pairs = cap // 2
    g, o = lax.axis_index("grp"), lax.axis_index("own")
    me = g * owners + o
    logit_scale = logit_gain / math.sqrt(devices * slots)
    rate = step_size * logit_scale / (samples * feature)
    inv_root = 1.0 / math.sqrt(feature)
    extra = 2 * LANES - samples

    run = samples // RUNS

    def load_fields(r):
        part = pl.ds(r * run, run)
        return pltpu.make_async_copy(fields_in.at[part], fields.at[part], sem_f.at[r])

    for r in range(RUNS):
        load_fields(r).start()
    load_mats = pltpu.make_async_copy(mats_in, mats, sem_m.at[0])
    load_mats.start()

    barrier = pltpu.get_barrier_semaphore()

    def greet(d, _):
        peer = lax.rem(me + d, devices)
        pl.semaphore_signal(
            barrier, inc=1, device_id=(lax.div(peer, owners), lax.rem(peer, owners)), device_id_type=MESH
        )
        return 0

    lax.fori_loop(1, devices, greet, 0)

    def gather(spots):
        wide = SUB * per_block
        lanes = lax.broadcasted_iota(jnp.int32, (SUB, wide), 1)
        lanes = lanes - lax.broadcasted_iota(jnp.int32, (SUB, wide), 0) * per_block
        pick = jnp.concatenate([jnp.where(lanes == f, 1.0, 0.0) for f in spots], axis=0).astype(jnp.bfloat16)

        def rows(out, start, size):
            def part(i, _):
                at = pl.multiple_of(start + i * 16, 16)
                halves = []
                for h in range(2):
                    block = fields[pl.ds(at + h * SUB, SUB)].reshape(wide, feature)
                    halves.append(dot32(pick, block).reshape(slots, SUB, feature))
                out[:, pl.ds(at, 16), :] = jnp.concatenate(halves, axis=1).astype(jnp.bfloat16)
                return 0

            lax.fori_loop(0, size // 16, part, 0)

        return rows

    def vec_copy(j, r):
        to = lax.rem(g + j, groups)
        part = pl.ds(r * run, run)
        return pltpu.make_async_remote_copy(
            src_ref=served_vec.at[pl.ds(to * cap, cap), part],
            dst_ref=second_vec.at[pl.ds(g * cap, cap), part],
            send_sem=sem_v.at[0, j, r],
            recv_sem=sem_v.at[1, j, r],
            device_id=(to, o),
            device_id_type=MESH,
        )

    served = []
    for q in range(groups):
        found, seen = [jnp.int32(0)] * cap, jnp.int32(0)
        for s in range(slots):
            field = second_ids[q, 0, s]
            hit = (field >> shift) == g
            found = [
                jnp.where(jnp.logical_and(hit, seen == c), field & (per_block - 1), f) for c, f in enumerate(found)
            ]
            seen = seen + hit.astype(jnp.int32)
        served += found
    gather_served = gather(served)
    for r in range(RUNS):
        load_fields(r).wait()
        gather_served(served_vec, r * run, run)
        if r == 0:
            pl.semaphore_wait(barrier, devices - 1)
        for j in range(1, groups):
            vec_copy(j, r).start()
    second_vec[pl.ds(g * cap, cap)] = served_vec[pl.ds(g * cap, cap)]

    owner_of = [jnp.int32(0)] * slots
    seen = [jnp.int32(0)] * groups
    for s in range(slots):
        block = second_ids[g, 0, s] >> shift
        place = jnp.int32(0)
        for q in range(groups):
            hit = block == q
            place = jnp.where(hit, q * cap + seen[q], place)
            seen[q] = seen[q] + hit.astype(jnp.int32)
        places[s] = place
        owner_of = [jnp.where(place == p, s, t) for p, t in enumerate(owner_of)]
    for p in range(slots):
        slot_of[p] = owner_of[p]
    first_at = [first_ids[0, 0, t] - g * per_block for t in owner_of]
    second_at = [second_ids[g, 0, t] & (per_block - 1) for t in owner_of]

    def live_of(p):
        return jnp.where(slot_of[p] < count[0, 0], 1.0, 0.0)

    gather(first_at)(first_vec, 0, samples)

    def turn(p, _):
        v = first_vec[p].astype(jnp.float32)
        v = jnp.concatenate([v, jnp.zeros((extra, feature), jnp.float32)], axis=0)
        first_t[p] = v.T.astype(jnp.bfloat16)
        return 0

    lax.fori_loop(0, slots, turn, 0)
    total[...] = jnp.zeros_like(total)

    def mix(p, mat):
        v1 = first_vec[p]
        high, low = two_parts(mat)
        return dot32(jnp.concatenate([v1, v1], axis=1), jnp.concatenate([high, low], axis=0)), high, low

    def first_pass(q):
        sums = total[...]
        for c in range(cap):
            p = q * cap + c
            mixed, _, _ = mix(p, mats[slot_of[p]])
            sums = sums + (mixed * second_vec[p].astype(jnp.float32)) * live_of(p)
        total[...] = sums

    load_mats.wait()
    first_pass(g)
    for j in range(1, groups):
        for r in range(RUNS):
            vec_copy(j, r).wait_recv()
        first_pass(lax.rem(g + groups - j, groups))

    def partial_rows():
        ones = jnp.ones((SUB, feature), jnp.float32)
        tail = jnp.concatenate([total[LANES:samples], jnp.zeros((extra, feature), jnp.float32)], axis=0)
        return [
            lax.dot_general(ones, t, NT, precision=highest, preferred_element_type=jnp.float32)
            for t in (total[0:LANES], tail)
        ]

    row_id = lax.broadcasted_iota(jnp.int32, (SUB, LANES), 0)
    lane_id = lax.broadcasted_iota(jnp.int32, (SUB, LANES), 1)
    segment = cap * SUB
    span = LANES // segment

    def spot_row(ids, q):
        spots = jnp.zeros((SUB, LANES), jnp.int32)
        for c in range(cap):
            spots = jnp.where((lane_id % segment) // SUB == c, ids[q * cap + c], spots)
        spots = spots + (lane_id % SUB) * per_block
        return jnp.where(lane_id // segment == lax.rem(o, span), spots, 0).astype(jnp.float32)

    tables = jnp.zeros((SUB, LANES), jnp.float32)
    for q in range(groups):
        tables = jnp.where(row_id == FIRST_ROW + q, spot_row(first_at, q), tables)
    r0, r1 = partial_rows()
    tables = jnp.where(row_id == 0, r0, jnp.where(row_id == 1, r1, tables))
    for q in range(groups):
        msg1[q] = jnp.where(row_id == SECOND_ROW, spot_row(second_at, q), tables)

    def tile_copy(src, dst, sems, d, pick_own):
        peer = lax.rem(me + d, devices)
        pg, po = lax.div(peer, owners), lax.rem(peer, owners)
        return pltpu.make_async_remote_copy(
            src_ref=src.at[po if pick_own else pg],
            dst_ref=dst.at[me],
            send_sem=sems.at[0, peer],
            recv_sem=sems.at[1, me],
            device_id=(pg, po),
            device_id_type=MESH,
        )

    def tile_arrival(src, dst, sems, d):
        peer = lax.rem(me + d, devices)
        return pltpu.make_async_remote_copy(
            src_ref=src.at[0],
            dst_ref=dst.at[peer],
            send_sem=sems.at[0, peer],
            recv_sem=sems.at[1, peer],
            device_id=(lax.div(peer, owners), lax.rem(peer, owners)),
            device_id_type=MESH,
        )

    def send_tiles(src, dst, sems, pick_own):
        def one(d, _):
            tile_copy(src, dst, sems, d, pick_own).start()
            return 0

        lax.fori_loop(1, devices, one, 0)

    def wait_tiles(src, dst, sems):
        def one(d, _):
            tile_arrival(src, dst, sems, d).wait_recv()
            return 0

        lax.fori_loop(1, devices, one, 0)

    wanted = labels[...].astype(jnp.float32)
    targets = jnp.concatenate(
        [
            wanted[:, 0:LANES],
            jnp.concatenate([wanted[:, LANES:samples], jnp.zeros((1, extra), jnp.float32)], axis=1),
        ],
        axis=0,
    )

    def errors_of(got, at):
        sums = got[0]
        for d in range(1, devices):
            sums = sums + got[d]
        sums = sums[at : at + 2] * (1.0 / feature)
        logits = logit_scale * sums
        return logits, jax.nn.sigmoid(logits) - targets

    def error_row(err):
        return jnp.concatenate([err[0:1], err[1:2, 0 : samples - LANES]], axis=1)

    def gradient(p, erow):
        v = first_t[p][:, 0:samples].astype(jnp.float32) * erow
        high, low = two_parts(v)
        v2 = second_vec[p]
        return dot32(high, v2) + dot32(low, v2)

    send_tiles(msg1, got1, sem_m1, False)
    got1[me] = msg1[g]
    wait_tiles(msg1, got1, sem_m1)
    _, err = errors_of(got1, 0)
    erow = error_row(err)
    total[...] = jnp.zeros_like(total)
    msg2[...] = jnp.zeros_like(msg2)

    def second_pass(j):
        q = lax.rem(g + j, groups)
        sums = total[...]
        for c in range(cap):
            p = q * cap + c
            live = live_of(p)
            mid = mats[slot_of[p]] - (rate * live) * gradient(p, erow)
            mats_mid[p] = mid
            mixed, high, low = mix(p, mid)
            v2 = second_vec[p]
            first = lax.dot_general(
                jnp.concatenate([v2, v2], axis=1),
                jnp.concatenate([high, low], axis=1),
                NT,
                preferred_element_type=jnp.float32,
            )
            sums = sums + (mixed * v2.astype(jnp.float32)) * live
            factor = live * inv_root
            term_a[c] = first * factor
            term_b[c] = mixed * factor
        total[...] = sums

        def code(w, _):
            rows = pl.ds(pl.multiple_of(w * chunk, SUB), chunk)
            terms = [t[c, rows, :] for t in (term_a, term_b) for c in range(cap)]
            big = functools.reduce(jnp.maximum, [jnp.abs(t) for t in terms])
            big = jnp.maximum(jnp.max(big, axis=0, keepdims=True), 1e-30)
            gain = TOP / big
            whole = [jnp.floor(t * gain + 0.5).astype(jnp.int32) for t in terms]
            for at, out in ((0, send_a), (cap, send_b)):
                for k in range(pairs):
                    a, b = whole[at + 2 * k], whole[at + 2 * k + 1]
                    out[q, w, pl.ds(k * chunk, chunk), :] = (a & 0xFFFF) | (b << 16)
            msg2[w, pl.ds(q, 1), :] = big * (1.0 / TOP)
            return 0

        lax.fori_loop(0, owners, code, 0)

    def partner(k):
        w, bit = o, 1
        while bit < owners:
            w = w + ((k // bit) % 2) * (bit - 2 * bit * ((w // bit) % 2))
            bit *= 2
        return w

    order = [k for pair in zip(range(owners // 2, owners), [*range(1, owners // 2), 0]) for k in pair if k]

    def unit_a(j, k):
        q, w = lax.rem(g + j, groups), partner(k)
        return pltpu.make_async_remote_copy(
            src_ref=send_a.at[q, w], dst_ref=got_a.at[o, q], send_sem=sem_a.at[0, q, w],
            recv_sem=sem_a.at[1, q, o], device_id=(g, w), device_id_type=MESH,
        )

    def unit_b(j, k):
        q, w = lax.rem(g + j, groups), partner(k)
        return pltpu.make_async_remote_copy(
            src_ref=send_b.at[q, w], dst_ref=got_b.at[g, o], send_sem=sem_b.at[0, q, w],
            recv_sem=sem_b.at[1, g, o], device_id=(q, w), device_id_type=MESH,
        )

    def send_units(j):
        for k in order:
            unit_a(j, k).start()
            unit_b(j, k).start()
        q = lax.rem(g + j, groups)
        got_a[o, q] = send_a[q, o]

    second_pass(0)
    got_b[g, o] = send_b[g, o]
    send_units(0)

    def later(j, _):
        second_pass(j)
        return 0

    lax.fori_loop(1, groups, later, 0)
    r0, r1 = partial_rows()
    for w in range(owners):
        msg2[w] = jnp.where(row_id == groups, r0, jnp.where(row_id == groups + 1, r1, msg2[w]))
    send_tiles(msg2, got2, sem_m2, True)

    def send_later(j, _):
        unit_b(j, 0).start()
        send_units(j)
        return 0

    lax.fori_loop(1, groups, send_later, 0)
    got2[me] = msg2[o]
    wait_tiles(msg2, got2, sem_m2)
    logits, err = errors_of(got2, groups)
    logits_out[...] = error_row(logits)
    erow = error_row(err)
    eye = lax.broadcasted_iota(jnp.int32, (LANES, LANES), 0) == lax.broadcasted_iota(jnp.int32, (LANES, LANES), 1)
    for half in range(2):
        column = jnp.sum(jnp.where(eye, err[half : half + 1], 0.0), axis=1, keepdims=True)
        err_col[pl.ds(half * LANES, LANES), :] = jnp.broadcast_to(column, (LANES, LANES))

    def last_update(s, _):
        p = places[s]
        mats_out[s] = mats_mid[p] - (rate * live_of(p)) * gradient(p, erow)
        return 0

    lax.fori_loop(0, slots, last_update, 0)

    col = err_col[pl.ds(pl.multiple_of(o * chunk, SUB), chunk), :]
    parts = chunk // SUB
    field_rows = lax.broadcasted_iota(jnp.int32, (SUB * per_block, LANES), 0)

    def decode(word_of, scale):
        out = []
        factor = col * scale
        for k in range(pairs):
            w = word_of(k)
            out.append(((w << 16) >> 16).astype(jnp.float32) * factor)
            out.append((w >> 16).astype(jnp.float32) * factor)
        return out

    def pick_of(spots):
        spots = (spots + 0.5).astype(jnp.int32)
        pick = jnp.where(field_rows == spots, 1.0, 0.0).astype(jnp.bfloat16)
        return [pick, pick]

    def rows_of(terms):
        x = jnp.concatenate(
            [jnp.concatenate([t[i * SUB : (i + 1) * SUB] for t in terms], axis=0) for i in range(parts)], axis=1
        )
        return list(two_parts(x))

    def wait_a(q, w):
        pltpu.make_async_remote_copy(
            src_ref=send_a.at[q, w], dst_ref=got_a.at[w, q], send_sem=sem_a.at[0, q, w],
            recv_sem=sem_a.at[1, q, w], device_id=(g, w), device_id_type=MESH,
        ).wait_recv()

    def wait_b(q, w):
        pltpu.make_async_remote_copy(
            src_ref=send_b.at[q, w], dst_ref=got_b.at[q, w], send_sem=sem_b.at[0, q, w],
            recv_sem=sem_b.at[1, q, w], device_id=(q, w), device_id_type=MESH,
        ).wait_recv()

    acc[...] = jnp.zeros_like(acc)

    def arrivals(n, _):
        j, h = n // (owners // span), n % (owners // span)
        qa, qb = lax.rem(g + j, groups), lax.rem(g + groups - j, groups)
        terms_a, terms_b, spots_a, spots_b = [], [], 0.0, 0.0
        for i in range(span):
            k = h * span + partner(i) % span
            w = partner(k)

            @pl.when(k > 0)
            def _():
                wait_a(qa, w)

            @pl.when(j + k > 0)
            def _():
                wait_b(qb, w)

            scale = got2[g * owners + w, pl.ds(qa, 1), :]
            terms_a += decode(lambda m: got_a[w, qa, pl.ds(m * chunk, chunk), :], scale)
            spots_a = spots_a + got1[g * owners + w, pl.ds(FIRST_ROW + qa, 1), :]
            scale = got2[qb * owners + w, pl.ds(g, 1), :]
            terms_b += decode(lambda m: got_b[qb, w, pl.ds(m * chunk, chunk), :], scale)
            spots_b = spots_b + got1[qb * owners + w][SECOND_ROW : SECOND_ROW + 1]
        pick = jnp.concatenate(pick_of(spots_a) + pick_of(spots_b), axis=1)
        acc[...] += dot32(pick, jnp.concatenate(rows_of(terms_a) + rows_of(terms_b), axis=0))
        return 0

    lax.fori_loop(0, groups * (owners // span), arrivals, 0)
    for i in range(parts):
        grad_out[i * SUB : (i + 1) * SUB] = acc[:, i * feature : (i + 1) * feature].reshape(SUB, per_block, feature)

    for j in range(1, groups):
        for r in range(RUNS):
            vec_copy(j, r).wait_send()

    def drain_tiles(d, _):
        tile_copy(msg1, got1, sem_m1, d, False).wait_send()
        tile_copy(msg2, got2, sem_m2, d, True).wait_send()
        return 0

    lax.fori_loop(1, devices, drain_tiles, 0)

    def drain_units(j, _):
        def one(k, _):
            unit_a(j, k).wait_send()
            unit_b(j, k).wait_send()
            return 0

        lax.fori_loop(1, owners, one, 0)

        @pl.when(j > 0)
        def _():
            unit_b(j, 0).wait_send()

        return 0

    lax.fori_loop(0, groups, drain_units, 0)


def on_device_kernel(fields, labels, pair_first, pair_second, pair_count, pair_mats):
    groups = lax.axis_size("grp")
    owners = lax.axis_size("own")
    samples, per_block, feature = fields.shape
    slots = pair_first.shape[2]
    cap = slots // groups
    chunk = samples // owners
    devices = groups * owners
    smem = pl.BlockSpec(memory_space=pltpu.SMEM)
    vmem = pl.BlockSpec(memory_space=pltpu.VMEM)
    hbm = pl.BlockSpec(memory_space=pltpu.HBM)
    rows = cap // 2 * chunk
    f32, bf16, i32 = jnp.float32, jnp.bfloat16, jnp.int32
    logits, grad, new_mats = pl.pallas_call(
        functools.partial(step_kernel, groups, owners),
        out_shape=(
            jax.ShapeDtypeStruct((1, samples), f32),
            jax.ShapeDtypeStruct((chunk, per_block, feature), f32),
            jax.ShapeDtypeStruct((slots, feature, feature), f32),
        ),
        in_specs=[smem] * 3 + [vmem] + [hbm] * 2,
        out_specs=(vmem,) * 3,
        scratch_shapes=[
            pltpu.SMEM((slots,), i32),
            pltpu.SMEM((slots,), i32),
            pltpu.VMEM(fields.shape, bf16),
            pltpu.VMEM((slots, feature, feature), f32),
            pltpu.VMEM((slots, samples, feature), bf16),
            pltpu.VMEM((slots, feature, 2 * LANES), bf16),
            pltpu.VMEM((slots, samples, feature), bf16),
            pltpu.VMEM((slots, samples, feature), bf16),
            pltpu.VMEM((slots, feature, feature), f32),
            pltpu.VMEM((samples, feature), f32),
            pltpu.VMEM((groups, SUB, LANES), f32),
            pltpu.VMEM((devices, SUB, LANES), f32),
            pltpu.VMEM((owners, SUB, LANES), f32),
            pltpu.VMEM((devices, SUB, LANES), f32),
            pltpu.VMEM((cap, samples, feature), f32),
            pltpu.VMEM((cap, samples, feature), f32),
            pltpu.VMEM((groups, owners, rows, feature), i32),
            pltpu.VMEM((groups, owners, rows, feature), i32),
            pltpu.VMEM((owners, groups, rows, feature), i32),
            pltpu.VMEM((groups, owners, rows, feature), i32),
            pltpu.VMEM((2 * LANES, LANES), f32),
            pltpu.VMEM((SUB * per_block, chunk // SUB * feature), f32),
            pltpu.SemaphoreType.DMA((RUNS,)),
            pltpu.SemaphoreType.DMA((1,)),
            pltpu.SemaphoreType.DMA((2, groups, RUNS)),
            pltpu.SemaphoreType.DMA((2, devices)),
            pltpu.SemaphoreType.DMA((2, devices)),
            pltpu.SemaphoreType.DMA((2, groups, owners)),
            pltpu.SemaphoreType.DMA((2, groups, owners)),
        ],
        compiler_params=pltpu.CompilerParams(
            collective_id=0, has_side_effects=True, vmem_limit_bytes=52 * 1024 * 1024
        ),
        cost_estimate=pl.CostEstimate(flops=4 * 10**9, bytes_accessed=8 * 10**6, transcendentals=400),
    )(pair_first, pair_second, pair_count, labels.reshape(1, samples), fields, pair_mats[0, 0])
    return (logits.reshape(samples), grad, new_mats[None, None])


def fits(groups, owners, fields, pair_first):
    samples, _, feature = fields.shape
    slots = pair_first.shape[2]
    cap = slots // groups
    return (
        feature == LANES
        and slots * SUB == LANES
        and slots % groups == 0
        and cap % 2 == 0
        and LANES < samples <= 2 * LANES
        and samples % (SUB * owners) == 0
        and samples % (16 * RUNS) == 0
        and fields.shape[1] & (fields.shape[1] - 1) == 0
        and owners & (owners - 1) == 0
        and owners % (LANES // (cap * SUB)) == 0
        and FIRST_ROW + groups <= SUB
    )


def dispatch(groups, owners, fields, labels, pair_first, pair_second, pair_count, pair_mats):
    args = (fields, labels, pair_first, pair_second, pair_count, pair_mats)
    if fits(groups, owners, fields, pair_first):
        return on_device_kernel(*args)
    return on_device(*args)


def solution(mesh):
    in_specs = (
        P(None, "grp", None),
        P(),
        P("grp", "own", None),
        P(None, "own", None),
        P("grp", "own"),
        P("grp", "own", None, None, None),
    )
    out_specs = (P(), P("own", "grp", None), P("grp", "own", None, None, None))
    per_device = functools.partial(dispatch, mesh.shape["grp"], mesh.shape["own"])
    return jax.shard_map(
        per_device, mesh=mesh, in_specs=in_specs, out_specs=out_specs, check_vma=False
    )
```

```python
import functools
import math

import jax
import jax.numpy as jnp
from jax import lax
from jax.experimental import pallas as pl
from jax.experimental.pallas import tpu as pltpu
from jax.sharding import PartitionSpec as P

STEPS = 2


logit_gain = 1.5
step_size = 1000.0
highest = lax.Precision.HIGHEST


def logit_errors(partial_value, targets, logit_scale):
    total_sum = lax.psum(partial_value, ("grp", "own"))
    logits = logit_scale * total_sum
    errors = jax.nn.sigmoid(logits) - targets
    return (logits, errors)


def on_device(fields, labels, pair_first, pair_second, pair_count, pair_mats):
    groups = lax.axis_size("grp")
    owners = lax.axis_size("own")
    my_group = lax.axis_index("grp")
    samples, per_block, feature = fields.shape
    slot_count = pair_first.shape[2]
    capacity = slot_count // groups
    second_table = pair_second[:, 0, :]
    block_ids = second_table // per_block
    offsets = second_table % per_block
    member = (block_ids[:, :, None] == jnp.arange(groups, dtype=jnp.int32)[None, None, :]).astype(
        jnp.int32
    )
    slot_ranks = jnp.sum((jnp.cumsum(member, axis=1) - 1) * member, axis=2)
    places = block_ids * capacity + slot_ranks
    chosen = (block_ids[:, :, None] == my_group) & (
        slot_ranks[:, :, None] == jnp.arange(capacity, dtype=jnp.int32)[None, None, :]
    )
    served = jnp.sum(jnp.where(chosen, offsets[:, :, None], 0), axis=1).reshape(-1)
    outgoing = jnp.take(fields, served, axis=1)
    incoming = lax.all_to_all(outgoing, "grp", split_axis=1, concat_axis=1, tiled=True)
    my_places = lax.dynamic_index_in_dim(places, my_group, 0, keepdims=False)
    second_vec = jnp.take(incoming, my_places, axis=1).astype(jnp.float32)
    first_local = pair_first[0, 0] - my_group * per_block
    first_vec = jnp.take(fields, first_local, axis=1).astype(jnp.float32)
    live_mask = (jnp.arange(slot_count, dtype=jnp.int32) < pair_count[0, 0]).astype(jnp.float32)
    matrices = pair_mats[0, 0]
    targets = labels.astype(jnp.float32)
    logit_scale = logit_gain / math.sqrt(groups * owners * slot_count)
    root_width = math.sqrt(feature)
    logits = jnp.zeros((samples,), jnp.float32)
    grad_first = jnp.zeros(first_vec.shape, jnp.float32)
    grad_second = jnp.zeros(first_vec.shape, jnp.float32)
    for step_index in range(STEPS):
        mixed = jnp.einsum("bsk,skl->bsl", first_vec, matrices, precision=highest)
        partial_value = jnp.sum(
            jnp.sum(mixed * second_vec, axis=2) / feature * live_mask[None, :], axis=1
        )
        logits, errors = logit_errors(partial_value, targets, logit_scale)
        if step_index == STEPS - 1:
            grad_first = (
                errors[:, None, None]
                * jnp.einsum("skl,bsl->bsk", matrices, second_vec, precision=highest)
                / root_width
                * live_mask[None, :, None]
            )
            grad_second = errors[:, None, None] * mixed / root_width * live_mask[None, :, None]
        gradient = jnp.einsum(
            "bsk,bsl->skl", first_vec * errors[:, None, None], second_vec, precision=highest
        )
        matrices = (
            matrices
            - step_size * logit_scale / (samples * feature) * live_mask[:, None, None] * gradient
        )
    slot_iota = jnp.arange(slot_count, dtype=jnp.int32)
    slot_of = jnp.sum(
        jnp.where(my_places[None, :] == slot_iota[:, None], slot_iota[None, :], 0), axis=1
    )
    returned = lax.all_to_all(
        jnp.take(grad_second, slot_of, axis=1), "grp", split_axis=1, concat_axis=1, tiled=True
    )
    block_iota = jnp.arange(per_block, dtype=jnp.int32)
    pick_second = (served[:, None] == block_iota[None, :]).astype(jnp.float32)
    pick_first = (first_local[:, None] == block_iota[None, :]).astype(jnp.float32)
    dense_grad = jnp.einsum("bsk,sf->bfk", grad_first, pick_first, precision=highest)
    dense_grad = dense_grad + jnp.einsum("bpk,pf->bfk", returned, pick_second, precision=highest)
    field_grad = lax.psum_scatter(dense_grad, "own", scatter_dimension=0, tiled=True)
    return (logits, field_grad, matrices[None, None])


LANES = 128
SUB = 8
TOP = 32760.0
RUNS = 4
EARLY = 2
SECOND_ROW = 2
FIRST_ROW = 4
MESH = pl.DeviceIdType.MESH
NT = (((1,), (1,)), ((), ()))


def two_parts(x):
    high = x.astype(jnp.bfloat16)
    low = (x - high.astype(jnp.float32)).astype(jnp.bfloat16)
    return high, low


def dot32(a, b):
    return jnp.dot(a, b, preferred_element_type=jnp.float32)


def step_kernel(
    groups, owners,
    small, small_vec, fields_in, mats_in,
    logits_out, grad_out, mats_out,
    slot_of, places, fields, mats,
    first_vec, first_t, served_vec, second_vec, mats_mid, total,
    msg1, got1, msg2, got2, term_a, term_b, send_a, send_b, got_a, got_b, err_col, acc,
    sem_f, sem_m, sem_v, sem_m1, sem_m2, sem_a, sem_b,
):
    samples, per_block, feature = fields.shape
    first_base = 2 * LANES
    second_base = first_base + mats.shape[0]
    count_at = second_base + groups * mats.shape[0]
    shift = per_block.bit_length() - 1
    slots = mats.shape[0]
    cap = slots // groups
    chunk = samples // owners
    devices = groups * owners
    pairs = cap // 2
    g, o = lax.axis_index("grp"), lax.axis_index("own")
    me = g * owners + o
    logit_scale = logit_gain / math.sqrt(devices * slots)
    rate = step_size * logit_scale / (samples * feature)
    inv_root = 1.0 / math.sqrt(feature)
    extra = 2 * LANES - samples

    run = samples // RUNS

    def load_fields(r):
        part = pl.ds(r * run, run)
        return pltpu.make_async_copy(fields_in.at[part], fields.at[part], sem_f.at[r])

    for r in range(RUNS):
        load_fields(r).start()
    load_mats = pltpu.make_async_copy(mats_in, mats, sem_m.at[0])
    load_mats.start()

    barrier = pltpu.get_barrier_semaphore()

    def greet(d, _):
        peer = lax.rem(me + d, devices)
        pl.semaphore_signal(
            barrier, inc=1, device_id=(lax.div(peer, owners), lax.rem(peer, owners)), device_id_type=MESH
        )
        return 0

    lax.fori_loop(1, devices, greet, 0)

    def gather(spots):
        wide = SUB * per_block
        lanes = lax.broadcasted_iota(jnp.int32, (SUB, wide), 1)
        lanes = lanes - lax.broadcasted_iota(jnp.int32, (SUB, wide), 0) * per_block
        pick = jnp.concatenate([jnp.where(lanes == f, 1.0, 0.0) for f in spots], axis=0).astype(jnp.bfloat16)

        def rows(out, start, size):
            def part(i, _):
                at = pl.multiple_of(start + i * 16, 16)
                halves = []
                for h in range(2):
                    block = fields[pl.ds(at + h * SUB, SUB)].reshape(wide, feature)
                    halves.append(dot32(pick, block).reshape(slots, SUB, feature))
                out[:, pl.ds(at, 16), :] = jnp.concatenate(halves, axis=1).astype(jnp.bfloat16)
                return 0

            lax.fori_loop(0, size // 16, part, 0)

        return rows

    def vec_copy(j, r):
        to = lax.rem(g + j, groups)
        part = pl.ds(r * run, run)
        return pltpu.make_async_remote_copy(
            src_ref=served_vec.at[pl.ds(to * cap, cap), part],
            dst_ref=second_vec.at[pl.ds(g * cap, cap), part],
            send_sem=sem_v.at[0, j, r],
            recv_sem=sem_v.at[1, j, r],
            device_id=(to, o),
            device_id_type=MESH,
        )

    served = []
    for q in range(groups):
        found, seen = [jnp.int32(0)] * cap, jnp.int32(0)
        for s in range(slots):
            field = small[0, second_base + q * slots + s]
            hit = (field >> shift) == g
            found = [
                jnp.where(jnp.logical_and(hit, seen == c), field & (per_block - 1), f) for c, f in enumerate(found)
            ]
            seen = seen + hit.astype(jnp.int32)
        served += found
    gather_served = gather(served)
    for r in range(RUNS):
        load_fields(r).wait()
        gather_served(served_vec, r * run, run)
        if r == 0:
            pl.semaphore_wait(barrier, devices - 1)
        for j in range(1, groups):
            vec_copy(j, r).start()
    second_vec[pl.ds(g * cap, cap)] = served_vec[pl.ds(g * cap, cap)]

    owner_of = [jnp.int32(0)] * slots
    seen = [jnp.int32(0)] * groups
    for s in range(slots):
        block = small[0, second_base + g * slots + s] >> shift
        place = jnp.int32(0)
        for q in range(groups):
            hit = block == q
            place = jnp.where(hit, q * cap + seen[q], place)
            seen[q] = seen[q] + hit.astype(jnp.int32)
        places[s] = place
        owner_of = [jnp.where(place == p, s, t) for p, t in enumerate(owner_of)]
    for p in range(slots):
        slot_of[p] = owner_of[p]
    first_at = [small[0, first_base + t] - g * per_block for t in owner_of]
    second_at = [small[0, second_base + g * slots + t] & (per_block - 1) for t in owner_of]

    def live_of(p):
        return jnp.where(slot_of[p] < small[0, count_at], 1.0, 0.0)

    gather(first_at)(first_vec, 0, samples)

    def turn(p, _):
        v = first_vec[p].astype(jnp.float32)
        v = jnp.concatenate([v, jnp.zeros((extra, feature), jnp.float32)], axis=0)
        first_t[p] = v.T.astype(jnp.bfloat16)
        return 0

    lax.fori_loop(0, slots, turn, 0)
    total[...] = jnp.zeros_like(total)

    def first_pass(q):
        spots = [q * cap + c for c in range(cap)]
        split = [two_parts(mats[slot_of[p]]) for p in spots]
        firsts = [first_vec[p] for p in spots]
        mixed = [
            dot32(jnp.concatenate([v, v], axis=1), jnp.concatenate(parts, axis=0)) for v, parts in zip(firsts, split)
        ]
        sums = total[...]
        for m, p in zip(mixed, spots):
            sums = sums + (m * second_vec[p].astype(jnp.float32)) * live_of(p)
        total[...] = sums

    load_mats.wait()
    first_pass(g)
    for j in range(1, groups):
        for r in range(RUNS):
            vec_copy(j, r).wait_recv()
        first_pass(lax.rem(g + groups - j, groups))

    def partial_rows():
        ones = jnp.ones((SUB, feature), jnp.float32)
        tail = jnp.concatenate([total[LANES:samples], jnp.zeros((extra, feature), jnp.float32)], axis=0)
        return [
            lax.dot_general(ones, t, NT, precision=highest, preferred_element_type=jnp.float32)
            for t in (total[0:LANES], tail)
        ]

    row_id = lax.broadcasted_iota(jnp.int32, (SUB, LANES), 0)
    lane_id = lax.broadcasted_iota(jnp.int32, (SUB, LANES), 1)
    segment = cap * SUB
    span = LANES // segment

    def spot_row(ids, q):
        spots = jnp.zeros((SUB, LANES), jnp.int32)
        for c in range(cap):
            spots = jnp.where((lane_id % segment) // SUB == c, ids[q * cap + c], spots)
        spots = spots + (lane_id % SUB) * per_block
        return jnp.where(lane_id // segment == lax.rem(o, span), spots, 0).astype(jnp.float32)

    tables = jnp.zeros((SUB, LANES), jnp.float32)
    for q in range(groups):
        tables = jnp.where(row_id == FIRST_ROW + q, spot_row(first_at, q), tables)
    r0, r1 = partial_rows()
    tables = jnp.where(row_id == 0, r0, jnp.where(row_id == 1, r1, tables))
    for q in range(groups):
        msg1[q] = jnp.where(row_id == SECOND_ROW, spot_row(second_at, q), tables)

    def tile_copy(src, dst, sems, d, pick_own):
        peer = lax.rem(me + d, devices)
        pg, po = lax.div(peer, owners), lax.rem(peer, owners)
        return pltpu.make_async_remote_copy(
            src_ref=src.at[po if pick_own else pg],
            dst_ref=dst.at[me],
            send_sem=sems.at[0, peer],
            recv_sem=sems.at[1, me],
            device_id=(pg, po),
            device_id_type=MESH,
        )

    def tile_arrival(src, dst, sems, d):
        peer = lax.rem(me + d, devices)
        return pltpu.make_async_remote_copy(
            src_ref=src.at[0],
            dst_ref=dst.at[peer],
            send_sem=sems.at[0, peer],
            recv_sem=sems.at[1, peer],
            device_id=(lax.div(peer, owners), lax.rem(peer, owners)),
            device_id_type=MESH,
        )

    def send_tiles(src, dst, sems, pick_own):
        def one(d, _):
            tile_copy(src, dst, sems, d, pick_own).start()
            return 0

        lax.fori_loop(1, devices, one, 0)

    def wait_tiles(src, dst, sems):
        def one(d, _):
            tile_arrival(src, dst, sems, d).wait_recv()
            return 0

        lax.fori_loop(1, devices, one, 0)

    targets = jnp.concatenate([small_vec[:, 0:LANES], small_vec[:, LANES : 2 * LANES]], axis=0).astype(jnp.float32)

    def errors_of(got, at):
        sums = got[0]
        for d in range(1, devices):
            sums = sums + got[d]
        sums = sums[at : at + 2] * (1.0 / feature)
        logits = logit_scale * sums
        return logits, jax.nn.sigmoid(logits) - targets

    def error_row(err):
        return jnp.concatenate([err[0:1], err[1:2, 0 : samples - LANES]], axis=1)

    def gradients(spots, erow):
        turned = [first_t[p][:, 0:samples].astype(jnp.float32) * erow for p in spots]
        both = [jnp.concatenate(two_parts(v), axis=0) for v in turned]
        out = [dot32(v, second_vec[p]) for v, p in zip(both, spots)]
        return [x[0:feature] + x[feature:] for x in out]

    send_tiles(msg1, got1, sem_m1, False)
    got1[me] = msg1[g]
    wait_tiles(msg1, got1, sem_m1)
    _, err = errors_of(got1, 0)
    erow = error_row(err)
    total[...] = jnp.zeros_like(total)
    msg2[...] = jnp.zeros_like(msg2)

    def second_pass(j):
        q = lax.rem(g + j, groups)
        spots = [q * cap + c for c in range(cap)]
        lives = [live_of(p) for p in spots]
        old = [mats[slot_of[p]] for p in spots]
        firsts = [first_vec[p] for p in spots]
        seconds = [second_vec[p] for p in spots]
        moves = gradients(spots, erow)
        mids = [m - (rate * live) * d for m, d, live in zip(old, moves, lives)]
        split = [two_parts(m) for m in mids]
        mixed = [
            dot32(jnp.concatenate([v, v], axis=1), jnp.concatenate(parts, axis=0)) for v, parts in zip(firsts, split)
        ]
        back = [
            lax.dot_general(
                jnp.concatenate([v, v], axis=1),
                jnp.concatenate(parts, axis=1),
                NT,
                preferred_element_type=jnp.float32,
            )
            for v, parts in zip(seconds, split)
        ]
        sums = total[...]
        for m, v, live in zip(mixed, seconds, lives):
            sums = sums + (m * v.astype(jnp.float32)) * live
        total[...] = sums
        for c, p in enumerate(spots):
            factor = lives[c] * inv_root
            mats_mid[p] = mids[c]
            term_a[c] = back[c] * factor
            term_b[c] = mixed[c] * factor

        def code(w, _):
            rows = pl.ds(pl.multiple_of(w * chunk, SUB), chunk)
            terms = [t[c, rows, :] for t in (term_a, term_b) for c in range(cap)]
            big = functools.reduce(jnp.maximum, [jnp.abs(t) for t in terms])
            big = jnp.maximum(jnp.max(big, axis=0, keepdims=True), 1e-30)
            gain = TOP / big
            whole = [jnp.floor(t * gain + 0.5).astype(jnp.int32) for t in terms]
            for at, out in ((0, send_a), (cap, send_b)):
                for k in range(pairs):
                    a, b = whole[at + 2 * k], whole[at + 2 * k + 1]
                    out[q, w, pl.ds(k * chunk, chunk), :] = (a & 0xFFFF) | (b << 16)
            msg2[w, pl.ds(q, 1), :] = big * (1.0 / TOP)
            return 0

        lax.fori_loop(0, owners, code, 0)

    def partner(k):
        w, bit = o, 1
        while bit < owners:
            w = w + ((k // bit) % 2) * (bit - 2 * bit * ((w // bit) % 2))
            bit *= 2
        return w

    order = [k for pair in zip(range(owners // 2, owners), [*range(1, owners // 2), 0]) for k in pair if k]

    def unit_a(j, k):
        q, w = lax.rem(g + j, groups), partner(k)
        return pltpu.make_async_remote_copy(
            src_ref=send_a.at[q, w], dst_ref=got_a.at[o, q], send_sem=sem_a.at[0, q, w],
            recv_sem=sem_a.at[1, q, o], device_id=(g, w), device_id_type=MESH,
        )

    def unit_b(j, k):
        q, w = lax.rem(g + j, groups), partner(k)
        return pltpu.make_async_remote_copy(
            src_ref=send_b.at[q, w], dst_ref=got_b.at[g, o], send_sem=sem_b.at[0, q, w],
            recv_sem=sem_b.at[1, g, o], device_id=(q, w), device_id_type=MESH,
        )

    def send_units(j):
        for k in order:
            unit_a(j, k).start()
            unit_b(j, k).start()
        q = lax.rem(g + j, groups)
        got_a[o, q] = send_a[q, o]

    second_pass(0)
    got_b[g, o] = send_b[g, o]
    send_units(0)

    def later(j, _):
        second_pass(j)

        @pl.when(j < EARLY)
        def _():
            unit_b(j, 0).start()
            send_units(j)

        return 0

    lax.fori_loop(1, groups, later, 0)
    r0, r1 = partial_rows()
    for w in range(owners):
        msg2[w] = jnp.where(row_id == groups, r0, jnp.where(row_id == groups + 1, r1, msg2[w]))
    send_tiles(msg2, got2, sem_m2, True)

    def send_later(j, _):
        unit_b(j, 0).start()
        send_units(j)
        return 0

    lax.fori_loop(EARLY, groups, send_later, 0)
    got2[me] = msg2[o]
    wait_tiles(msg2, got2, sem_m2)
    logits, err = errors_of(got2, groups)
    logits_out[...] = error_row(logits)
    erow = error_row(err)
    eye = lax.broadcasted_iota(jnp.int32, (LANES, LANES), 0) == lax.broadcasted_iota(jnp.int32, (LANES, LANES), 1)
    for half in range(2):
        column = jnp.sum(jnp.where(eye, err[half : half + 1], 0.0), axis=1, keepdims=True)
        err_col[pl.ds(half * LANES, LANES), :] = jnp.broadcast_to(column, (LANES, LANES))

    def last_update(n, _):
        spots = [places[n * cap + c] for c in range(cap)]
        moves = gradients(spots, erow)
        news = [mats_mid[p] - (rate * live_of(p)) * d for p, d in zip(spots, moves)]
        for c in range(cap):
            mats_out[n * cap + c] = news[c]
        return 0

    lax.fori_loop(0, slots // cap, last_update, 0)

    col = err_col[pl.ds(pl.multiple_of(o * chunk, SUB), chunk), :]
    parts = chunk // SUB
    field_rows = lax.broadcasted_iota(jnp.int32, (SUB * per_block, LANES), 0)

    def decode(word_of, scale):
        out = []
        factor = col * scale
        for k in range(pairs):
            w = word_of(k)
            out.append(((w << 16) >> 16).astype(jnp.float32) * factor)
            out.append((w >> 16).astype(jnp.float32) * factor)
        return out

    def pick_of(spots):
        spots = (spots + 0.5).astype(jnp.int32)
        pick = jnp.where(field_rows == spots, 1.0, 0.0).astype(jnp.bfloat16)
        return [pick, pick]

    def rows_of(terms):
        x = jnp.concatenate(
            [jnp.concatenate([t[i * SUB : (i + 1) * SUB] for t in terms], axis=0) for i in range(parts)], axis=1
        )
        return list(two_parts(x))

    def wait_a(q, w):
        pltpu.make_async_remote_copy(
            src_ref=send_a.at[q, w], dst_ref=got_a.at[w, q], send_sem=sem_a.at[0, q, w],
            recv_sem=sem_a.at[1, q, w], device_id=(g, w), device_id_type=MESH,
        ).wait_recv()

    def wait_b(q, w):
        pltpu.make_async_remote_copy(
            src_ref=send_b.at[q, w], dst_ref=got_b.at[q, w], send_sem=sem_b.at[0, q, w],
            recv_sem=sem_b.at[1, q, w], device_id=(q, w), device_id_type=MESH,
        ).wait_recv()

    acc[...] = jnp.zeros_like(acc)

    def arrivals(n, _):
        j, h = n // (owners // span), n % (owners // span)
        qa, qb = lax.rem(g + j, groups), lax.rem(g + groups - j, groups)
        terms_a, terms_b, spots_a, spots_b = [], [], 0.0, 0.0
        for i in range(span):
            k = h * span + partner(i) % span
            w = partner(k)

            @pl.when(k > 0)
            def _():
                wait_a(qa, w)

            @pl.when(j + k > 0)
            def _():
                wait_b(qb, w)

            scale = got2[g * owners + w, pl.ds(qa, 1), :]
            terms_a += decode(lambda m: got_a[w, qa, pl.ds(m * chunk, chunk), :], scale)
            spots_a = spots_a + got1[g * owners + w, pl.ds(FIRST_ROW + qa, 1), :]
            scale = got2[qb * owners + w, pl.ds(g, 1), :]
            terms_b += decode(lambda m: got_b[qb, w, pl.ds(m * chunk, chunk), :], scale)
            spots_b = spots_b + got1[qb * owners + w][SECOND_ROW : SECOND_ROW + 1]
        pick = jnp.concatenate(pick_of(spots_a) + pick_of(spots_b), axis=1)
        acc[...] += dot32(pick, jnp.concatenate(rows_of(terms_a) + rows_of(terms_b), axis=0))
        return 0

    lax.fori_loop(0, groups * (owners // span), arrivals, 0)
    for i in range(parts):
        grad_out[i * SUB : (i + 1) * SUB] = acc[:, i * feature : (i + 1) * feature].reshape(SUB, per_block, feature)

    for j in range(1, groups):
        for r in range(RUNS):
            vec_copy(j, r).wait_send()

    def drain_tiles(d, _):
        tile_copy(msg1, got1, sem_m1, d, False).wait_send()
        tile_copy(msg2, got2, sem_m2, d, True).wait_send()
        return 0

    lax.fori_loop(1, devices, drain_tiles, 0)

    def drain_units(j, _):
        def one(k, _):
            unit_a(j, k).wait_send()
            unit_b(j, k).wait_send()
            return 0

        lax.fori_loop(1, owners, one, 0)

        @pl.when(j > 0)
        def _():
            unit_b(j, 0).wait_send()

        return 0

    lax.fori_loop(0, groups, drain_units, 0)


def on_device_kernel(fields, labels, pair_first, pair_second, pair_count, pair_mats):
    groups = lax.axis_size("grp")
    owners = lax.axis_size("own")
    samples, per_block, feature = fields.shape
    slots = pair_first.shape[2]
    cap = slots // groups
    chunk = samples // owners
    devices = groups * owners
    pad = jnp.zeros((2 * LANES - samples,), labels.dtype)
    small = jnp.concatenate([labels, pad] + [x.reshape(-1) for x in (pair_first, pair_second, pair_count)])[None]
    smem = pl.BlockSpec(memory_space=pltpu.SMEM)
    vmem = pl.BlockSpec(memory_space=pltpu.VMEM)
    hbm = pl.BlockSpec(memory_space=pltpu.HBM)
    rows = cap // 2 * chunk
    f32, bf16, i32 = jnp.float32, jnp.bfloat16, jnp.int32
    logits, grad, new_mats = pl.pallas_call(
        functools.partial(step_kernel, groups, owners),
        out_shape=(
            jax.ShapeDtypeStruct((1, samples), f32),
            jax.ShapeDtypeStruct((chunk, per_block, feature), f32),
            jax.ShapeDtypeStruct((slots, feature, feature), f32),
        ),
        in_specs=[smem, vmem, hbm, hbm],
        out_specs=(vmem,) * 3,
        scratch_shapes=[
            pltpu.SMEM((slots,), i32),
            pltpu.SMEM((slots,), i32),
            pltpu.VMEM(fields.shape, bf16),
            pltpu.VMEM((slots, feature, feature), f32),
            pltpu.VMEM((slots, samples, feature), bf16),
            pltpu.VMEM((slots, feature, 2 * LANES), bf16),
            pltpu.VMEM((slots, samples, feature), bf16),
            pltpu.VMEM((slots, samples, feature), bf16),
            pltpu.VMEM((slots, feature, feature), f32),
            pltpu.VMEM((samples, feature), f32),
            pltpu.VMEM((groups, SUB, LANES), f32),
            pltpu.VMEM((devices, SUB, LANES), f32),
            pltpu.VMEM((owners, SUB, LANES), f32),
            pltpu.VMEM((devices, SUB, LANES), f32),
            pltpu.VMEM((cap, samples, feature), f32),
            pltpu.VMEM((cap, samples, feature), f32),
            pltpu.VMEM((groups, owners, rows, feature), i32),
            pltpu.VMEM((groups, owners, rows, feature), i32),
            pltpu.VMEM((owners, groups, rows, feature), i32),
            pltpu.VMEM((groups, owners, rows, feature), i32),
            pltpu.VMEM((2 * LANES, LANES), f32),
            pltpu.VMEM((SUB * per_block, chunk // SUB * feature), f32),
            pltpu.SemaphoreType.DMA((RUNS,)),
            pltpu.SemaphoreType.DMA((1,)),
            pltpu.SemaphoreType.DMA((2, groups, RUNS)),
            pltpu.SemaphoreType.DMA((2, devices)),
            pltpu.SemaphoreType.DMA((2, devices)),
            pltpu.SemaphoreType.DMA((2, groups, owners)),
            pltpu.SemaphoreType.DMA((2, groups, owners)),
        ],
        compiler_params=pltpu.CompilerParams(
            collective_id=0, has_side_effects=True, vmem_limit_bytes=52 * 1024 * 1024
        ),
        cost_estimate=pl.CostEstimate(flops=4 * 10**9, bytes_accessed=8 * 10**6, transcendentals=400),
    )(small, small, fields, pair_mats[0, 0])
    return (logits.reshape(samples), grad, new_mats[None, None])


def fits(groups, owners, fields, pair_first):
    samples, _, feature = fields.shape
    slots = pair_first.shape[2]
    cap = slots // groups
    return (
        feature == LANES
        and slots * SUB == LANES
        and slots % groups == 0
        and cap % 2 == 0
        and LANES < samples <= 2 * LANES
        and samples % (SUB * owners) == 0
        and samples % (16 * RUNS) == 0
        and fields.shape[1] & (fields.shape[1] - 1) == 0
        and owners & (owners - 1) == 0
        and owners % (LANES // (cap * SUB)) == 0
        and FIRST_ROW + groups <= SUB
    )


def dispatch(groups, owners, fields, labels, pair_first, pair_second, pair_count, pair_mats):
    args = (fields, labels, pair_first, pair_second, pair_count, pair_mats)
    if fits(groups, owners, fields, pair_first):
        return on_device_kernel(*args)
    return on_device(*args)


def solution(mesh):
    in_specs = (
        P(None, "grp", None),
        P(),
        P("grp", "own", None),
        P(None, "own", None),
        P("grp", "own"),
        P("grp", "own", None, None, None),
    )
    out_specs = (P(), P("own", "grp", None), P("grp", "own", None, None, None))
    per_device = functools.partial(dispatch, mesh.shape["grp"], mesh.shape["own"])
    return jax.shard_map(
        per_device, mesh=mesh, in_specs=in_specs, out_specs=out_specs, check_vma=False
    )
```

```python
import functools
import math

import jax
import jax.numpy as jnp
from jax import lax
from jax.experimental import pallas as pl
from jax.experimental.pallas import tpu as pltpu
from jax.sharding import PartitionSpec as P

STEPS = 2


logit_gain = 1.5
step_size = 1000.0
highest = lax.Precision.HIGHEST


def logit_errors(partial_value, targets, logit_scale):
    total_sum = lax.psum(partial_value, ("grp", "own"))
    logits = logit_scale * total_sum
    errors = jax.nn.sigmoid(logits) - targets
    return (logits, errors)


def on_device(fields, labels, pair_first, pair_second, pair_count, pair_mats):
    groups = lax.axis_size("grp")
    owners = lax.axis_size("own")
    my_group = lax.axis_index("grp")
    samples, per_block, feature = fields.shape
    slot_count = pair_first.shape[2]
    capacity = slot_count // groups
    second_table = pair_second[:, 0, :]
    block_ids = second_table // per_block
    offsets = second_table % per_block
    member = (block_ids[:, :, None] == jnp.arange(groups, dtype=jnp.int32)[None, None, :]).astype(
        jnp.int32
    )
    slot_ranks = jnp.sum((jnp.cumsum(member, axis=1) - 1) * member, axis=2)
    places = block_ids * capacity + slot_ranks
    chosen = (block_ids[:, :, None] == my_group) & (
        slot_ranks[:, :, None] == jnp.arange(capacity, dtype=jnp.int32)[None, None, :]
    )
    served = jnp.sum(jnp.where(chosen, offsets[:, :, None], 0), axis=1).reshape(-1)
    outgoing = jnp.take(fields, served, axis=1)
    incoming = lax.all_to_all(outgoing, "grp", split_axis=1, concat_axis=1, tiled=True)
    my_places = lax.dynamic_index_in_dim(places, my_group, 0, keepdims=False)
    second_vec = jnp.take(incoming, my_places, axis=1).astype(jnp.float32)
    first_local = pair_first[0, 0] - my_group * per_block
    first_vec = jnp.take(fields, first_local, axis=1).astype(jnp.float32)
    live_mask = (jnp.arange(slot_count, dtype=jnp.int32) < pair_count[0, 0]).astype(jnp.float32)
    matrices = pair_mats[0, 0]
    targets = labels.astype(jnp.float32)
    logit_scale = logit_gain / math.sqrt(groups * owners * slot_count)
    root_width = math.sqrt(feature)
    logits = jnp.zeros((samples,), jnp.float32)
    grad_first = jnp.zeros(first_vec.shape, jnp.float32)
    grad_second = jnp.zeros(first_vec.shape, jnp.float32)
    for step_index in range(STEPS):
        mixed = jnp.einsum("bsk,skl->bsl", first_vec, matrices, precision=highest)
        partial_value = jnp.sum(
            jnp.sum(mixed * second_vec, axis=2) / feature * live_mask[None, :], axis=1
        )
        logits, errors = logit_errors(partial_value, targets, logit_scale)
        if step_index == STEPS - 1:
            grad_first = (
                errors[:, None, None]
                * jnp.einsum("skl,bsl->bsk", matrices, second_vec, precision=highest)
                / root_width
                * live_mask[None, :, None]
            )
            grad_second = errors[:, None, None] * mixed / root_width * live_mask[None, :, None]
        gradient = jnp.einsum(
            "bsk,bsl->skl", first_vec * errors[:, None, None], second_vec, precision=highest
        )
        matrices = (
            matrices
            - step_size * logit_scale / (samples * feature) * live_mask[:, None, None] * gradient
        )
    slot_iota = jnp.arange(slot_count, dtype=jnp.int32)
    slot_of = jnp.sum(
        jnp.where(my_places[None, :] == slot_iota[:, None], slot_iota[None, :], 0), axis=1
    )
    returned = lax.all_to_all(
        jnp.take(grad_second, slot_of, axis=1), "grp", split_axis=1, concat_axis=1, tiled=True
    )
    block_iota = jnp.arange(per_block, dtype=jnp.int32)
    pick_second = (served[:, None] == block_iota[None, :]).astype(jnp.float32)
    pick_first = (first_local[:, None] == block_iota[None, :]).astype(jnp.float32)
    dense_grad = jnp.einsum("bsk,sf->bfk", grad_first, pick_first, precision=highest)
    dense_grad = dense_grad + jnp.einsum("bpk,pf->bfk", returned, pick_second, precision=highest)
    field_grad = lax.psum_scatter(dense_grad, "own", scatter_dimension=0, tiled=True)
    return (logits, field_grad, matrices[None, None])


LANES = 128
SUB = 8
TOP = 32760.0
RUNS = 4
SECOND_ROW = 2
FIRST_ROW = 4
MESH = pl.DeviceIdType.MESH
NT = (((1,), (1,)), ((), ()))


def two_parts(x):
    high = x.astype(jnp.bfloat16)
    low = (x - high.astype(jnp.float32)).astype(jnp.bfloat16)
    return high, low


def dot32(a, b):
    return jnp.dot(a, b, preferred_element_type=jnp.float32)


def step_kernel(
    groups, owners,
    first_ids, second_ids, count, labels, fields_in, mats_in,
    logits_out, grad_out, mats_out,
    slot_of, places, fields, mats,
    first_vec, first_t, served_vec, second_vec, mats_mid, total,
    tab_out, tab_in, served_mate, mate_second, mate_first, mate_t, send_m, got_m, unit_m, got_unit_m,
    msg1, got1, msg2, got2, term_a, term_b, send_a, send_b, got_a, got_b, err_col, acc,
    sem_f, sem_m, sem_v, sem_m1, sem_m2, sem_as, sem_ar, sem_bs, sem_br, sem_tab, sem_w, sem_mat,
):
    samples, per_block, feature = fields.shape
    shift = per_block.bit_length() - 1
    slots = mats.shape[0]
    cap = slots // groups
    chunk = samples // owners
    devices = groups * owners
    pairs = cap // 2
    g, o = lax.axis_index("grp"), lax.axis_index("own")
    me = g * owners + o
    logit_scale = logit_gain / math.sqrt(devices * slots)
    rate = step_size * logit_scale / (samples * feature)
    wing = owners // 2
    mate = lax.rem(o + wing, owners)
    side = lax.div(o, wing)
    half = samples // 2
    base = pl.multiple_of(side * half, 16)
    row_id = lax.broadcasted_iota(jnp.int32, (SUB, LANES), 0)
    lane_id = lax.broadcasted_iota(jnp.int32, (SUB, LANES), 1)
    eye = lax.broadcasted_iota(jnp.int32, (LANES, LANES), 0) == lax.broadcasted_iota(jnp.int32, (LANES, LANES), 1)
    inv_root = 1.0 / math.sqrt(feature)
    extra = 2 * LANES - samples

    run = samples // RUNS

    def load_fields(r):
        part = pl.ds(r * run, run)
        return pltpu.make_async_copy(fields_in.at[part], fields.at[part], sem_f.at[r])

    for r in range(RUNS):
        load_fields(r).start()
    load_mats = pltpu.make_async_copy(mats_in, mats, sem_m.at[0])
    load_mats.start()

    barrier = pltpu.get_barrier_semaphore()

    def greet(d, _):
        peer = lax.rem(me + d, devices)
        pl.semaphore_signal(
            barrier, inc=1, device_id=(lax.div(peer, owners), lax.rem(peer, owners)), device_id_type=MESH
        )
        return 0

    lax.fori_loop(1, devices, greet, 0)

    wide = SUB * per_block

    def pick_scalars(spots):
        lanes = lax.broadcasted_iota(jnp.int32, (SUB, wide), 1)
        lanes = lanes - lax.broadcasted_iota(jnp.int32, (SUB, wide), 0) * per_block
        return jnp.concatenate([jnp.where(lanes == f, 1.0, 0.0) for f in spots], axis=0).astype(jnp.bfloat16)

    def pick_row(row):
        column = jnp.sum(jnp.where(eye, row, 0.0), axis=1, keepdims=True)
        column = (column + 0.5).astype(jnp.int32)
        lanes = lax.broadcasted_iota(jnp.int32, (LANES, wide), 1)
        return jnp.where(lanes == column, 1.0, 0.0).astype(jnp.bfloat16)

    def gather(pick):
        def rows(out, start, size):
            def part(i, _):
                at = pl.multiple_of(start + i * 16, 16)
                halves = []
                for h in range(2):
                    block = fields[pl.ds(at + h * SUB, SUB)].reshape(wide, feature)
                    halves.append(dot32(pick, block).reshape(slots, SUB, feature))
                out[:, pl.ds(at, 16), :] = jnp.concatenate(halves, axis=1).astype(jnp.bfloat16)
                return 0

            lax.fori_loop(0, size // 16, part, 0)

        return rows

    def vec_copy(j, r):
        to = lax.rem(g + j, groups)
        part = pl.ds(r * run, run)
        return pltpu.make_async_remote_copy(
            src_ref=served_vec.at[pl.ds(to * cap, cap), part],
            dst_ref=second_vec.at[pl.ds(g * cap, cap), part],
            send_sem=sem_v.at[0, j, r],
            recv_sem=sem_v.at[1, j, r],
            device_id=(to, o),
            device_id_type=MESH,
        )

    served = []
    for q in range(groups):
        found, seen = [jnp.int32(0)] * cap, jnp.int32(0)
        for s in range(slots):
            field = second_ids[q, 0, s]
            hit = (field >> shift) == g
            found = [
                jnp.where(jnp.logical_and(hit, seen == c), field & (per_block - 1), f) for c, f in enumerate(found)
            ]
            seen = seen + hit.astype(jnp.int32)
        served += found
    owner_of = [jnp.int32(0)] * slots
    seen = [jnp.int32(0)] * groups
    for s in range(slots):
        block = second_ids[g, 0, s] >> shift
        place = jnp.int32(0)
        for q in range(groups):
            hit = block == q
            place = jnp.where(hit, q * cap + seen[q], place)
            seen[q] = seen[q] + hit.astype(jnp.int32)
        places[s] = place
        owner_of = [jnp.where(place == p, s, t) for p, t in enumerate(owner_of)]
    for p in range(slots):
        slot_of[p] = owner_of[p]
    first_at = [first_ids[0, 0, t] - g * per_block for t in owner_of]
    second_at = [second_ids[g, 0, t] & (per_block - 1) for t in owner_of]

    def live_of(p):
        return jnp.where(slot_of[p] < count[0, 0], 1.0, 0.0)

    gather_served = gather(pick_scalars(served))
    for r in range(RUNS):
        load_fields(r).wait()
        gather_served(served_vec, r * run, run)
        if r == 0:
            pl.semaphore_wait(barrier, devices - 1)
        for j in range(1, groups):
            vec_copy(j, r).start()
    second_vec[pl.ds(g * cap, cap)] = served_vec[pl.ds(g * cap, cap)]

    def full_row(ids):
        spots = jnp.zeros((SUB, LANES), jnp.int32)
        for t in range(slots):
            spots = jnp.where(lane_id // SUB == t, ids[t], spots)
        return (spots + (lane_id % SUB) * per_block).astype(jnp.float32)

    tab_out[0:SUB, :] = jnp.where(row_id == 0, full_row(first_at), jnp.where(row_id == 1, full_row(served), 0.0))
    for p in range(slots):
        tab_out[SUB + p : SUB + p + 1, :] = jnp.zeros((1, LANES), jnp.float32) + live_of(p)

    def to_mate(src, dst, sems, at):
        return pltpu.make_async_remote_copy(
            src_ref=src, dst_ref=dst, send_sem=sems.at[0, at], recv_sem=sems.at[1, at],
            device_id=(g, mate), device_id_type=MESH,
        )

    tab_copy = to_mate(tab_out, tab_in, sem_tab, 0)
    tab_copy.start()
    load_mats.wait()

    def code_mats(t, _):
        a, b = mats[slot_of[2 * t]], mats[slot_of[2 * t + 1]]
        big = jnp.maximum(jnp.max(jnp.maximum(jnp.abs(a), jnp.abs(b)), axis=0, keepdims=True), 1e-30)
        gain = TOP / big
        a, b = [jnp.floor(x * gain + 0.5).astype(jnp.int32) for x in (a, b)]
        send_m[t] = (a & 0xFFFF) | (b << 16)
        unit_m[pl.ds(t, 1), :] = big * (1.0 / TOP)
        return 0

    lax.fori_loop(0, slots // 2, code_mats, 0)
    part = slots // 4
    mat_copies = [to_mate(send_m.at[pl.ds(h * part, part)], got_m.at[pl.ds(h * part, part)], sem_mat, h) for h in range(2)]
    mat_copies.append(to_mate(unit_m, got_unit_m, sem_mat, 2))
    mat_copies[2].start()
    mat_copies[0].start()

    tab_copy.wait_recv()
    gather(pick_row(tab_in[1:2, :]))(served_mate, 0, samples)

    def mate_copy(j):
        to = lax.rem(g + j, groups)
        return pltpu.make_async_remote_copy(
            src_ref=served_mate.at[pl.ds(to * cap, cap)], dst_ref=mate_second.at[pl.ds(g * cap, cap)],
            send_sem=sem_w.at[0, j], recv_sem=sem_w.at[1, j], device_id=(to, o), device_id_type=MESH,
        )

    for j in range(1, groups):
        mate_copy(j).start()
    mate_second[pl.ds(g * cap, cap)] = served_mate[pl.ds(g * cap, cap)]
    gather(pick_scalars(first_at))(first_vec, 0, samples)

    def turn_all(vecs, turned):
        def turn(p, _):
            v = vecs[p].astype(jnp.float32)
            v = jnp.concatenate([v, jnp.zeros((extra, feature), jnp.float32)], axis=0)
            turned[p] = v.T.astype(jnp.bfloat16)
            return 0

        lax.fori_loop(0, slots, turn, 0)

    turn_all(first_vec, first_t)
    total[...] = jnp.zeros_like(total)

    def first_pass(q):
        spots = [q * cap + c for c in range(cap)]
        split = [two_parts(mats[slot_of[p]]) for p in spots]
        firsts = [first_vec[p] for p in spots]
        mixed = [
            dot32(jnp.concatenate([v, v], axis=1), jnp.concatenate(parts, axis=0)) for v, parts in zip(firsts, split)
        ]
        sums = total[...]
        for m, p in zip(mixed, spots):
            sums = sums + (m * second_vec[p].astype(jnp.float32)) * live_of(p)
        total[...] = sums

    first_pass(g)
    for j in range(1, groups):
        for r in range(RUNS):
            vec_copy(j, r).wait_recv()
        first_pass(lax.rem(g + groups - j, groups))

    def partial_rows():
        ones = jnp.ones((SUB, feature), jnp.float32)
        tail = jnp.concatenate([total[LANES:samples], jnp.zeros((extra, feature), jnp.float32)], axis=0)
        return [
            lax.dot_general(ones, t, NT, precision=highest, preferred_element_type=jnp.float32)
            for t in (total[0:LANES], tail)
        ]

    segment = cap * SUB
    span = LANES // segment

    def spot_row(ids, q):
        spots = jnp.zeros((SUB, LANES), jnp.int32)
        for c in range(cap):
            spots = jnp.where((lane_id % segment) // SUB == c, ids[q * cap + c], spots)
        spots = spots + (lane_id % SUB) * per_block
        return jnp.where(lane_id // segment == lax.rem(o, span), spots, 0).astype(jnp.float32)

    tables = jnp.zeros((SUB, LANES), jnp.float32)
    for q in range(groups):
        tables = jnp.where(row_id == FIRST_ROW + q, spot_row(first_at, q), tables)
    r0, r1 = partial_rows()
    tables = jnp.where(row_id == 0, r0, jnp.where(row_id == 1, r1, tables))
    for q in range(groups):
        msg1[q] = jnp.where(row_id == SECOND_ROW, spot_row(second_at, q), tables)

    def tile_copy(src, dst, sems, d, pick_own):
        peer = lax.rem(me + d, devices)
        pg, po = lax.div(peer, owners), lax.rem(peer, owners)
        return pltpu.make_async_remote_copy(
            src_ref=src.at[lax.rem(po, wing) if pick_own else pg],
            dst_ref=dst.at[me],
            send_sem=sems.at[0, peer],
            recv_sem=sems.at[1, me],
            device_id=(pg, po),
            device_id_type=MESH,
        )

    def tile_arrival(src, dst, sems, d):
        peer = lax.rem(me + d, devices)
        return pltpu.make_async_remote_copy(
            src_ref=src.at[0],
            dst_ref=dst.at[peer],
            send_sem=sems.at[0, peer],
            recv_sem=sems.at[1, peer],
            device_id=(lax.div(peer, owners), lax.rem(peer, owners)),
            device_id_type=MESH,
        )

    def send_tiles(src, dst, sems, pick_own):
        def one(d, _):
            tile_copy(src, dst, sems, d, pick_own).start()
            return 0

        lax.fori_loop(1, devices, one, 0)

    def wait_tiles(src, dst, sems):
        def one(d, _):
            tile_arrival(src, dst, sems, d).wait_recv()
            return 0

        lax.fori_loop(1, devices, one, 0)

    wanted = labels[...].astype(jnp.float32)
    targets = jnp.concatenate(
        [
            wanted[:, 0:LANES],
            jnp.concatenate([wanted[:, LANES:samples], jnp.zeros((1, extra), jnp.float32)], axis=1),
        ],
        axis=0,
    )

    def errors_of(got, at):
        sums = got[0]
        for d in range(1, devices):
            sums = sums + got[d]
        sums = sums[at : at + 2] * (1.0 / feature)
        logits = logit_scale * sums
        return logits, jax.nn.sigmoid(logits) - targets

    def error_row(err):
        return jnp.concatenate([err[0:1], err[1:2, 0 : samples - LANES]], axis=1)

    def gradients(spots, erow, turned_ref, second_ref):
        turned = [turned_ref[p][:, 0:samples].astype(jnp.float32) * erow for p in spots]
        both = [jnp.concatenate(two_parts(v), axis=0) for v in turned]
        out = [dot32(v, second_ref[p]) for v, p in zip(both, spots)]
        return [x[0:feature] + x[feature:] for x in out]

    send_tiles(msg1, got1, sem_m1, False)
    mat_copies[1].start()
    got1[me] = msg1[g]
    wait_tiles(msg1, got1, sem_m1)
    _, err = errors_of(got1, 0)
    erow = error_row(err)
    total[...] = jnp.zeros_like(total)
    msg2[...] = jnp.zeros_like(msg2)

    def halved(ref, p):
        return ref[p, pl.ds(base, half), :]

    def twice(v):
        return jnp.concatenate([v, v], axis=1)

    def second_pass(q, m):
        spots = [q * cap + c for c in range(cap)]
        if m == 0:
            lives = [live_of(p) for p in spots]
            old = [mats[slot_of[p]] for p in spots]
            firsts = [first_vec[p] for p in spots]
            seconds = [halved(second_vec, p) for p in spots]
            moves = gradients(spots, erow, first_t, second_vec)
        else:
            lives = [tab_in[pl.ds(SUB + p, 1), :] for p in spots]
            old = []
            for k in range(pairs):
                w = got_m[q * pairs + k]
                unit = got_unit_m[pl.ds(q * pairs + k, 1), :]
                old += [((w << 16) >> 16).astype(jnp.float32) * unit, (w >> 16).astype(jnp.float32) * unit]
            firsts = [halved(mate_first, p) for p in spots]
            seconds = [halved(mate_second, p) for p in spots]
            moves = gradients(spots, erow, mate_t, mate_second)
        mids = [x - (rate * live) * d for x, d, live in zip(old, moves, lives)]
        split = [two_parts(x) for x in mids]
        mixed = [dot32(twice(v), jnp.concatenate(parts, axis=0)) for v, parts in zip(firsts, split)]
        back = [
            lax.dot_general(twice(v), jnp.concatenate(parts, axis=1), NT, preferred_element_type=jnp.float32)
            for v, parts in zip(seconds, split)
        ]
        if m == 0:
            sums = total[...]
            for x, p, live in zip(mixed, spots, lives):
                sums = sums + (x * second_vec[p].astype(jnp.float32)) * live
            total[...] = sums
        for c, p in enumerate(spots):
            factor = lives[c] * inv_root
            term_a[c, pl.ds(base, half), :] = back[c] * factor
            if m == 0:
                mats_mid[p] = mids[c]
                term_b[c] = mixed[c] * factor
            else:
                term_b[c, pl.ds(base, half), :] = mixed[c] * factor

        def code(w, _):
            rows = pl.ds(pl.multiple_of(base + w * chunk, SUB), chunk)
            terms = [t[c, rows, :] for t in (term_a, term_b) for c in range(cap)]
            big = functools.reduce(jnp.maximum, [jnp.abs(t) for t in terms])
            big = jnp.maximum(jnp.max(big, axis=0, keepdims=True), 1e-30)
            gain = TOP / big
            whole = [jnp.floor(t * gain + 0.5).astype(jnp.int32) for t in terms]
            for at, out in ((0, send_a), (cap, send_b)):
                for k in range(pairs):
                    a, b = whole[at + 2 * k], whole[at + 2 * k + 1]
                    out[m, q, w, pl.ds(k * chunk, chunk), :] = (a & 0xFFFF) | (b << 16)
            msg2[w, pl.ds(m * SUB + q, 1), :] = big * (1.0 / TOP)
            return 0

        lax.fori_loop(0, wing, code, 0)

    def partner(k):
        w, bit = o, 1
        while bit < owners:
            w = w + ((k // bit) % 2) * (bit - 2 * bit * ((w // bit) % 2))
            bit *= 2
        return w

    mine = o - side * wing

    def unit_a(m, q, k):
        w = partner(k)
        return pltpu.make_async_remote_copy(
            src_ref=send_a.at[m, q, w - side * wing], dst_ref=got_a.at[mate if m else o, q],
            send_sem=sem_as.at[m, q, k], recv_sem=sem_ar.at[q, mate if m else o],
            device_id=(g, w), device_id_type=MESH,
        )

    def unit_b(m, q, k):
        w = partner(k)
        return pltpu.make_async_remote_copy(
            src_ref=send_b.at[m, q, w - side * wing], dst_ref=got_b.at[g, mate if m else o],
            send_sem=sem_bs.at[m, q, k], recv_sem=sem_br.at[g, mate if m else o],
            device_id=(q, w), device_id_type=MESH,
        )

    def send_units(q, m):
        for k in range(1, wing):
            unit_a(m, q, k).start()
            unit_b(m, q, k).start()
        got_a[mate if m else o, q] = send_a[m, q, mine]

        @pl.when(q == g)
        def _():
            got_b[g, mate if m else o] = send_b[m, g, mine]

        @pl.when(q != g)
        def _():
            unit_b(m, q, 0).start()

    def own_part(j, _):
        q = lax.rem(g + j, groups)
        second_pass(q, 0)
        send_units(q, 0)
        return 0

    lax.fori_loop(0, groups, own_part, 0)
    r0, r1 = partial_rows()
    gather(pick_row(tab_in[0:1, :]))(mate_first, 0, samples)
    turn_all(mate_first, mate_t)
    for j in range(1, groups):
        mate_copy(j).wait_recv()
    for copy in mat_copies:
        copy.wait_recv()

    def mate_part(q, _):
        second_pass(q, 1)
        send_units(q, 1)
        return 0

    lax.fori_loop(0, groups, mate_part, 0)
    for w in range(wing):
        low = msg2[w, 0:SUB, :]
        msg2[w, 0:SUB, :] = jnp.where(row_id == groups, r0, jnp.where(row_id == groups + 1, r1, low))
    send_tiles(msg2, got2, sem_m2, True)
    got2[me] = msg2[mine]
    wait_tiles(msg2, got2, sem_m2)
    logits, err = errors_of(got2, groups)
    logits_out[...] = error_row(logits)
    erow = error_row(err)
    for n in range(2):
        column = jnp.sum(jnp.where(eye, err[n : n + 1], 0.0), axis=1, keepdims=True)
        err_col[pl.ds(n * LANES, LANES), :] = jnp.broadcast_to(column, (LANES, LANES))

    def last_update(n, _):
        spots = [places[n * cap + c] for c in range(cap)]
        moves = gradients(spots, erow, first_t, second_vec)
        news = [mats_mid[p] - (rate * live_of(p)) * d for p, d in zip(spots, moves)]
        for c in range(cap):
            mats_out[n * cap + c] = news[c]
        return 0

    lax.fori_loop(0, slots // cap, last_update, 0)

    col = err_col[pl.ds(pl.multiple_of(o * chunk, SUB), chunk), :]
    parts = chunk // SUB
    field_rows = lax.broadcasted_iota(jnp.int32, (SUB * per_block, LANES), 0)

    def decode(word_of, scale):
        out = []
        factor = col * scale
        for k in range(pairs):
            w = word_of(k)
            out.append(((w << 16) >> 16).astype(jnp.float32) * factor)
            out.append((w >> 16).astype(jnp.float32) * factor)
        return out

    def pick_of(spots):
        spots = (spots + 0.5).astype(jnp.int32)
        pick = jnp.where(field_rows == spots, 1.0, 0.0).astype(jnp.bfloat16)
        return [pick, pick]

    def rows_of(terms):
        x = jnp.concatenate(
            [jnp.concatenate([t[i * SUB : (i + 1) * SUB] for t in terms], axis=0) for i in range(parts)], axis=1
        )
        return list(two_parts(x))

    def wait_a(q, w):
        pltpu.make_async_remote_copy(
            src_ref=send_a.at[0, q, 0], dst_ref=got_a.at[w, q], send_sem=sem_as.at[0, q, 0],
            recv_sem=sem_ar.at[q, w], device_id=(g, w), device_id_type=MESH,
        ).wait_recv()

    def wait_b(q, w):
        pltpu.make_async_remote_copy(
            src_ref=send_b.at[0, q, 0], dst_ref=got_b.at[q, w], send_sem=sem_bs.at[0, q, 0],
            recv_sem=sem_br.at[q, w], device_id=(q, w), device_id_type=MESH,
        ).wait_recv()

    acc[...] = jnp.zeros_like(acc)

    def arrivals(n, _):
        j, h = n % groups, n // groups
        qa, qb = lax.rem(g + j, groups), lax.rem(g + groups - j, groups)
        terms_a, terms_b, spots_a, spots_b = [], [], 0.0, 0.0
        for i in range(span):
            k = h * span + partner(i) % span
            w = partner(k)
            near = k % wing
            real = partner(near)

            @pl.when(near > 0)
            def _():
                wait_a(qa, w)

            @pl.when(j + near > 0)
            def _():
                wait_b(qb, w)

            scale = got2[g * owners + real, pl.ds(h * SUB + qa, 1), :]
            terms_a += decode(lambda m: got_a[w, qa, pl.ds(m * chunk, chunk), :], scale)
            spots_a = spots_a + got1[g * owners + w, pl.ds(FIRST_ROW + qa, 1), :]
            scale = got2[qb * owners + real, pl.ds(h * SUB + g, 1), :]
            terms_b += decode(lambda m: got_b[qb, w, pl.ds(m * chunk, chunk), :], scale)
            spots_b = spots_b + got1[qb * owners + w][SECOND_ROW : SECOND_ROW + 1]
        pick = jnp.concatenate(pick_of(spots_a) + pick_of(spots_b), axis=1)
        acc[...] += dot32(pick, jnp.concatenate(rows_of(terms_a) + rows_of(terms_b), axis=0))
        return 0

    lax.fori_loop(0, groups * (owners // span), arrivals, 0)
    for i in range(parts):
        grad_out[i * SUB : (i + 1) * SUB] = acc[:, i * feature : (i + 1) * feature].reshape(SUB, per_block, feature)

    for j in range(1, groups):
        for r in range(RUNS):
            vec_copy(j, r).wait_send()

    def drain_tiles(d, _):
        tile_copy(msg1, got1, sem_m1, d, False).wait_send()
        tile_copy(msg2, got2, sem_m2, d, True).wait_send()
        return 0

    lax.fori_loop(1, devices, drain_tiles, 0)

    for j in range(1, groups):
        mate_copy(j).wait_send()
    for copy in mat_copies + [tab_copy]:
        copy.wait_send()

    def drain_units(q, _):
        for m in range(2):
            for k in range(1, wing):
                unit_a(m, q, k).wait_send()
                unit_b(m, q, k).wait_send()

            @pl.when(q != g)
            def _():
                unit_b(m, q, 0).wait_send()

        return 0

    lax.fori_loop(0, groups, drain_units, 0)


def on_device_kernel(fields, labels, pair_first, pair_second, pair_count, pair_mats):
    groups = lax.axis_size("grp")
    owners = lax.axis_size("own")
    samples, per_block, feature = fields.shape
    slots = pair_first.shape[2]
    cap = slots // groups
    chunk = samples // owners
    devices = groups * owners
    smem = pl.BlockSpec(memory_space=pltpu.SMEM)
    vmem = pl.BlockSpec(memory_space=pltpu.VMEM)
    hbm = pl.BlockSpec(memory_space=pltpu.HBM)
    rows = cap // 2 * chunk
    f32, bf16, i32 = jnp.float32, jnp.bfloat16, jnp.int32
    logits, grad, new_mats = pl.pallas_call(
        functools.partial(step_kernel, groups, owners),
        out_shape=(
            jax.ShapeDtypeStruct((1, samples), f32),
            jax.ShapeDtypeStruct((chunk, per_block, feature), f32),
            jax.ShapeDtypeStruct((slots, feature, feature), f32),
        ),
        in_specs=[smem] * 3 + [vmem] + [hbm] * 2,
        out_specs=(vmem,) * 3,
        scratch_shapes=[
            pltpu.SMEM((slots,), i32),
            pltpu.SMEM((slots,), i32),
            pltpu.VMEM(fields.shape, bf16),
            pltpu.VMEM((slots, feature, feature), f32),
            pltpu.VMEM((slots, samples, feature), bf16),
            pltpu.VMEM((slots, feature, 2 * LANES), bf16),
            pltpu.VMEM((slots, samples, feature), bf16),
            pltpu.VMEM((slots, samples, feature), bf16),
            pltpu.VMEM((slots, feature, feature), f32),
            pltpu.VMEM((samples, feature), f32),
            pltpu.VMEM((SUB + slots, LANES), f32),
            pltpu.VMEM((SUB + slots, LANES), f32),
            pltpu.VMEM((slots, samples, feature), bf16),
            pltpu.VMEM((slots, samples, feature), bf16),
            pltpu.VMEM((slots, samples, feature), bf16),
            pltpu.VMEM((slots, feature, 2 * LANES), bf16),
            pltpu.VMEM((slots // 2, feature, feature), i32),
            pltpu.VMEM((slots // 2, feature, feature), i32),
            pltpu.VMEM((slots // 2, feature), f32),
            pltpu.VMEM((slots // 2, feature), f32),
            pltpu.VMEM((groups, SUB, LANES), f32),
            pltpu.VMEM((devices, SUB, LANES), f32),
            pltpu.VMEM((owners // 2, 2 * SUB, LANES), f32),
            pltpu.VMEM((devices, 2 * SUB, LANES), f32),
            pltpu.VMEM((cap, samples, feature), f32),
            pltpu.VMEM((cap, samples, feature), f32),
            pltpu.VMEM((2, groups, owners // 2, rows, feature), i32),
            pltpu.VMEM((2, groups, owners // 2, rows, feature), i32),
            pltpu.VMEM((owners, groups, rows, feature), i32),
            pltpu.VMEM((groups, owners, rows, feature), i32),
            pltpu.VMEM((2 * LANES, LANES), f32),
            pltpu.VMEM((SUB * per_block, chunk // SUB * feature), f32),
            pltpu.SemaphoreType.DMA((RUNS,)),
            pltpu.SemaphoreType.DMA((1,)),
            pltpu.SemaphoreType.DMA((2, groups, RUNS)),
            pltpu.SemaphoreType.DMA((2, devices)),
            pltpu.SemaphoreType.DMA((2, devices)),
            pltpu.SemaphoreType.DMA((2, groups, owners // 2)),
            pltpu.SemaphoreType.DMA((groups, owners)),
            pltpu.SemaphoreType.DMA((2, groups, owners // 2)),
            pltpu.SemaphoreType.DMA((groups, owners)),
            pltpu.SemaphoreType.DMA((2, 1)),
            pltpu.SemaphoreType.DMA((2, groups)),
            pltpu.SemaphoreType.DMA((2, 3)),
        ],
        compiler_params=pltpu.CompilerParams(
            collective_id=0, has_side_effects=True, vmem_limit_bytes=52 * 1024 * 1024
        ),
        cost_estimate=pl.CostEstimate(flops=4 * 10**9, bytes_accessed=8 * 10**6, transcendentals=400),
    )(pair_first, pair_second, pair_count, labels.reshape(1, samples), fields, pair_mats[0, 0])
    return (logits.reshape(samples), grad, new_mats[None, None])


def fits(groups, owners, fields, pair_first):
    samples, _, feature = fields.shape
    slots = pair_first.shape[2]
    cap = slots // groups
    return (
        feature == LANES
        and slots * SUB == LANES
        and slots % groups == 0
        and cap % 2 == 0
        and LANES < samples <= 2 * LANES
        and samples % (SUB * owners) == 0
        and samples % (16 * RUNS) == 0
        and fields.shape[1] & (fields.shape[1] - 1) == 0
        and owners & (owners - 1) == 0
        and owners == 2 * (LANES // (cap * SUB))
        and samples % 32 == 0
        and FIRST_ROW + groups <= SUB
    )


def dispatch(groups, owners, fields, labels, pair_first, pair_second, pair_count, pair_mats):
    args = (fields, labels, pair_first, pair_second, pair_count, pair_mats)
    if fits(groups, owners, fields, pair_first):
        return on_device_kernel(*args)
    return on_device(*args)


def solution(mesh):
    in_specs = (
        P(None, "grp", None),
        P(),
        P("grp", "own", None),
        P(None, "own", None),
        P("grp", "own"),
        P("grp", "own", None, None, None),
    )
    out_specs = (P(), P("own", "grp", None), P("grp", "own", None, None, None))
    per_device = functools.partial(dispatch, mesh.shape["grp"], mesh.shape["own"])
    return jax.shard_map(
        per_device, mesh=mesh, in_specs=in_specs, out_specs=out_specs, check_vma=False
    )
```

```python
import functools
import math

import jax
import jax.numpy as jnp
from jax import lax
from jax.experimental import pallas as pl
from jax.experimental.pallas import tpu as pltpu
from jax.sharding import PartitionSpec as P

STEPS = 2


logit_gain = 1.5
step_size = 1000.0
highest = lax.Precision.HIGHEST


def logit_errors(partial_value, targets, logit_scale):
    total_sum = lax.psum(partial_value, ("grp", "own"))
    logits = logit_scale * total_sum
    errors = jax.nn.sigmoid(logits) - targets
    return (logits, errors)


def on_device(fields, labels, pair_first, pair_second, pair_count, pair_mats):
    groups = lax.axis_size("grp")
    owners = lax.axis_size("own")
    my_group = lax.axis_index("grp")
    samples, per_block, feature = fields.shape
    slot_count = pair_first.shape[2]
    capacity = slot_count // groups
    second_table = pair_second[:, 0, :]
    block_ids = second_table // per_block
    offsets = second_table % per_block
    member = (block_ids[:, :, None] == jnp.arange(groups, dtype=jnp.int32)[None, None, :]).astype(
        jnp.int32
    )
    slot_ranks = jnp.sum((jnp.cumsum(member, axis=1) - 1) * member, axis=2)
    places = block_ids * capacity + slot_ranks
    chosen = (block_ids[:, :, None] == my_group) & (
        slot_ranks[:, :, None] == jnp.arange(capacity, dtype=jnp.int32)[None, None, :]
    )
    served = jnp.sum(jnp.where(chosen, offsets[:, :, None], 0), axis=1).reshape(-1)
    outgoing = jnp.take(fields, served, axis=1)
    incoming = lax.all_to_all(outgoing, "grp", split_axis=1, concat_axis=1, tiled=True)
    my_places = lax.dynamic_index_in_dim(places, my_group, 0, keepdims=False)
    second_vec = jnp.take(incoming, my_places, axis=1).astype(jnp.float32)
    first_local = pair_first[0, 0] - my_group * per_block
    first_vec = jnp.take(fields, first_local, axis=1).astype(jnp.float32)
    live_mask = (jnp.arange(slot_count, dtype=jnp.int32) < pair_count[0, 0]).astype(jnp.float32)
    matrices = pair_mats[0, 0]
    targets = labels.astype(jnp.float32)
    logit_scale = logit_gain / math.sqrt(groups * owners * slot_count)
    root_width = math.sqrt(feature)
    logits = jnp.zeros((samples,), jnp.float32)
    grad_first = jnp.zeros(first_vec.shape, jnp.float32)
    grad_second = jnp.zeros(first_vec.shape, jnp.float32)
    for step_index in range(STEPS):
        mixed = jnp.einsum("bsk,skl->bsl", first_vec, matrices, precision=highest)
        partial_value = jnp.sum(
            jnp.sum(mixed * second_vec, axis=2) / feature * live_mask[None, :], axis=1
        )
        logits, errors = logit_errors(partial_value, targets, logit_scale)
        if step_index == STEPS - 1:
            grad_first = (
                errors[:, None, None]
                * jnp.einsum("skl,bsl->bsk", matrices, second_vec, precision=highest)
                / root_width
                * live_mask[None, :, None]
            )
            grad_second = errors[:, None, None] * mixed / root_width * live_mask[None, :, None]
        gradient = jnp.einsum(
            "bsk,bsl->skl", first_vec * errors[:, None, None], second_vec, precision=highest
        )
        matrices = (
            matrices
            - step_size * logit_scale / (samples * feature) * live_mask[:, None, None] * gradient
        )
    slot_iota = jnp.arange(slot_count, dtype=jnp.int32)
    slot_of = jnp.sum(
        jnp.where(my_places[None, :] == slot_iota[:, None], slot_iota[None, :], 0), axis=1
    )
    returned = lax.all_to_all(
        jnp.take(grad_second, slot_of, axis=1), "grp", split_axis=1, concat_axis=1, tiled=True
    )
    block_iota = jnp.arange(per_block, dtype=jnp.int32)
    pick_second = (served[:, None] == block_iota[None, :]).astype(jnp.float32)
    pick_first = (first_local[:, None] == block_iota[None, :]).astype(jnp.float32)
    dense_grad = jnp.einsum("bsk,sf->bfk", grad_first, pick_first, precision=highest)
    dense_grad = dense_grad + jnp.einsum("bpk,pf->bfk", returned, pick_second, precision=highest)
    field_grad = lax.psum_scatter(dense_grad, "own", scatter_dimension=0, tiled=True)
    return (logits, field_grad, matrices[None, None])


LANES = 128
SUB = 8
TOP = 32760.0
RUNS = 4
SECOND_ROW = 2
FIRST_ROW = 4
MESH = pl.DeviceIdType.MESH
NT = (((1,), (1,)), ((), ()))


def two_parts(x):
    high = x.astype(jnp.bfloat16)
    low = (x - high.astype(jnp.float32)).astype(jnp.bfloat16)
    return high, low


def dot32(a, b):
    return jnp.dot(a, b, preferred_element_type=jnp.float32)


def step_kernel(
    groups, owners,
    first_ids, second_ids, count, labels, fields_in, mats_in,
    logits_out, grad_out, mats_out,
    slot_of, places, fields, mats,
    first_vec, first_t, served_vec, second_vec, mats_mid, total,
    tab_out, tab_in, served_mate, mate_second, mate_first, mate_t, send_m, got_m, unit_m, got_unit_m,
    msg1, got1, msg2, got2, msg3, got3, term_a, term_b, send_a, send_b, got_a, got_b, err_col, acc,
    sem_f, sem_m, sem_v, sem_m1, sem_m2, sem_m3, sem_as, sem_ar, sem_bs, sem_br, sem_tab, sem_w, sem_mat,
):
    samples, per_block, feature = fields.shape
    shift = per_block.bit_length() - 1
    slots = mats.shape[0]
    cap = slots // groups
    chunk = samples // owners
    devices = groups * owners
    pairs = cap // 2
    g, o = lax.axis_index("grp"), lax.axis_index("own")
    me = g * owners + o
    logit_scale = logit_gain / math.sqrt(devices * slots)
    rate = step_size * logit_scale / (samples * feature)
    wing = owners // 2
    mate = lax.rem(o + wing, owners)
    side = lax.div(o, wing)
    half = samples // 2
    base = pl.multiple_of(side * half, 16)
    row_id = lax.broadcasted_iota(jnp.int32, (SUB, LANES), 0)
    lane_id = lax.broadcasted_iota(jnp.int32, (SUB, LANES), 1)
    eye = lax.broadcasted_iota(jnp.int32, (LANES, LANES), 0) == lax.broadcasted_iota(jnp.int32, (LANES, LANES), 1)
    inv_root = 1.0 / math.sqrt(feature)
    extra = 2 * LANES - samples

    run = samples // RUNS

    def load_fields(r):
        part = pl.ds(r * run, run)
        return pltpu.make_async_copy(fields_in.at[part], fields.at[part], sem_f.at[r])

    for r in range(RUNS):
        load_fields(r).start()
    load_mats = pltpu.make_async_copy(mats_in, mats, sem_m.at[0])
    load_mats.start()

    barrier = pltpu.get_barrier_semaphore()

    def greet(d, _):
        peer = lax.rem(me + d, devices)
        pl.semaphore_signal(
            barrier, inc=1, device_id=(lax.div(peer, owners), lax.rem(peer, owners)), device_id_type=MESH
        )
        return 0

    lax.fori_loop(1, devices, greet, 0)

    wide = SUB * per_block

    def pick_scalars(spots):
        lanes = lax.broadcasted_iota(jnp.int32, (SUB, wide), 1)
        lanes = lanes - lax.broadcasted_iota(jnp.int32, (SUB, wide), 0) * per_block
        return jnp.concatenate([jnp.where(lanes == f, 1.0, 0.0) for f in spots], axis=0).astype(jnp.bfloat16)

    def pick_row(row):
        column = jnp.sum(jnp.where(eye, row, 0.0), axis=1, keepdims=True)
        column = (column + 0.5).astype(jnp.int32)
        lanes = lax.broadcasted_iota(jnp.int32, (LANES, wide), 1)
        return jnp.where(lanes == column, 1.0, 0.0).astype(jnp.bfloat16)

    def gather(pick):
        def rows(out, start, size):
            def part(i, _):
                at = pl.multiple_of(start + i * 16, 16)
                blocks = [fields[pl.ds(at + h * SUB, SUB)].reshape(wide, feature) for h in range(2)]
                both = dot32(pick, jnp.concatenate(blocks, axis=1))
                halves = [both[:, h * feature : (h + 1) * feature].reshape(slots, SUB, feature) for h in range(2)]
                out[:, pl.ds(at, 16), :] = jnp.concatenate(halves, axis=1).astype(jnp.bfloat16)
                return 0

            lax.fori_loop(0, size // 16, part, 0, unroll=3)

        return rows

    def vec_copy(j, r):
        to = lax.rem(g + j, groups)
        part = pl.ds(r * run, run)
        return pltpu.make_async_remote_copy(
            src_ref=served_vec.at[pl.ds(to * cap, cap), part],
            dst_ref=second_vec.at[pl.ds(g * cap, cap), part],
            send_sem=sem_v.at[0, j, r],
            recv_sem=sem_v.at[1, j, r],
            device_id=(to, o),
            device_id_type=MESH,
        )

    served = []
    for q in range(groups):
        found, seen = [jnp.int32(0)] * cap, jnp.int32(0)
        for s in range(slots):
            field = second_ids[q, 0, s]
            hit = (field >> shift) == g
            found = [
                jnp.where(jnp.logical_and(hit, seen == c), field & (per_block - 1), f) for c, f in enumerate(found)
            ]
            seen = seen + hit.astype(jnp.int32)
        served += found
    owner_of = [jnp.int32(0)] * slots
    seen = [jnp.int32(0)] * groups
    for s in range(slots):
        block = second_ids[g, 0, s] >> shift
        place = jnp.int32(0)
        for q in range(groups):
            hit = block == q
            place = jnp.where(hit, q * cap + seen[q], place)
            seen[q] = seen[q] + hit.astype(jnp.int32)
        places[s] = place
        owner_of = [jnp.where(place == p, s, t) for p, t in enumerate(owner_of)]
    for p in range(slots):
        slot_of[p] = owner_of[p]
    first_at = [first_ids[0, 0, t] - g * per_block for t in owner_of]
    second_at = [second_ids[g, 0, t] & (per_block - 1) for t in owner_of]

    def live_of(p):
        return jnp.where(slot_of[p] < count[0, 0], 1.0, 0.0)

    gather_served = gather(pick_scalars(served))
    for r in range(RUNS):
        load_fields(r).wait()
        gather_served(served_vec, r * run, run)
        if r == 0:
            pl.semaphore_wait(barrier, devices - 1)
        for j in range(1, groups):
            vec_copy(j, r).start()
    second_vec[pl.ds(g * cap, cap)] = served_vec[pl.ds(g * cap, cap)]

    def full_row(ids):
        spots = jnp.zeros((SUB, LANES), jnp.int32)
        for t in range(slots):
            spots = jnp.where(lane_id // SUB == t, ids[t], spots)
        return (spots + (lane_id % SUB) * per_block).astype(jnp.float32)

    tab_out[0:SUB, :] = jnp.where(row_id == 0, full_row(first_at), jnp.where(row_id == 1, full_row(served), 0.0))
    for p in range(slots):
        tab_out[SUB + p : SUB + p + 1, :] = jnp.zeros((1, LANES), jnp.float32) + live_of(p)

    def to_mate(src, dst, sems, at):
        return pltpu.make_async_remote_copy(
            src_ref=src, dst_ref=dst, send_sem=sems.at[0, at], recv_sem=sems.at[1, at],
            device_id=(g, mate), device_id_type=MESH,
        )

    tab_copy = to_mate(tab_out, tab_in, sem_tab, 0)
    tab_copy.start()
    load_mats.wait()

    def code_mats(t, _):
        a, b = mats[slot_of[2 * t]], mats[slot_of[2 * t + 1]]
        big = jnp.maximum(jnp.max(jnp.maximum(jnp.abs(a), jnp.abs(b)), axis=0, keepdims=True), 1e-30)
        gain = TOP / big
        a, b = [jnp.floor(x * gain + 0.5).astype(jnp.int32) for x in (a, b)]
        send_m[t] = (a & 0xFFFF) | (b << 16)
        unit_m[pl.ds(t, 1), :] = big * (1.0 / TOP)
        return 0

    lax.fori_loop(0, slots // 4, code_mats, 0, unroll=2)
    part = slots // 4
    mat_copies = [to_mate(send_m.at[pl.ds(h * part, part)], got_m.at[pl.ds(h * part, part)], sem_mat, h) for h in range(2)]
    mat_copies.append(to_mate(unit_m, got_unit_m, sem_mat, 2))
    mat_copies[0].start()

    gather(pick_scalars(first_at))(first_vec, 0, samples)

    def turn_all(vecs, turned):
        def turn(p, _):
            v = vecs[p].astype(jnp.float32)
            v = jnp.concatenate([v, jnp.zeros((extra, feature), jnp.float32)], axis=0)
            turned[p] = v.T.astype(jnp.bfloat16)
            return 0

        lax.fori_loop(0, slots, turn, 0, unroll=4)

    lax.fori_loop(slots // 4, slots // 2, code_mats, 0, unroll=2)
    turn_all(first_vec, first_t)
    total[...] = jnp.zeros_like(total)

    def first_pass(q):
        spots = [q * cap + c for c in range(cap)]
        split = [two_parts(mats[slot_of[p]]) for p in spots]
        firsts = [first_vec[p] for p in spots]
        mixed = [
            dot32(jnp.concatenate([v, v], axis=1), jnp.concatenate(parts, axis=0)) for v, parts in zip(firsts, split)
        ]
        sums = total[...]
        for m, p in zip(mixed, spots):
            sums = sums + (m * second_vec[p].astype(jnp.float32)) * live_of(p)
        total[...] = sums

    first_pass(g)
    for j in range(1, groups):
        for r in range(RUNS):
            vec_copy(j, r).wait_recv()
        first_pass(lax.rem(g + groups - j, groups))

    def partial_rows():
        ones = jnp.ones((SUB, feature), jnp.float32)
        tail = jnp.concatenate([total[LANES:samples], jnp.zeros((extra, feature), jnp.float32)], axis=0)
        return [
            lax.dot_general(ones, t, NT, precision=highest, preferred_element_type=jnp.float32)
            for t in (total[0:LANES], tail)
        ]

    segment = cap * SUB
    span = LANES // segment

    def spot_row(ids, q):
        spots = jnp.zeros((SUB, LANES), jnp.int32)
        for c in range(cap):
            spots = jnp.where((lane_id % segment) // SUB == c, ids[q * cap + c], spots)
        spots = spots + (lane_id % SUB) * per_block
        return jnp.where(lane_id // segment == lax.rem(o, span), spots, 0).astype(jnp.float32)

    tables = jnp.zeros((SUB, LANES), jnp.float32)
    for q in range(groups):
        tables = jnp.where(row_id == FIRST_ROW + q, spot_row(first_at, q), tables)
    r0, r1 = partial_rows()
    tables = jnp.where(row_id == 0, r0, jnp.where(row_id == 1, r1, tables))
    for q in range(groups):
        msg1[q] = jnp.where(row_id == SECOND_ROW, spot_row(second_at, q), tables)

    def tile_copy(src, dst, sems, d, pick_own):
        peer = lax.rem(me + d, devices)
        pg, po = lax.div(peer, owners), lax.rem(peer, owners)
        return pltpu.make_async_remote_copy(
            src_ref=src.at[lax.rem(po, wing) if pick_own else pg],
            dst_ref=dst.at[me],
            send_sem=sems.at[0, peer],
            recv_sem=sems.at[1, me],
            device_id=(pg, po),
            device_id_type=MESH,
        )

    def tile_arrival(src, dst, sems, d):
        peer = lax.rem(me + d, devices)
        return pltpu.make_async_remote_copy(
            src_ref=src.at[0],
            dst_ref=dst.at[peer],
            send_sem=sems.at[0, peer],
            recv_sem=sems.at[1, peer],
            device_id=(lax.div(peer, owners), lax.rem(peer, owners)),
            device_id_type=MESH,
        )

    def send_tiles(src, dst, sems, pick_own):
        def one(d, _):
            tile_copy(src, dst, sems, d, pick_own).start()
            return 0

        lax.fori_loop(1, devices, one, 0)

    def wait_tiles(src, dst, sems):
        def one(d, _):
            tile_arrival(src, dst, sems, d).wait_recv()
            return 0

        lax.fori_loop(1, devices, one, 0)

    wanted = labels[...].astype(jnp.float32)
    targets = jnp.concatenate(
        [
            wanted[:, 0:LANES],
            jnp.concatenate([wanted[:, LANES:samples], jnp.zeros((1, extra), jnp.float32)], axis=1),
        ],
        axis=0,
    )

    def errors_of(got, at):
        sums = got[0]
        for d in range(1, devices):
            sums = sums + got[d]
        sums = sums[at : at + 2] * (1.0 / feature)
        logits = logit_scale * sums
        return logits, jax.nn.sigmoid(logits) - targets

    def error_row(err):
        return jnp.concatenate([err[0:1], err[1:2, 0 : samples - LANES]], axis=1)

    def gradients(spots, erow, turned_ref, second_ref):
        turned = [turned_ref[p][:, 0:samples].astype(jnp.float32) * erow for p in spots]
        both = [jnp.concatenate(two_parts(v), axis=0) for v in turned]
        out = [dot32(v, second_ref[p]) for v, p in zip(both, spots)]
        return [x[0:feature] + x[feature:] for x in out]

    send_tiles(msg1, got1, sem_m1, False)
    mat_copies[2].start()
    mat_copies[1].start()
    tab_copy.wait_recv()
    gather(pick_row(tab_in[1:2, :]))(served_mate, 0, samples)

    def mate_copy(j):
        to = lax.rem(g + j, groups)
        return pltpu.make_async_remote_copy(
            src_ref=served_mate.at[pl.ds(to * cap, cap)], dst_ref=mate_second.at[pl.ds(g * cap, cap)],
            send_sem=sem_w.at[0, j], recv_sem=sem_w.at[1, j], device_id=(to, o), device_id_type=MESH,
        )

    for j in range(1, groups):
        mate_copy(j).start()
    mate_second[pl.ds(g * cap, cap)] = served_mate[pl.ds(g * cap, cap)]
    got1[me] = msg1[g]
    wait_tiles(msg1, got1, sem_m1)
    _, err = errors_of(got1, 0)
    erow = error_row(err)
    total[...] = jnp.zeros_like(total)
    msg2[...] = jnp.zeros_like(msg2)
    msg3[...] = jnp.zeros_like(msg3)

    def halved(ref, p):
        return ref[p, pl.ds(base, half), :]

    def twice(v):
        return jnp.concatenate([v, v], axis=1)

    def second_pass(q, m):
        spots = [q * cap + c for c in range(cap)]
        if m == 0:
            lives = [live_of(p) for p in spots]
            old = [mats[slot_of[p]] for p in spots]
            firsts = [first_vec[p] for p in spots]
            seconds = [halved(second_vec, p) for p in spots]
            moves = gradients(spots, erow, first_t, second_vec)
        else:
            lives = [tab_in[pl.ds(SUB + p, 1), :] for p in spots]
            old = []
            for k in range(pairs):
                w = got_m[q * pairs + k]
                unit = got_unit_m[pl.ds(q * pairs + k, 1), :]
                old += [((w << 16) >> 16).astype(jnp.float32) * unit, (w >> 16).astype(jnp.float32) * unit]
            firsts = [halved(mate_first, p) for p in spots]
            seconds = [halved(mate_second, p) for p in spots]
            moves = gradients(spots, erow, mate_t, mate_second)
        mids = [x - (rate * live) * d for x, d, live in zip(old, moves, lives)]
        split = [two_parts(x) for x in mids]
        mixed = [dot32(twice(v), jnp.concatenate(parts, axis=0)) for v, parts in zip(firsts, split)]
        back = [
            lax.dot_general(twice(v), jnp.concatenate(parts, axis=1), NT, preferred_element_type=jnp.float32)
            for v, parts in zip(seconds, split)
        ]
        if m == 0:
            sums = total[...]
            for x, p, live in zip(mixed, spots, lives):
                sums = sums + (x * second_vec[p].astype(jnp.float32)) * live
            total[...] = sums
        for c, p in enumerate(spots):
            factor = lives[c] * inv_root
            term_a[c, pl.ds(base, half), :] = back[c] * factor
            if m == 0:
                mats_mid[p] = mids[c]
                term_b[c] = mixed[c] * factor
            else:
                term_b[c, pl.ds(base, half), :] = mixed[c] * factor

        def code(w, _):
            rows = pl.ds(pl.multiple_of(base + w * chunk, SUB), chunk)
            terms = [t[c, rows, :] for t in (term_a, term_b) for c in range(cap)]
            big = functools.reduce(jnp.maximum, [jnp.abs(t) for t in terms])
            big = jnp.maximum(jnp.max(big, axis=0, keepdims=True), 1e-30)
            gain = TOP / big
            whole = [jnp.floor(t * gain + 0.5).astype(jnp.int32) for t in terms]
            for at, out in ((0, send_a), (cap, send_b)):
                for k in range(pairs):
                    a, b = whole[at + 2 * k], whole[at + 2 * k + 1]
                    out[m, q, w, pl.ds(k * chunk, chunk), :] = (a & 0xFFFF) | (b << 16)
            (msg3 if m else msg2)[w, pl.ds(q, 1), :] = big * (1.0 / TOP)
            return 0

        lax.fori_loop(0, wing, code, 0)

    def partner(k):
        w, bit = o, 1
        while bit < owners:
            w = w + ((k // bit) % 2) * (bit - 2 * bit * ((w // bit) % 2))
            bit *= 2
        return w

    mine = o - side * wing

    def unit_a(m, q, k):
        w = partner(k)
        return pltpu.make_async_remote_copy(
            src_ref=send_a.at[m, q, w - side * wing], dst_ref=got_a.at[mate if m else o, q],
            send_sem=sem_as.at[m, q, k], recv_sem=sem_ar.at[q, mate if m else o],
            device_id=(g, w), device_id_type=MESH,
        )

    def unit_b(m, q, k):
        w = partner(k)
        return pltpu.make_async_remote_copy(
            src_ref=send_b.at[m, q, w - side * wing], dst_ref=got_b.at[g, mate if m else o],
            send_sem=sem_bs.at[m, q, k], recv_sem=sem_br.at[g, mate if m else o],
            device_id=(q, w), device_id_type=MESH,
        )

    def send_units(q, m):
        for k in range(1, wing):
            unit_a(m, q, k).start()
            unit_b(m, q, k).start()
        got_a[mate if m else o, q] = send_a[m, q, mine]

        @pl.when(q == g)
        def _():
            got_b[g, mate if m else o] = send_b[m, g, mine]

        @pl.when(q != g)
        def _():
            unit_b(m, q, 0).start()

    def own_part(j, _):
        q = lax.rem(g + j, groups)
        second_pass(q, 0)
        send_units(q, 0)
        return 0

    lax.fori_loop(0, groups, own_part, 0)
    r0, r1 = partial_rows()
    for w in range(wing):
        msg2[w] = jnp.where(row_id == groups, r0, jnp.where(row_id == groups + 1, r1, msg2[w]))
    send_tiles(msg2, got2, sem_m2, True)
    gather(pick_row(tab_in[0:1, :]))(mate_first, 0, samples)
    turn_all(mate_first, mate_t)
    for j in range(1, groups):
        mate_copy(j).wait_recv()
    for copy in mat_copies:
        copy.wait_recv()

    def mate_part(q, _):
        second_pass(q, 1)
        send_units(q, 1)
        return 0

    lax.fori_loop(0, groups, mate_part, 0)
    def scale_copy(n, k):
        gg, w = lax.rem(g + n, groups), partner(k)
        return pltpu.make_async_remote_copy(
            src_ref=msg3.at[w - side * wing], dst_ref=got3.at[me],
            send_sem=sem_m3.at[0, gg * owners + w], recv_sem=sem_m3.at[1, me],
            device_id=(gg, w), device_id_type=MESH,
        )

    def scale_arrival(n, k):
        gg, w = lax.rem(g + n, groups), partner(k)
        src = gg * owners + w
        return pltpu.make_async_remote_copy(
            src_ref=msg3.at[0], dst_ref=got3.at[src], send_sem=sem_m3.at[0, src], recv_sem=sem_m3.at[1, src],
            device_id=(gg, w), device_id_type=MESH,
        )

    near_peers = [(n, k) for n in range(groups) for k in range(wing) if n + k]
    for n, k in near_peers:
        scale_copy(n, k).start()
    got3[me] = msg3[mine]
    got2[me] = msg2[mine]
    wait_tiles(msg2, got2, sem_m2)
    logits, err = errors_of(got2, groups)
    logits_out[...] = error_row(logits)
    erow = error_row(err)
    for n in range(2):
        column = jnp.sum(jnp.where(eye, err[n : n + 1], 0.0), axis=1, keepdims=True)
        err_col[pl.ds(n * LANES, LANES), :] = jnp.broadcast_to(column, (LANES, LANES))

    def last_update(n, _):
        spots = [places[n * cap + c] for c in range(cap)]
        moves = gradients(spots, erow, first_t, second_vec)
        news = [mats_mid[p] - (rate * live_of(p)) * d for p, d in zip(spots, moves)]
        for c in range(cap):
            mats_out[n * cap + c] = news[c]
        return 0

    lax.fori_loop(0, slots // cap, last_update, 0)

    col = err_col[pl.ds(pl.multiple_of(o * chunk, SUB), chunk), :]
    parts = chunk // SUB
    field_rows = lax.broadcasted_iota(jnp.int32, (SUB * per_block, LANES), 0)

    def decode(word_of, scale):
        out = []
        factor = col * scale
        for k in range(pairs):
            w = word_of(k)
            out.append(((w << 16) >> 16).astype(jnp.float32) * factor)
            out.append((w >> 16).astype(jnp.float32) * factor)
        return out

    def pick_of(spots):
        spots = (spots + 0.5).astype(jnp.int32)
        pick = jnp.where(field_rows == spots, 1.0, 0.0).astype(jnp.bfloat16)
        return [pick, pick]

    def rows_of(terms):
        x = jnp.concatenate(
            [jnp.concatenate([t[i * SUB : (i + 1) * SUB] for t in terms], axis=0) for i in range(parts)], axis=1
        )
        return list(two_parts(x))

    def wait_a(q, w):
        pltpu.make_async_remote_copy(
            src_ref=send_a.at[0, q, 0], dst_ref=got_a.at[w, q], send_sem=sem_as.at[0, q, 0],
            recv_sem=sem_ar.at[q, w], device_id=(g, w), device_id_type=MESH,
        ).wait_recv()

    def wait_b(q, w):
        pltpu.make_async_remote_copy(
            src_ref=send_b.at[0, q, 0], dst_ref=got_b.at[q, w], send_sem=sem_bs.at[0, q, 0],
            recv_sem=sem_br.at[q, w], device_id=(q, w), device_id_type=MESH,
        ).wait_recv()

    acc[...] = jnp.zeros_like(acc)

    for n, k in near_peers:
        scale_arrival(n, k).wait_recv()

    def scale_row(h, src, row):
        rows = pl.ds(row, 1)
        return jnp.where(h == 0, got2[src, rows, :], got3[src, rows, :])

    def arrivals(n, _):
        j, h = n % groups, n // groups
        qa, qb = lax.rem(g + j, groups), lax.rem(g + groups - j, groups)
        terms_a, terms_b, spots_a, spots_b = [], [], 0.0, 0.0
        for i in range(span):
            k = h * span + partner(i) % span
            w = partner(k)
            near = k % wing
            real = partner(near)

            @pl.when(near > 0)
            def _():
                wait_a(qa, w)

            @pl.when(j + near > 0)
            def _():
                wait_b(qb, w)

            scale = scale_row(h, g * owners + real, qa)
            terms_a += decode(lambda m: got_a[w, qa, pl.ds(m * chunk, chunk), :], scale)
            spots_a = spots_a + got1[g * owners + w, pl.ds(FIRST_ROW + qa, 1), :]
            scale = scale_row(h, qb * owners + real, g)
            terms_b += decode(lambda m: got_b[qb, w, pl.ds(m * chunk, chunk), :], scale)
            spots_b = spots_b + got1[qb * owners + w][SECOND_ROW : SECOND_ROW + 1]
        pick = jnp.concatenate(pick_of(spots_a) + pick_of(spots_b), axis=1)
        acc[...] += dot32(pick, jnp.concatenate(rows_of(terms_a) + rows_of(terms_b), axis=0))
        return 0

    lax.fori_loop(0, groups * (owners // span), arrivals, 0)
    for i in range(parts):
        grad_out[i * SUB : (i + 1) * SUB] = acc[:, i * feature : (i + 1) * feature].reshape(SUB, per_block, feature)

    for j in range(1, groups):
        for r in range(RUNS):
            vec_copy(j, r).wait_send()

    def drain_tiles(d, _):
        tile_copy(msg1, got1, sem_m1, d, False).wait_send()
        tile_copy(msg2, got2, sem_m2, d, True).wait_send()
        return 0

    lax.fori_loop(1, devices, drain_tiles, 0)

    for j in range(1, groups):
        mate_copy(j).wait_send()
    for copy in mat_copies + [tab_copy]:
        copy.wait_send()
    for n, k in near_peers:
        scale_copy(n, k).wait_send()

    def drain_units(q, _):
        for m in range(2):
            for k in range(1, wing):
                unit_a(m, q, k).wait_send()
                unit_b(m, q, k).wait_send()

            @pl.when(q != g)
            def _():
                unit_b(m, q, 0).wait_send()

        return 0

    lax.fori_loop(0, groups, drain_units, 0)


def on_device_kernel(fields, labels, pair_first, pair_second, pair_count, pair_mats):
    groups = lax.axis_size("grp")
    owners = lax.axis_size("own")
    samples, per_block, feature = fields.shape
    slots = pair_first.shape[2]
    cap = slots // groups
    chunk = samples // owners
    devices = groups * owners
    smem = pl.BlockSpec(memory_space=pltpu.SMEM)
    vmem = pl.BlockSpec(memory_space=pltpu.VMEM)
    hbm = pl.BlockSpec(memory_space=pltpu.HBM)
    rows = cap // 2 * chunk
    f32, bf16, i32 = jnp.float32, jnp.bfloat16, jnp.int32
    logits, grad, new_mats = pl.pallas_call(
        functools.partial(step_kernel, groups, owners),
        out_shape=(
            jax.ShapeDtypeStruct((1, samples), f32),
            jax.ShapeDtypeStruct((chunk, per_block, feature), f32),
            jax.ShapeDtypeStruct((slots, feature, feature), f32),
        ),
        in_specs=[smem] * 3 + [vmem] + [hbm] * 2,
        out_specs=(vmem,) * 3,
        scratch_shapes=[
            pltpu.SMEM((slots,), i32),
            pltpu.SMEM((slots,), i32),
            pltpu.VMEM(fields.shape, bf16),
            pltpu.VMEM((slots, feature, feature), f32),
            pltpu.VMEM((slots, samples, feature), bf16),
            pltpu.VMEM((slots, feature, 2 * LANES), bf16),
            pltpu.VMEM((slots, samples, feature), bf16),
            pltpu.VMEM((slots, samples, feature), bf16),
            pltpu.VMEM((slots, feature, feature), f32),
            pltpu.VMEM((samples, feature), f32),
            pltpu.VMEM((SUB + slots, LANES), f32),
            pltpu.VMEM((SUB + slots, LANES), f32),
            pltpu.VMEM((slots, samples, feature), bf16),
            pltpu.VMEM((slots, samples, feature), bf16),
            pltpu.VMEM((slots, samples, feature), bf16),
            pltpu.VMEM((slots, feature, 2 * LANES), bf16),
            pltpu.VMEM((slots // 2, feature, feature), i32),
            pltpu.VMEM((slots // 2, feature, feature), i32),
            pltpu.VMEM((slots // 2, feature), f32),
            pltpu.VMEM((slots // 2, feature), f32),
            pltpu.VMEM((groups, SUB, LANES), f32),
            pltpu.VMEM((devices, SUB, LANES), f32),
            pltpu.VMEM((owners // 2, SUB, LANES), f32),
            pltpu.VMEM((devices, SUB, LANES), f32),
            pltpu.VMEM((owners // 2, SUB, LANES), f32),
            pltpu.VMEM((devices, SUB, LANES), f32),
            pltpu.VMEM((cap, samples, feature), f32),
            pltpu.VMEM((cap, samples, feature), f32),
            pltpu.VMEM((2, groups, owners // 2, rows, feature), i32),
            pltpu.VMEM((2, groups, owners // 2, rows, feature), i32),
            pltpu.VMEM((owners, groups, rows, feature), i32),
            pltpu.VMEM((groups, owners, rows, feature), i32),
            pltpu.VMEM((2 * LANES, LANES), f32),
            pltpu.VMEM((SUB * per_block, chunk // SUB * feature), f32),
            pltpu.SemaphoreType.DMA((RUNS,)),
            pltpu.SemaphoreType.DMA((1,)),
            pltpu.SemaphoreType.DMA((2, groups, RUNS)),
            pltpu.SemaphoreType.DMA((2, devices)),
            pltpu.SemaphoreType.DMA((2, devices)),
            pltpu.SemaphoreType.DMA((2, devices)),
            pltpu.SemaphoreType.DMA((2, groups, owners // 2)),
            pltpu.SemaphoreType.DMA((groups, owners)),
            pltpu.SemaphoreType.DMA((2, groups, owners // 2)),
            pltpu.SemaphoreType.DMA((groups, owners)),
            pltpu.SemaphoreType.DMA((2, 1)),
            pltpu.SemaphoreType.DMA((2, groups)),
            pltpu.SemaphoreType.DMA((2, 3)),
        ],
        compiler_params=pltpu.CompilerParams(
            collective_id=0, has_side_effects=True, vmem_limit_bytes=52 * 1024 * 1024
        ),
        cost_estimate=pl.CostEstimate(flops=4 * 10**9, bytes_accessed=8 * 10**6, transcendentals=400),
    )(pair_first, pair_second, pair_count, labels.reshape(1, samples), fields, pair_mats[0, 0])
    return (logits.reshape(samples), grad, new_mats[None, None])


def fits(groups, owners, fields, pair_first):
    samples, _, feature = fields.shape
    slots = pair_first.shape[2]
    cap = slots // groups
    return (
        feature == LANES
        and slots * SUB == LANES
        and slots % groups == 0
        and cap % 2 == 0
        and LANES < samples <= 2 * LANES
        and samples % (SUB * owners) == 0
        and samples % (16 * RUNS) == 0
        and fields.shape[1] & (fields.shape[1] - 1) == 0
        and owners & (owners - 1) == 0
        and owners == 2 * (LANES // (cap * SUB))
        and samples % 32 == 0
        and FIRST_ROW + groups <= SUB
    )


def dispatch(groups, owners, fields, labels, pair_first, pair_second, pair_count, pair_mats):
    args = (fields, labels, pair_first, pair_second, pair_count, pair_mats)
    if fits(groups, owners, fields, pair_first):
        return on_device_kernel(*args)
    return on_device(*args)


def solution(mesh):
    in_specs = (
        P(None, "grp", None),
        P(),
        P("grp", "own", None),
        P(None, "own", None),
        P("grp", "own"),
        P("grp", "own", None, None, None),
    )
    out_specs = (P(), P("own", "grp", None), P("grp", "own", None, None, None))
    per_device = functools.partial(dispatch, mesh.shape["grp"], mesh.shape["own"])
    return jax.shard_map(
        per_device, mesh=mesh, in_specs=in_specs, out_specs=out_specs, check_vma=False
    )
```

```python
import functools
import math

import jax
import jax.numpy as jnp
from jax import lax
from jax.experimental import pallas as pl
from jax.experimental.pallas import tpu as pltpu
from jax.sharding import PartitionSpec as P

STEPS = 2


logit_gain = 1.5
step_size = 1000.0
highest = lax.Precision.HIGHEST


def logit_errors(partial_value, targets, logit_scale):
    total_sum = lax.psum(partial_value, ("grp", "own"))
    logits = logit_scale * total_sum
    errors = jax.nn.sigmoid(logits) - targets
    return (logits, errors)


def on_device(fields, labels, pair_first, pair_second, pair_count, pair_mats):
    groups = lax.axis_size("grp")
    owners = lax.axis_size("own")
    my_group = lax.axis_index("grp")
    samples, per_block, feature = fields.shape
    slot_count = pair_first.shape[2]
    capacity = slot_count // groups
    second_table = pair_second[:, 0, :]
    block_ids = second_table // per_block
    offsets = second_table % per_block
    member = (block_ids[:, :, None] == jnp.arange(groups, dtype=jnp.int32)[None, None, :]).astype(
        jnp.int32
    )
    slot_ranks = jnp.sum((jnp.cumsum(member, axis=1) - 1) * member, axis=2)
    places = block_ids * capacity + slot_ranks
    chosen = (block_ids[:, :, None] == my_group) & (
        slot_ranks[:, :, None] == jnp.arange(capacity, dtype=jnp.int32)[None, None, :]
    )
    served = jnp.sum(jnp.where(chosen, offsets[:, :, None], 0), axis=1).reshape(-1)
    outgoing = jnp.take(fields, served, axis=1)
    incoming = lax.all_to_all(outgoing, "grp", split_axis=1, concat_axis=1, tiled=True)
    my_places = lax.dynamic_index_in_dim(places, my_group, 0, keepdims=False)
    second_vec = jnp.take(incoming, my_places, axis=1).astype(jnp.float32)
    first_local = pair_first[0, 0] - my_group * per_block
    first_vec = jnp.take(fields, first_local, axis=1).astype(jnp.float32)
    live_mask = (jnp.arange(slot_count, dtype=jnp.int32) < pair_count[0, 0]).astype(jnp.float32)
    matrices = pair_mats[0, 0]
    targets = labels.astype(jnp.float32)
    logit_scale = logit_gain / math.sqrt(groups * owners * slot_count)
    root_width = math.sqrt(feature)
    logits = jnp.zeros((samples,), jnp.float32)
    grad_first = jnp.zeros(first_vec.shape, jnp.float32)
    grad_second = jnp.zeros(first_vec.shape, jnp.float32)
    for step_index in range(STEPS):
        mixed = jnp.einsum("bsk,skl->bsl", first_vec, matrices, precision=highest)
        partial_value = jnp.sum(
            jnp.sum(mixed * second_vec, axis=2) / feature * live_mask[None, :], axis=1
        )
        logits, errors = logit_errors(partial_value, targets, logit_scale)
        if step_index == STEPS - 1:
            grad_first = (
                errors[:, None, None]
                * jnp.einsum("skl,bsl->bsk", matrices, second_vec, precision=highest)
                / root_width
                * live_mask[None, :, None]
            )
            grad_second = errors[:, None, None] * mixed / root_width * live_mask[None, :, None]
        gradient = jnp.einsum(
            "bsk,bsl->skl", first_vec * errors[:, None, None], second_vec, precision=highest
        )
        matrices = (
            matrices
            - step_size * logit_scale / (samples * feature) * live_mask[:, None, None] * gradient
        )
    slot_iota = jnp.arange(slot_count, dtype=jnp.int32)
    slot_of = jnp.sum(
        jnp.where(my_places[None, :] == slot_iota[:, None], slot_iota[None, :], 0), axis=1
    )
    returned = lax.all_to_all(
        jnp.take(grad_second, slot_of, axis=1), "grp", split_axis=1, concat_axis=1, tiled=True
    )
    block_iota = jnp.arange(per_block, dtype=jnp.int32)
    pick_second = (served[:, None] == block_iota[None, :]).astype(jnp.float32)
    pick_first = (first_local[:, None] == block_iota[None, :]).astype(jnp.float32)
    dense_grad = jnp.einsum("bsk,sf->bfk", grad_first, pick_first, precision=highest)
    dense_grad = dense_grad + jnp.einsum("bpk,pf->bfk", returned, pick_second, precision=highest)
    field_grad = lax.psum_scatter(dense_grad, "own", scatter_dimension=0, tiled=True)
    return (logits, field_grad, matrices[None, None])


LANES = 128
SUB = 8
TOP = 32760.0
RUNS = 4
SECOND_ROW = 2
FIRST_ROW = 4
MESH = pl.DeviceIdType.MESH
NT = (((1,), (1,)), ((), ()))


def two_parts(x):
    high = x.astype(jnp.bfloat16)
    low = (x - high.astype(jnp.float32)).astype(jnp.bfloat16)
    return high, low


def dot32(a, b):
    return jnp.dot(a, b, preferred_element_type=jnp.float32)


def step_kernel(
    groups, owners,
    first_ids, second_ids, count, labels, fields_in, mats_in,
    logits_out, grad_out, mats_out,
    slot_of, places, fields, mats,
    first_vec, first_t, served_vec, second_vec, mats_mid, total,
    tab_out, tab_in, served_mate, mate_second, mate_first, mate_t, send_m, got_m, unit_m, got_unit_m,
    msg1, got1, msg2, got2, msg3, got3, term_a, term_b, send_a, send_b, got_a, got_b, err_col, acc,
    sem_f, sem_m, sem_v, sem_m1, sem_m2, sem_m3, sem_as, sem_ar, sem_bs, sem_br, sem_tab, sem_w, sem_mat,
):
    samples, per_block, feature = fields.shape
    shift = per_block.bit_length() - 1
    slots = mats.shape[0]
    cap = slots // groups
    chunk = samples // owners
    devices = groups * owners
    pairs = cap // 2
    g, o = lax.axis_index("grp"), lax.axis_index("own")
    me = g * owners + o
    logit_scale = logit_gain / math.sqrt(devices * slots)
    rate = step_size * logit_scale / (samples * feature)
    wing = owners // 2
    mate = lax.rem(o + wing, owners)
    side = lax.div(o, wing)
    half = samples // 2
    base = pl.multiple_of(side * half, 16)
    row_id = lax.broadcasted_iota(jnp.int32, (SUB, LANES), 0)
    lane_id = lax.broadcasted_iota(jnp.int32, (SUB, LANES), 1)
    eye = lax.broadcasted_iota(jnp.int32, (LANES, LANES), 0) == lax.broadcasted_iota(jnp.int32, (LANES, LANES), 1)
    inv_root = 1.0 / math.sqrt(feature)
    extra = 2 * LANES - samples

    run = samples // RUNS

    def load_fields(r):
        part = pl.ds(r * run, run)
        return pltpu.make_async_copy(fields_in.at[part], fields.at[part], sem_f.at[r])

    for r in range(RUNS):
        load_fields(r).start()
    load_mats = pltpu.make_async_copy(mats_in, mats, sem_m.at[0])
    load_mats.start()

    barrier = pltpu.get_barrier_semaphore()

    def greet(d, _):
        peer = lax.rem(me + d, devices)
        pl.semaphore_signal(
            barrier, inc=1, device_id=(lax.div(peer, owners), lax.rem(peer, owners)), device_id_type=MESH
        )
        return 0

    lax.fori_loop(1, devices, greet, 0)

    wide = SUB * per_block

    def pick_scalars(spots):
        lanes = lax.broadcasted_iota(jnp.int32, (SUB, wide), 1)
        lanes = lanes - lax.broadcasted_iota(jnp.int32, (SUB, wide), 0) * per_block
        return jnp.concatenate([jnp.where(lanes == f, 1.0, 0.0) for f in spots], axis=0).astype(jnp.bfloat16)

    def pick_row(row):
        column = jnp.sum(jnp.where(eye, row, 0.0), axis=1, keepdims=True)
        column = (column + 0.5).astype(jnp.int32)
        lanes = lax.broadcasted_iota(jnp.int32, (LANES, wide), 1)
        return jnp.where(lanes == column, 1.0, 0.0).astype(jnp.bfloat16)

    def gather(pick):
        def rows(out, start, size):
            def part(i, _):
                at = pl.multiple_of(start + i * 16, 16)
                blocks = [fields[pl.ds(at + h * SUB, SUB)].reshape(wide, feature) for h in range(2)]
                both = dot32(pick, jnp.concatenate(blocks, axis=1))
                halves = [both[:, h * feature : (h + 1) * feature].reshape(slots, SUB, feature) for h in range(2)]
                out[:, pl.ds(at, 16), :] = jnp.concatenate(halves, axis=1).astype(jnp.bfloat16)
                return 0

            lax.fori_loop(0, size // 16, part, 0, unroll=3)

        return rows

    def vec_copy(j, r):
        to = lax.rem(g + j, groups)
        part = pl.ds(r * run, run)
        return pltpu.make_async_remote_copy(
            src_ref=served_vec.at[pl.ds(to * cap, cap), part],
            dst_ref=second_vec.at[pl.ds(g * cap, cap), part],
            send_sem=sem_v.at[0, j, r],
            recv_sem=sem_v.at[1, j, r],
            device_id=(to, o),
            device_id_type=MESH,
        )

    served = []
    for q in range(groups):
        found, seen = [jnp.int32(0)] * cap, jnp.int32(0)
        for s in range(slots):
            field = second_ids[q, 0, s]
            hit = (field >> shift) == g
            found = [
                jnp.where(jnp.logical_and(hit, seen == c), field & (per_block - 1), f) for c, f in enumerate(found)
            ]
            seen = seen + hit.astype(jnp.int32)
        served += found
    owner_of = [jnp.int32(0)] * slots
    seen = [jnp.int32(0)] * groups
    for s in range(slots):
        block = second_ids[g, 0, s] >> shift
        place = jnp.int32(0)
        for q in range(groups):
            hit = block == q
            place = jnp.where(hit, q * cap + seen[q], place)
            seen[q] = seen[q] + hit.astype(jnp.int32)
        places[s] = place
        owner_of = [jnp.where(place == p, s, t) for p, t in enumerate(owner_of)]
    for p in range(slots):
        slot_of[p] = owner_of[p]
    first_at = [first_ids[0, 0, t] - g * per_block for t in owner_of]
    second_at = [second_ids[g, 0, t] & (per_block - 1) for t in owner_of]

    def live_of(p):
        return jnp.where(slot_of[p] < count[0, 0], 1.0, 0.0)

    gather_served = gather(pick_scalars(served))
    for r in range(RUNS):
        load_fields(r).wait()
        gather_served(served_vec, r * run, run)
        if r == 0:
            pl.semaphore_wait(barrier, devices - 1)
        for j in range(1, groups):
            vec_copy(j, r).start()
    second_vec[pl.ds(g * cap, cap)] = served_vec[pl.ds(g * cap, cap)]

    def full_row(ids):
        spots = jnp.zeros((SUB, LANES), jnp.int32)
        for t in range(slots):
            spots = jnp.where(lane_id // SUB == t, ids[t], spots)
        return (spots + (lane_id % SUB) * per_block).astype(jnp.float32)

    tab_out[0:SUB, :] = jnp.where(row_id == 0, full_row(first_at), jnp.where(row_id == 1, full_row(served), 0.0))
    for p in range(slots):
        tab_out[SUB + p : SUB + p + 1, :] = jnp.zeros((1, LANES), jnp.float32) + live_of(p)

    def to_mate(src, dst, sems, at):
        return pltpu.make_async_remote_copy(
            src_ref=src, dst_ref=dst, send_sem=sems.at[0, at], recv_sem=sems.at[1, at],
            device_id=(g, mate), device_id_type=MESH,
        )

    tab_copy = to_mate(tab_out, tab_in, sem_tab, 0)
    tab_copy.start()
    load_mats.wait()

    def code_mats(t, _):
        a, b = mats[slot_of[2 * t]], mats[slot_of[2 * t + 1]]
        big = jnp.maximum(jnp.max(jnp.maximum(jnp.abs(a), jnp.abs(b)), axis=0, keepdims=True), 1e-30)
        gain = TOP / big
        a, b = [jnp.floor(x * gain + 0.5).astype(jnp.int32) for x in (a, b)]
        send_m[t] = (a & 0xFFFF) | (b << 16)
        unit_m[pl.ds(t, 1), :] = big * (1.0 / TOP)
        return 0

    lax.fori_loop(0, slots // 4, code_mats, 0, unroll=4)
    part = slots // 4
    mat_copies = [to_mate(send_m.at[pl.ds(h * part, part)], got_m.at[pl.ds(h * part, part)], sem_mat, h) for h in range(2)]
    mat_copies.append(to_mate(unit_m, got_unit_m, sem_mat, 2))
    mat_copies[0].start()

    gather(pick_scalars(first_at))(first_vec, 0, samples)

    def turn_all(vecs, turned):
        def turn(p, _):
            v = vecs[p].astype(jnp.float32)
            v = jnp.concatenate([v, jnp.zeros((extra, feature), jnp.float32)], axis=0)
            turned[p] = v.T.astype(jnp.bfloat16)
            return 0

        lax.fori_loop(0, slots, turn, 0, unroll=4)

    lax.fori_loop(slots // 4, slots // 2, code_mats, 0, unroll=4)
    turn_all(first_vec, first_t)
    total[...] = jnp.zeros_like(total)

    def first_pass(q):
        spots = [q * cap + c for c in range(cap)]
        split = [two_parts(mats[slot_of[p]]) for p in spots]
        firsts = [first_vec[p] for p in spots]
        mixed = [
            dot32(jnp.concatenate([v, v], axis=1), jnp.concatenate(parts, axis=0)) for v, parts in zip(firsts, split)
        ]
        sums = total[...]
        for m, p in zip(mixed, spots):
            sums = sums + (m * second_vec[p].astype(jnp.float32)) * live_of(p)
        total[...] = sums

    first_pass(g)
    for j in range(1, groups):
        for r in range(RUNS):
            vec_copy(j, r).wait_recv()
        first_pass(lax.rem(g + groups - j, groups))

    def partial_rows():
        ones = jnp.ones((SUB, feature), jnp.float32)
        tail = jnp.concatenate([total[LANES:samples], jnp.zeros((extra, feature), jnp.float32)], axis=0)
        return [
            lax.dot_general(ones, t, NT, precision=highest, preferred_element_type=jnp.float32)
            for t in (total[0:LANES], tail)
        ]

    segment = cap * SUB
    span = LANES // segment

    def spot_row(ids, q):
        spots = jnp.zeros((SUB, LANES), jnp.int32)
        for c in range(cap):
            spots = jnp.where((lane_id % segment) // SUB == c, ids[q * cap + c], spots)
        spots = spots + (lane_id % SUB) * per_block
        return jnp.where(lane_id // segment == lax.rem(o, span), spots, 0).astype(jnp.float32)

    tables = jnp.zeros((SUB, LANES), jnp.float32)
    for q in range(groups):
        tables = jnp.where(row_id == FIRST_ROW + q, spot_row(first_at, q), tables)
    r0, r1 = partial_rows()
    tables = jnp.where(row_id == 0, r0, jnp.where(row_id == 1, r1, tables))
    for q in range(groups):
        msg1[q] = jnp.where(row_id == SECOND_ROW, spot_row(second_at, q), tables)

    def tile_copy(src, dst, sems, d, pick_own):
        peer = lax.rem(me + d, devices)
        pg, po = lax.div(peer, owners), lax.rem(peer, owners)
        return pltpu.make_async_remote_copy(
            src_ref=src.at[lax.rem(po, wing) if pick_own else pg],
            dst_ref=dst.at[me],
            send_sem=sems.at[0, peer],
            recv_sem=sems.at[1, me],
            device_id=(pg, po),
            device_id_type=MESH,
        )

    def tile_arrival(src, dst, sems, d):
        peer = lax.rem(me + d, devices)
        return pltpu.make_async_remote_copy(
            src_ref=src.at[0],
            dst_ref=dst.at[peer],
            send_sem=sems.at[0, peer],
            recv_sem=sems.at[1, peer],
            device_id=(lax.div(peer, owners), lax.rem(peer, owners)),
            device_id_type=MESH,
        )

    def send_tiles(src, dst, sems, pick_own):
        def one(d, _):
            tile_copy(src, dst, sems, d, pick_own).start()
            return 0

        lax.fori_loop(1, devices, one, 0)

    def wait_tiles(src, dst, sems):
        def one(d, _):
            tile_arrival(src, dst, sems, d).wait_recv()
            return 0

        lax.fori_loop(1, devices, one, 0)

    wanted = labels[...].astype(jnp.float32)
    targets = jnp.concatenate(
        [
            wanted[:, 0:LANES],
            jnp.concatenate([wanted[:, LANES:samples], jnp.zeros((1, extra), jnp.float32)], axis=1),
        ],
        axis=0,
    )

    def errors_of(got, at):
        sums = got[0]
        for d in range(1, devices):
            sums = sums + got[d]
        sums = sums[at : at + 2] * (1.0 / feature)
        logits = logit_scale * sums
        return logits, jax.nn.sigmoid(logits) - targets

    def error_row(err):
        return jnp.concatenate([err[0:1], err[1:2, 0 : samples - LANES]], axis=1)

    def gradients(spots, erow, turned_ref, second_ref):
        turned = [turned_ref[p][:, 0:samples].astype(jnp.float32) * erow for p in spots]
        both = [jnp.concatenate(two_parts(v), axis=0) for v in turned]
        out = [dot32(v, second_ref[p]) for v, p in zip(both, spots)]
        return [x[0:feature] + x[feature:] for x in out]

    send_tiles(msg1, got1, sem_m1, False)
    mat_copies[2].start()
    mat_copies[1].start()
    tab_copy.wait_recv()
    gather(pick_row(tab_in[1:2, :]))(served_mate, 0, samples)

    def mate_copy(j):
        to = lax.rem(g + j, groups)
        return pltpu.make_async_remote_copy(
            src_ref=served_mate.at[pl.ds(to * cap, cap)], dst_ref=mate_second.at[pl.ds(g * cap, cap)],
            send_sem=sem_w.at[0, j], recv_sem=sem_w.at[1, j], device_id=(to, o), device_id_type=MESH,
        )

    for j in range(1, groups):
        mate_copy(j).start()
    mate_second[pl.ds(g * cap, cap)] = served_mate[pl.ds(g * cap, cap)]
    got1[me] = msg1[g]
    wait_tiles(msg1, got1, sem_m1)
    _, err = errors_of(got1, 0)
    erow = error_row(err)
    total[...] = jnp.zeros_like(total)
    msg2[...] = jnp.zeros_like(msg2)
    msg3[...] = jnp.zeros_like(msg3)

    def halved(ref, p):
        return ref[p, pl.ds(base, half), :]

    def twice(v):
        return jnp.concatenate([v, v], axis=1)

    def second_pass(q, m):
        spots = [q * cap + c for c in range(cap)]
        if m == 0:
            lives = [live_of(p) for p in spots]
            old = [mats[slot_of[p]] for p in spots]
            firsts = [first_vec[p] for p in spots]
            seconds = [halved(second_vec, p) for p in spots]
            moves = gradients(spots, erow, first_t, second_vec)
        else:
            lives = [tab_in[pl.ds(SUB + p, 1), :] for p in spots]
            old = []
            for k in range(pairs):
                w = got_m[q * pairs + k]
                unit = got_unit_m[pl.ds(q * pairs + k, 1), :]
                old += [((w << 16) >> 16).astype(jnp.float32) * unit, (w >> 16).astype(jnp.float32) * unit]
            firsts = [halved(mate_first, p) for p in spots]
            seconds = [halved(mate_second, p) for p in spots]
            moves = gradients(spots, erow, mate_t, mate_second)
        mids = [x - (rate * live) * d for x, d, live in zip(old, moves, lives)]
        split = [two_parts(x) for x in mids]
        mixed = [dot32(twice(v), jnp.concatenate(parts, axis=0)) for v, parts in zip(firsts, split)]
        back = [
            lax.dot_general(twice(v), jnp.concatenate(parts, axis=1), NT, preferred_element_type=jnp.float32)
            for v, parts in zip(seconds, split)
        ]
        if m == 0:
            sums = total[...]
            for x, p, live in zip(mixed, spots, lives):
                sums = sums + (x * second_vec[p].astype(jnp.float32)) * live
            total[...] = sums
        for c, p in enumerate(spots):
            factor = lives[c] * inv_root
            term_a[c, pl.ds(base, half), :] = back[c] * factor
            if m == 0:
                mats_mid[p] = mids[c]
                term_b[c] = mixed[c] * factor
            else:
                term_b[c, pl.ds(base, half), :] = mixed[c] * factor

        def code(w, _):
            rows = pl.ds(pl.multiple_of(base + w * chunk, SUB), chunk)
            terms = [t[c, rows, :] for t in (term_a, term_b) for c in range(cap)]
            big = functools.reduce(jnp.maximum, [jnp.abs(t) for t in terms])
            big = jnp.maximum(jnp.max(big, axis=0, keepdims=True), 1e-30)
            gain = TOP / big
            whole = [jnp.floor(t * gain + 0.5).astype(jnp.int32) for t in terms]
            for at, out in ((0, send_a), (cap, send_b)):
                for k in range(pairs):
                    a, b = whole[at + 2 * k], whole[at + 2 * k + 1]
                    out[m, q, w, pl.ds(k * chunk, chunk), :] = (a & 0xFFFF) | (b << 16)
            (msg3 if m else msg2)[w, pl.ds(q, 1), :] = big * (1.0 / TOP)
            return 0

        lax.fori_loop(0, wing, code, 0, unroll=True)

    def partner(k):
        w, bit = o, 1
        while bit < owners:
            w = w + ((k // bit) % 2) * (bit - 2 * bit * ((w // bit) % 2))
            bit *= 2
        return w

    mine = o - side * wing

    def unit_a(m, q, k):
        w = partner(k)
        return pltpu.make_async_remote_copy(
            src_ref=send_a.at[m, q, w - side * wing], dst_ref=got_a.at[mate if m else o, q],
            send_sem=sem_as.at[m, q, k], recv_sem=sem_ar.at[q, mate if m else o],
            device_id=(g, w), device_id_type=MESH,
        )

    def unit_b(m, q, k):
        w = partner(k)
        return pltpu.make_async_remote_copy(
            src_ref=send_b.at[m, q, w - side * wing], dst_ref=got_b.at[g, mate if m else o],
            send_sem=sem_bs.at[m, q, k], recv_sem=sem_br.at[g, mate if m else o],
            device_id=(q, w), device_id_type=MESH,
        )

    def send_units(q, m):
        for k in range(1, wing):
            unit_a(m, q, k).start()
            unit_b(m, q, k).start()
        got_a[mate if m else o, q] = send_a[m, q, mine]

        @pl.when(q == g)
        def _():
            got_b[g, mate if m else o] = send_b[m, g, mine]

        @pl.when(q != g)
        def _():
            unit_b(m, q, 0).start()

    def own_part(j, _):
        q = lax.rem(g + j, groups)
        second_pass(q, 0)
        send_units(q, 0)
        return 0

    lax.fori_loop(0, groups, own_part, 0)
    r0, r1 = partial_rows()
    for w in range(wing):
        msg2[w] = jnp.where(row_id == groups, r0, jnp.where(row_id == groups + 1, r1, msg2[w]))
    send_tiles(msg2, got2, sem_m2, True)
    gather(pick_row(tab_in[0:1, :]))(mate_first, 0, samples)
    turn_all(mate_first, mate_t)
    for j in range(1, groups):
        mate_copy(j).wait_recv()
    for copy in mat_copies:
        copy.wait_recv()

    def mate_part(q, _):
        second_pass(q, 1)
        send_units(q, 1)
        return 0

    lax.fori_loop(0, groups, mate_part, 0)
    def scale_copy(n, k):
        gg, w = lax.rem(g + n, groups), partner(k)
        return pltpu.make_async_remote_copy(
            src_ref=msg3.at[w - side * wing], dst_ref=got3.at[me],
            send_sem=sem_m3.at[0, gg * owners + w], recv_sem=sem_m3.at[1, me],
            device_id=(gg, w), device_id_type=MESH,
        )

    def scale_arrival(n, k):
        gg, w = lax.rem(g + n, groups), partner(k)
        src = gg * owners + w
        return pltpu.make_async_remote_copy(
            src_ref=msg3.at[0], dst_ref=got3.at[src], send_sem=sem_m3.at[0, src], recv_sem=sem_m3.at[1, src],
            device_id=(gg, w), device_id_type=MESH,
        )

    near_peers = [(n, k) for n in range(groups) for k in range(wing) if n + k]
    for n, k in near_peers:
        scale_copy(n, k).start()
    got3[me] = msg3[mine]
    got2[me] = msg2[mine]
    wait_tiles(msg2, got2, sem_m2)
    logits, err = errors_of(got2, groups)
    logits_out[...] = error_row(logits)
    erow = error_row(err)
    for n in range(2):
        column = jnp.sum(jnp.where(eye, err[n : n + 1], 0.0), axis=1, keepdims=True)
        err_col[pl.ds(n * LANES, LANES), :] = jnp.broadcast_to(column, (LANES, LANES))

    def last_update(n, _):
        spots = [places[n * cap + c] for c in range(cap)]
        moves = gradients(spots, erow, first_t, second_vec)
        news = [mats_mid[p] - (rate * live_of(p)) * d for p, d in zip(spots, moves)]
        for c in range(cap):
            mats_out[n * cap + c] = news[c]
        return 0

    lax.fori_loop(0, slots // cap, last_update, 0, unroll=2)

    col = err_col[pl.ds(pl.multiple_of(o * chunk, SUB), chunk), :]
    parts = chunk // SUB
    field_rows = lax.broadcasted_iota(jnp.int32, (SUB * per_block, LANES), 0)

    def decode(word_of, scale):
        out = []
        factor = col * scale
        for k in range(pairs):
            w = word_of(k)
            out.append(((w << 16) >> 16).astype(jnp.float32) * factor)
            out.append((w >> 16).astype(jnp.float32) * factor)
        return out

    def pick_of(spots):
        spots = (spots + 0.5).astype(jnp.int32)
        pick = jnp.where(field_rows == spots, 1.0, 0.0).astype(jnp.bfloat16)
        return [pick, pick]

    def rows_of(terms):
        x = jnp.concatenate(
            [jnp.concatenate([t[i * SUB : (i + 1) * SUB] for t in terms], axis=0) for i in range(parts)], axis=1
        )
        return list(two_parts(x))

    def wait_a(q, w):
        pltpu.make_async_remote_copy(
            src_ref=send_a.at[0, q, 0], dst_ref=got_a.at[w, q], send_sem=sem_as.at[0, q, 0],
            recv_sem=sem_ar.at[q, w], device_id=(g, w), device_id_type=MESH,
        ).wait_recv()

    def wait_b(q, w):
        pltpu.make_async_remote_copy(
            src_ref=send_b.at[0, q, 0], dst_ref=got_b.at[q, w], send_sem=sem_bs.at[0, q, 0],
            recv_sem=sem_br.at[q, w], device_id=(q, w), device_id_type=MESH,
        ).wait_recv()

    acc[...] = jnp.zeros_like(acc)

    for n, k in near_peers:
        scale_arrival(n, k).wait_recv()

    def scale_row(h, src, row):
        rows = pl.ds(row, 1)
        return jnp.where(h == 0, got2[src, rows, :], got3[src, rows, :])

    def arrivals(n, _):
        j, h = n % groups, n // groups
        qa, qb = lax.rem(g + j, groups), lax.rem(g + groups - j, groups)
        terms_a, terms_b, spots_a, spots_b = [], [], 0.0, 0.0
        for i in range(span):
            k = h * span + partner(i) % span
            w = partner(k)
            near = k % wing
            real = partner(near)

            @pl.when(near > 0)
            def _():
                wait_a(qa, w)

            @pl.when(j + near > 0)
            def _():
                wait_b(qb, w)

            scale = scale_row(h, g * owners + real, qa)
            terms_a += decode(lambda m: got_a[w, qa, pl.ds(m * chunk, chunk), :], scale)
            spots_a = spots_a + got1[g * owners + w, pl.ds(FIRST_ROW + qa, 1), :]
            scale = scale_row(h, qb * owners + real, g)
            terms_b += decode(lambda m: got_b[qb, w, pl.ds(m * chunk, chunk), :], scale)
            spots_b = spots_b + got1[qb * owners + w][SECOND_ROW : SECOND_ROW + 1]
        pick = jnp.concatenate(pick_of(spots_a) + pick_of(spots_b), axis=1)
        acc[...] += dot32(pick, jnp.concatenate(rows_of(terms_a) + rows_of(terms_b), axis=0))
        return 0

    lax.fori_loop(0, groups * (owners // span), arrivals, 0, unroll=2)
    for i in range(parts):
        grad_out[i * SUB : (i + 1) * SUB] = acc[:, i * feature : (i + 1) * feature].reshape(SUB, per_block, feature)

    for j in range(1, groups):
        for r in range(RUNS):
            vec_copy(j, r).wait_send()

    def drain_tiles(d, _):
        tile_copy(msg1, got1, sem_m1, d, False).wait_send()
        tile_copy(msg2, got2, sem_m2, d, True).wait_send()
        return 0

    lax.fori_loop(1, devices, drain_tiles, 0)

    for j in range(1, groups):
        mate_copy(j).wait_send()
    for copy in mat_copies + [tab_copy]:
        copy.wait_send()
    for n, k in near_peers:
        scale_copy(n, k).wait_send()

    def drain_units(q, _):
        for m in range(2):
            for k in range(1, wing):
                unit_a(m, q, k).wait_send()
                unit_b(m, q, k).wait_send()

            @pl.when(q != g)
            def _():
                unit_b(m, q, 0).wait_send()

        return 0

    lax.fori_loop(0, groups, drain_units, 0)


def on_device_kernel(fields, labels, pair_first, pair_second, pair_count, pair_mats):
    groups = lax.axis_size("grp")
    owners = lax.axis_size("own")
    samples, per_block, feature = fields.shape
    slots = pair_first.shape[2]
    cap = slots // groups
    chunk = samples // owners
    devices = groups * owners
    smem = pl.BlockSpec(memory_space=pltpu.SMEM)
    vmem = pl.BlockSpec(memory_space=pltpu.VMEM)
    hbm = pl.BlockSpec(memory_space=pltpu.HBM)
    rows = cap // 2 * chunk
    f32, bf16, i32 = jnp.float32, jnp.bfloat16, jnp.int32
    logits, grad, new_mats = pl.pallas_call(
        functools.partial(step_kernel, groups, owners),
        out_shape=(
            jax.ShapeDtypeStruct((1, samples), f32),
            jax.ShapeDtypeStruct((chunk, per_block, feature), f32),
            jax.ShapeDtypeStruct((slots, feature, feature), f32),
        ),
        in_specs=[smem] * 3 + [vmem] + [hbm] * 2,
        out_specs=(vmem,) * 3,
        scratch_shapes=[
            pltpu.SMEM((slots,), i32),
            pltpu.SMEM((slots,), i32),
            pltpu.VMEM(fields.shape, bf16),
            pltpu.VMEM((slots, feature, feature), f32),
            pltpu.VMEM((slots, samples, feature), bf16),
            pltpu.VMEM((slots, feature, 2 * LANES), bf16),
            pltpu.VMEM((slots, samples, feature), bf16),
            pltpu.VMEM((slots, samples, feature), bf16),
            pltpu.VMEM((slots, feature, feature), f32),
            pltpu.VMEM((samples, feature), f32),
            pltpu.VMEM((SUB + slots, LANES), f32),
            pltpu.VMEM((SUB + slots, LANES), f32),
            pltpu.VMEM((slots, samples, feature), bf16),
            pltpu.VMEM((slots, samples, feature), bf16),
            pltpu.VMEM((slots, samples, feature), bf16),
            pltpu.VMEM((slots, feature, 2 * LANES), bf16),
            pltpu.VMEM((slots // 2, feature, feature), i32),
            pltpu.VMEM((slots // 2, feature, feature), i32),
            pltpu.VMEM((slots // 2, feature), f32),
            pltpu.VMEM((slots // 2, feature), f32),
            pltpu.VMEM((groups, SUB, LANES), f32),
            pltpu.VMEM((devices, SUB, LANES), f32),
            pltpu.VMEM((owners // 2, SUB, LANES), f32),
            pltpu.VMEM((devices, SUB, LANES), f32),
            pltpu.VMEM((owners // 2, SUB, LANES), f32),
            pltpu.VMEM((devices, SUB, LANES), f32),
            pltpu.VMEM((cap, samples, feature), f32),
            pltpu.VMEM((cap, samples, feature), f32),
            pltpu.VMEM((2, groups, owners // 2, rows, feature), i32),
            pltpu.VMEM((2, groups, owners // 2, rows, feature), i32),
            pltpu.VMEM((owners, groups, rows, feature), i32),
            pltpu.VMEM((groups, owners, rows, feature), i32),
            pltpu.VMEM((2 * LANES, LANES), f32),
            pltpu.VMEM((SUB * per_block, chunk // SUB * feature), f32),
            pltpu.SemaphoreType.DMA((RUNS,)),
            pltpu.SemaphoreType.DMA((1,)),
            pltpu.SemaphoreType.DMA((2, groups, RUNS)),
            pltpu.SemaphoreType.DMA((2, devices)),
            pltpu.SemaphoreType.DMA((2, devices)),
            pltpu.SemaphoreType.DMA((2, devices)),
            pltpu.SemaphoreType.DMA((2, groups, owners // 2)),
            pltpu.SemaphoreType.DMA((groups, owners)),
            pltpu.SemaphoreType.DMA((2, groups, owners // 2)),
            pltpu.SemaphoreType.DMA((groups, owners)),
            pltpu.SemaphoreType.DMA((2, 1)),
            pltpu.SemaphoreType.DMA((2, groups)),
            pltpu.SemaphoreType.DMA((2, 3)),
        ],
        compiler_params=pltpu.CompilerParams(
            collective_id=0, has_side_effects=True, vmem_limit_bytes=52 * 1024 * 1024
        ),
        cost_estimate=pl.CostEstimate(flops=4 * 10**9, bytes_accessed=8 * 10**6, transcendentals=400),
    )(pair_first, pair_second, pair_count, labels.reshape(1, samples), fields, pair_mats[0, 0])
    return (logits.reshape(samples), grad, new_mats[None, None])


def fits(groups, owners, fields, pair_first):
    samples, _, feature = fields.shape
    slots = pair_first.shape[2]
    cap = slots // groups
    return (
        feature == LANES
        and slots * SUB == LANES
        and slots % groups == 0
        and cap % 2 == 0
        and LANES < samples <= 2 * LANES
        and samples % (SUB * owners) == 0
        and samples % (16 * RUNS) == 0
        and fields.shape[1] & (fields.shape[1] - 1) == 0
        and owners & (owners - 1) == 0
        and owners == 2 * (LANES // (cap * SUB))
        and samples % 32 == 0
        and FIRST_ROW + groups <= SUB
    )


def dispatch(groups, owners, fields, labels, pair_first, pair_second, pair_count, pair_mats):
    args = (fields, labels, pair_first, pair_second, pair_count, pair_mats)
    if fits(groups, owners, fields, pair_first):
        return on_device_kernel(*args)
    return on_device(*args)


def solution(mesh):
    in_specs = (
        P(None, "grp", None),
        P(),
        P("grp", "own", None),
        P(None, "own", None),
        P("grp", "own"),
        P("grp", "own", None, None, None),
    )
    out_specs = (P(), P("own", "grp", None), P("grp", "own", None, None, None))
    per_device = functools.partial(dispatch, mesh.shape["grp"], mesh.shape["own"])
    return jax.shard_map(
        per_device, mesh=mesh, in_specs=in_specs, out_specs=out_specs, check_vma=False
    )
```
